32 devices in a mesh: seq: 16 (over z, y, x), head: 2 (over core).
Axes of the slice: x: 2, y: 2, z: 4, core: 2. Of those that a mesh axis runs over, the one named last changes fastest.
Arguments:
- query: bfloat16 [2048, 4096], P('seq', 'head'), may hold values from -20 to 20
- keys: bfloat16 [2048, 4096], P('seq', 'head'), may hold values from -6 to 6
- values: bfloat16 [2048, 4096], P('seq', 'head'), may hold values from -20 to 20
- grad_normed: bfloat16 [2048, 4096], P('seq', 'head'), may hold values from -18 to 18
- norm_gain: float32 [4096], P('head'), may hold values from 0.25 to 1.75
- doc_ids: int32 [2048], P('seq'), may hold values from 0 to 3, never falling along the last dimension, each value on 1 to 1024 neighbouring positions
- home: int32 [2048], P('seq'), may hold values from 0 to 2047, as said below
Outputs:
- input_grads: bfloat16 [2048, 3, 4096], P('seq', None, 'head')
The draws below stay inside these ranges and needn't reach their ends.
Inputs may be any that keep to these rules, and one draw needn't show every extreme that they name: home is a permutation of 0 to 2047; the owner index along seq of token t is home[t] // 128. Of the 128 tokens on one index of seq, at most 16 have one owner index, and that many is reached for some pairs; every index of seq sends the same multiset of counts to the owners, in a drawn order of owners.
All inputs are finite; a program needn't handle non-finite values.
Results may differ from the reference program's by a relative error of at most 0.0058.
Values may be sent and summed in bfloat16 or wider, within the bound.
A program may use at most 128 MiB of HBM per device.

```python
import math
import jax
import jax.numpy as jnp
import numpy as np
from jax import lax

TOK_DEV = 128
HEADS = 32
HS = 128
TOKENS = 2048
DOCS = 4
DOC_MOST = 1024
N_SEQ = 16


def draw_query(key, part):
    base_key, row_key = jax.random.split(jax.random.fold_in(key, 11))
    shape = (TOKENS, HEADS * HS)
    base = jnp.clip(jax.random.normal(base_key, shape, jnp.float32), -4.0, 4.0)
    row_scale = jnp.exp(jax.random.uniform(row_key, (TOKENS, 1), jnp.float32, math.log(0.5), math.log(5.0)))
    return (base * row_scale).astype(jnp.bfloat16)


def draw_values(key, part):
    base_key, column_key = jax.random.split(jax.random.fold_in(key, 17))
    shape = (TOKENS, HEADS * HS)
    head_of = (jnp.arange(HEADS * HS) // HS).astype(jnp.float32)
    rise = head_of / max(HEADS - 1, 1)
    noise = jnp.exp(jax.random.uniform(column_key, (HEADS * HS,), jnp.float32, 0.0, math.log(2.0)))
    base = jnp.clip(jax.random.normal(base_key, shape, jnp.float32), -4.0, 4.0)
    column_scale = 0.25 * jnp.exp(math.log(10.0) * rise) * noise
    return (base * column_scale[None, :]).astype(jnp.bfloat16)


def draw_home(key, part):
    count = N_SEQ
    per_dev = TOK_DEV
    bound = 2 * per_dev // count
    heavy = max(1, count // 8)
    remain = per_dev - heavy * bound
    share = remain // (count - heavy)
    extra = remain - share * (count - heavy)
    pattern = np.array([bound] * heavy + [share + 1] * extra + [share] * (count - heavy - extra), dtype=np.int32)
    offset_key, label_key, owner_key, source_key = jax.random.split(jax.random.fold_in(key, 23), 4)
    weights = jnp.asarray(pattern)[jax.random.permutation(offset_key, count)]
    labels = jax.random.permutation(label_key, count)
    unlabel = jnp.argsort(labels)
    offsets = jnp.arange(count, dtype=jnp.int32)
    owner_of = unlabel[(labels[:, None] + offsets[None, :]) % count]
    counts = jnp.zeros((count, count), jnp.int32).at[offsets[:, None], owner_of].set(jnp.broadcast_to(weights[None, :], (count, count)))
    base = jnp.cumsum(counts, axis=0) - counts
    which = jnp.repeat(offsets, weights, total_repeat_length=per_dev)
    start = jnp.cumsum(weights) - weights
    within = jnp.arange(per_dev, dtype=jnp.int32) - start[which]
    owner = owner_of[:, which]
    slot = base[offsets[:, None], owner] + within[None, :]
    owner_orders = jax.vmap(lambda one: jax.random.permutation(one, per_dev))(jax.random.split(owner_key, count))
    row_in_owner = owner_orders[owner, slot]
    homes = owner * per_dev + row_in_owner
    source_orders = jax.vmap(lambda one: jax.random.permutation(one, per_dev))(jax.random.split(source_key, count))
    homes = jnp.take_along_axis(homes, source_orders, axis=1)
    return homes.reshape(-1).astype(jnp.int32)


def levels(rng, shape, cuts, low, top_value):
    gain, own = 1.0, jax.random.fold_in(rng, 6)
    for axis_at, blocks in cuts:
        heights = jnp.exp(jax.random.uniform(jax.random.fold_in(own, axis_at), (blocks,), jnp.float32, low / len(cuts), top_value / len(cuts)))
        gain = gain * jnp.repeat(heights, shape[axis_at] // blocks).reshape([-1 if axis == axis_at else 1 for axis in range(len(shape))])
    return gain


def profile(amount, total, most, skew):
    loads = [(1 << 20) // math.isqrt(grade ** skew) + 1 for grade in range(2, amount + 1)]
    surplus, holding = total - most - (amount - 1), [1] * (amount - 1)
    while surplus > 0:
        free = [i for i in range(amount - 1) if holding[i] < most]
        pool, remaining = sum([loads[i] for i in free]), surplus
        for i in free:
            addition = min(most - holding[i], max(1, remaining * loads[i] // pool), surplus)
            holding[i] = holding[i] + addition
            surplus = surplus - addition
    return np.array([most] + holding)


def ragged(key, amount, total, most, slope):
    if amount == 2:
        one = jax.random.randint(key, (), max(1, total - most), min(most, total - 1) + 1)
        return jnp.stack([one, total - one])
    sizes = jnp.asarray(profile(amount, total, most, slope), jnp.int32)
    twos = (amount - 1) // 2
    giver, sink = sizes[1:1 + 2 * twos:2], sizes[2:2 + 2 * twos:2]
    margin = jnp.minimum(giver - 1, most - sink)
    shifted = jax.random.randint(jax.random.fold_in(key, 1), (twos,), 0, 1 << 20) % (margin + 1)
    sizes = sizes.at[1:1 + 2 * twos:2].set(giver - shifted).at[2:2 + 2 * twos:2].set(sink + shifted)
    return sizes[jax.random.permutation(jax.random.fold_in(key, 2), amount)]


def centred(rng, dims, spread, most, pieces=(), kind=jnp.bfloat16):
    values = jax.random.normal(rng, dims, jnp.float32) * spread
    if len(pieces) > 0:
        values = levels(rng, dims, pieces, -0.22, 0.18) * values
    return jnp.clip(values, min=-most, max=most).astype(kind)


def setup_inputs(seed: int = 0) -> dict:
    splits = jax.random.split(jax.random.key(seed), 8)
    return {
        "query": draw_query(jax.random.fold_in(splits[7], 71), 0),
        "keys": centred(splits[1], (TOKENS, HEADS * HS), 1.0, 6.0, ((0, 16), (1, 2))),
        "values": draw_values(jax.random.fold_in(splits[7], 71), 0),
        "grad_normed": centred(splits[3], (TOKENS, HEADS * HS), 3.0, 18.0, ((0, 16), (1, 2))),
        "norm_gain": jnp.clip(1.0 + 0.15 * jax.random.normal(splits[4], (HEADS * HS,), jnp.float32), 0.25, 1.75),
        "doc_ids": jnp.searchsorted(jnp.cumsum(ragged(splits[5], DOCS, TOKENS, DOC_MOST, 1)), jnp.arange(TOKENS), side="right").astype(jnp.int32),
        "home": draw_home(jax.random.fold_in(splits[7], 71), 0),
    }


EPSILON = 1e-05
LOW_SENTINEL = -1.0
HIGH_SENTINEL = 1000000000.0

def masked_scores(left, right, doc_block):
    places = jnp.arange(doc_block.shape[0])
    visible = (doc_block[:, None] == doc_block[None, :]) & (places[:, None] >= places[None, :])
    raw = jnp.einsum('thd,shd->hts', left.astype(jnp.float32), right.astype(jnp.float32))
    return jnp.where(visible[None], raw, 0.0).astype(jnp.bfloat16)

def outer_sum(left, right, keep):
    kept = jnp.where(keep[:, None, None], left, jnp.zeros_like(left))
    return jnp.einsum('tha,thb->hab', kept.astype(jnp.float32), right.astype(jnp.float32))

def join_high(earlier, later):
    top = jnp.maximum(earlier[0], later[0])
    state = jnp.where(earlier[0] == top, earlier[1], 0.0) + jnp.where(later[0] == top, later[1], 0.0)
    return (top, state)

def join_low(earlier, later):
    bottom = jnp.minimum(earlier[0], later[0])
    state = jnp.where(earlier[0] == bottom, earlier[1], 0.0) + jnp.where(later[0] == bottom, later[1], 0.0)
    return (bottom, state)

def mixed(left, right, form):
    return jnp.einsum(form, left.astype(jnp.float32), right.astype(jnp.float32))

def reference(query, keys, values, grad_normed, norm_gain, doc_ids, home):
    full_width = HEADS * HS

    def split(array):
        return array.reshape(N_SEQ, TOK_DEV, HEADS, HS)
    query_b = split(query)
    keys_b = split(keys)
    values_b = split(values)
    normed_b = grad_normed.reshape(N_SEQ, TOK_DEV, full_width)
    doc_b = doc_ids.reshape(N_SEQ, TOK_DEV)
    first_keys = doc_b[:, 0].astype(jnp.float32)
    last_keys = doc_b[:, -1].astype(jnp.float32)

    def forward_own(items):
        keys_one, values_one, doc_one = items
        return outer_sum(keys_one, values_one, doc_one == doc_one[-1])
    own_forward = lax.map(forward_own, (keys_b, values_b, doc_b))
    zero_state = jnp.zeros((HEADS, HS, HS), jnp.float32)

    def forward_step(carry, item):
        return (join_high(carry, item), carry)
    _, (fwd_key, fwd_state) = lax.scan(forward_step, (jnp.array(LOW_SENTINEL, jnp.float32), zero_state), (last_keys, own_forward))

    def section_one(items):
        query_one, keys_one, values_one, normed_one, doc_one, carry_key, carry_state = items
        first_rows = (doc_one == doc_one[0])[:, None, None]
        carry = jnp.where(carry_key == doc_one[0].astype(jnp.float32), carry_state, 0.0).astype(jnp.bfloat16)
        attn = masked_scores(query_one, keys_one, doc_one)
        output = mixed(attn, values_one, 'hts,shd->thd') + jnp.where(first_rows, mixed(query_one, carry, 'tha,hab->thb'), 0.0)
        flat = output.reshape(TOK_DEV, full_width)
        scaled = norm_gain[None, :] * normed_one.astype(jnp.float32)
        squares = lax.optimization_barrier(jnp.sum(flat * flat, axis=1))
        inner = lax.optimization_barrier(jnp.sum(scaled * flat, axis=1))
        inv_rms = lax.rsqrt(squares / full_width + EPSILON)
        grad_out = (inv_rms[:, None] * scaled - flat * (inv_rms * inv_rms * inv_rms * inner / full_width)[:, None]).astype(jnp.bfloat16)
        grad_h = grad_out.reshape(TOK_DEV, HEADS, HS)
        back = masked_scores(grad_h, values_one, doc_one)
        grad_query = mixed(back, keys_one, 'hts,shd->thd') + jnp.where(first_rows, mixed(grad_h, carry, 'thb,hab->tha'), 0.0)
        own_reverse = outer_sum(query_one, grad_h, doc_one == doc_one[0])
        return (grad_h, grad_query.astype(jnp.bfloat16).reshape(TOK_DEV, full_width), own_reverse)
    grad_out_b, grad_query_b, own_reverse = lax.map(section_one, (query_b, keys_b, values_b, normed_b, doc_b, fwd_key, fwd_state))

    def reverse_step(carry, item):
        return (join_low(carry, item), carry)
    _, (rev_key, rev_state) = lax.scan(reverse_step, (jnp.array(HIGH_SENTINEL, jnp.float32), zero_state), (first_keys, own_reverse), reverse=True)

    def section_two(items):
        query_one, keys_one, values_one, grad_h, doc_one, carry_key, carry_state = items
        last_rows = (doc_one == doc_one[-1])[:, None, None]
        carry = jnp.where(carry_key == doc_one[-1].astype(jnp.float32), carry_state, 0.0).astype(jnp.bfloat16)
        attn = masked_scores(query_one, keys_one, doc_one)
        back = masked_scores(grad_h, values_one, doc_one)
        grad_keys = mixed(back, query_one, 'hts,thd->shd') + jnp.where(last_rows, mixed(values_one, carry, 'thb,hab->tha'), 0.0)
        grad_values = mixed(attn, grad_h, 'hts,thd->shd') + jnp.where(last_rows, mixed(keys_one, carry, 'tha,hab->thb'), 0.0)
        return (grad_keys.astype(jnp.bfloat16).reshape(TOK_DEV, full_width), grad_values.astype(jnp.bfloat16).reshape(TOK_DEV, full_width))
    grad_keys_b, grad_values_b = lax.map(section_two, (query_b, keys_b, values_b, grad_out_b, doc_b, rev_key, rev_state))
    rows = jnp.stack([grad_query_b.reshape(TOKENS, full_width), grad_keys_b.reshape(TOKENS, full_width), grad_values_b.reshape(TOKENS, full_width)], axis=1)
    return jnp.zeros_like(rows).at[home].set(rows)
```

```python
import functools

import jax
import jax.numpy as jnp
from jax import lax
from jax.experimental import pallas as pl
from jax.experimental.pallas import tpu as pltpu
from jax.sharding import PartitionSpec as P

HEADS = 32
HS = 128
EPSILON = 1e-05
GROUP = 4
F32 = jnp.float32
BF16 = jnp.bfloat16


def dot(left, right, left_dim, right_dim):
    return lax.dot_general(
        left, right, (((left_dim,), (right_dim,)), ((), ())), preferred_element_type=F32
    )


def rows_at(index, size):
    return pl.ds(pl.multiple_of(index * size, size), size)


def kernel(
    n, nh, chunk, cap,
    q_ref, k_ref, v_ref, gn_ref, gain_ref, meta_ref,
    out_ref,
    metas, fw_own, fw_in, fw_send, fw_carry, rv_own, rv_in, rv_send, rv_carry,
    attn_ref, back_ref, o_ref, go_ref, gk_ref, gv_ref, sums_out, sums_in,
    pack_ref, unpack_ref, bq_send, bq_in, bkv_send, bkv_in,
    sem_send, sem_recv, sum_send, sum_recv,
):
    tok, width = q_ref.shape
    heads = width // HS
    me = lax.axis_index("seq")
    me_head = lax.axis_index("head")

    barrier = pltpu.get_barrier_semaphore()

    def greet(step, _):
        pl.semaphore_signal(
            barrier, inc=1, device_id={"seq": lax.rem(me + step, n)},
            device_id_type=pl.DeviceIdType.MESH,
        )
        return 0

    def greet_head(step, _):
        pl.semaphore_signal(
            barrier, inc=1, device_id={"head": lax.rem(me_head + step, nh)},
            device_id_type=pl.DeviceIdType.MESH,
        )
        return 0

    lax.fori_loop(1, n, greet, 0)
    lax.fori_loop(1, nh, greet_head, 0)

    def remote(which, src, dst, rows, to, slot, whole_src=False):
        return pltpu.make_async_remote_copy(
            src_ref=src if whole_src else src.at[rows_at(to, rows)],
            dst_ref=dst.at[rows_at(slot, rows)],
            send_sem=sem_send.at[which, to],
            recv_sem=sem_recv.at[which, slot],
            device_id={"seq": to},
            device_id_type=pl.DeviceIdType.MESH,
        )

    def start(which, src, dst, rows, whole_src=False):
        def body(step, _):
            remote(which, src, dst, rows, lax.rem(me + step, n), me, whole_src).start()
            return 0

        lax.fori_loop(1, n, body, 0)

    def finish_recv(which, src, dst, rows, whole_src=False):
        def body(step, _):
            other = lax.rem(me + step, n)
            remote(which, src, dst, rows, other, other, whole_src).wait_recv()
            return 0

        lax.fori_loop(1, n, body, 0)

    def finish_send(which, src, dst, rows, whole_src=False):
        def body(step, _):
            remote(which, src, dst, rows, lax.rem(me + step, n), me, whole_src).wait_send()
            return 0

        lax.fori_loop(1, n, body, 0)

    def each_head(body):
        group = GROUP if heads % GROUP == 0 else 1

        def outer(index, _):
            for inner in range(group):
                head = index * group + inner
                body(head, rows_at(head, HS))
            return 0

        lax.fori_loop(0, heads // group, outer, 0)

    doc_row = jnp.broadcast_to(meta_ref[4:5, :], (tok, tok))
    doc_col = doc_row.T
    first_doc, last_doc = meta_ref[2:3, :], meta_ref[3:4, :]
    place_row = lax.broadcasted_iota(jnp.int32, (tok, tok), 0)
    place_col = lax.broadcasted_iota(jnp.int32, (tok, tok), 1)
    visible = (doc_col == doc_row) & (place_col <= place_row)
    first_mask = doc_col == first_doc
    last_mask = doc_col == last_doc
    before = jnp.where(place_row < place_col, 1.0, 0.0).astype(BF16)

    def own_forward(head, at):
        kept = jnp.where(last_mask, k_ref[:, at].astype(F32), 0.0).astype(BF16)
        fw_own[at, :] = dot(kept, v_ref[:, at], 0, 0).astype(BF16)

    if n * chunk > heads * HS:
        fw_own[heads * HS :, :] = jnp.zeros((n * chunk - heads * HS, HS), BF16)
        rv_own[heads * HS :, :] = jnp.zeros((n * chunk - heads * HS, HS), BF16)
    each_head(own_forward)
    metas[rows_at(me, 8), :] = meta_ref[...]
    fw_in[rows_at(me, chunk), :] = fw_own[rows_at(me, chunk), :]
    pl.semaphore_wait(barrier, (n - 1) + (nh - 1))
    start(0, meta_ref, metas, 8, True)
    start(1, fw_own, fw_in, chunk)

    def inside(head, at):
        attn = jnp.where(visible, dot(q_ref[:, at], k_ref[:, at], 1, 1), 0.0).astype(BF16)
        attn_ref[at, :] = attn
        o_ref[:, at] = dot(attn, v_ref[:, at], 1, 0)

    each_head(inside)

    slots = lax.broadcasted_iota(jnp.int32, (cap, tok), 0).astype(F32)
    lanes = lax.broadcasted_iota(jnp.int32, (cap, tok), 1).astype(F32)

    def picks(owners, owner):
        chosen = jnp.broadcast_to(jnp.where(owners == owner, 1.0, 0.0), (cap, tok))
        rank = dot(chosen.astype(BF16), before, 1, 0)
        return jnp.where(rank == slots, chosen, 0.0)

    def pack(owner, _):
        pack_ref[rows_at(owner, cap), :] = picks(meta_ref[0:1, :], owner.astype(F32)).astype(BF16)
        return 0

    lax.fori_loop(0, n, pack, 0)

    finish_recv(0, meta_ref, metas, 8, True)
    finish_recv(1, fw_own, fw_in, chunk)

    def doc(block, which):
        return metas[pl.ds(block * 8 + which, 1), :]

    fw_send[rows_at(0, chunk), :] = jnp.zeros((chunk, HS), BF16)

    def forward_step(block, total):
        total = fw_in[rows_at(block - 1, chunk), :].astype(F32) + total
        met = jnp.where(doc(block, 2) == doc(block - 1, 3), 1.0, 0.0)
        fw_send[rows_at(block, chunk), :] = (total * met).astype(BF16)
        return total * jnp.where(doc(block, 3) == doc(block - 1, 3), 1.0, 0.0)

    lax.fori_loop(1, n, forward_step, jnp.zeros((chunk, HS), F32))
    start(2, fw_send, fw_carry, chunk)
    fw_carry[rows_at(me, chunk), :] = fw_send[rows_at(me, chunk), :]

    def unpack(source, _):
        chosen = picks(metas[pl.ds(source * 8, 1), :], me.astype(F32))
        row = jnp.sum(chosen * metas[pl.ds(source * 8 + 1, 1), :], axis=1, keepdims=True)
        used = jnp.sum(chosen, axis=1, keepdims=True)
        unpack_ref[rows_at(source, cap), :] = (
            jnp.where(row == lanes, 1.0, 0.0) * used
        ).astype(BF16)
        return 0

    lax.fori_loop(0, n, unpack, 0)
    finish_recv(2, fw_send, fw_carry, chunk)

    def output(head, at):
        add = dot(q_ref[:, at], fw_carry[at, :], 1, 0)
        total = o_ref[:, at] + jnp.where(first_mask, add, 0.0)
        o_ref[:, at] = total
        scaled = gain_ref[:, at] * gn_ref[:, at].astype(F32)
        return total * total, scaled * total

    squares = jnp.zeros((tok, HS), F32)
    inner = jnp.zeros((tok, HS), F32)

    group = GROUP if heads % GROUP == 0 else 1

    def output_step(index, sums):
        squares, inner = sums
        for part in range(group):
            head = index * group + part
            one, two = output(head, rows_at(head, HS))
            squares, inner = squares + one, inner + two
        return squares, inner

    squares, inner = lax.fori_loop(0, heads // group, output_step, (squares, inner))
    squares = jnp.sum(squares, axis=1, keepdims=True)
    inner = jnp.sum(inner, axis=1, keepdims=True)
    pair = jnp.where(place_col < HS // 2, squares, inner)
    sums_out[...] = pair

    def sum_copy(to, slot):
        return pltpu.make_async_remote_copy(
            src_ref=sums_out,
            dst_ref=sums_in.at[rows_at(slot, tok)],
            send_sem=sum_send.at[to],
            recv_sem=sum_recv.at[slot],
            device_id={"head": to},
            device_id_type=pl.DeviceIdType.MESH,
        )

    def sum_start(step, _):
        sum_copy(lax.rem(me_head + step, nh), me_head).start()
        return 0

    def sum_finish(step, total):
        other = lax.rem(me_head + step, nh)
        sum_copy(other, other).wait_recv()
        return total + sums_in[rows_at(other, tok), :]

    def sum_sent(step, _):
        sum_copy(lax.rem(me_head + step, nh), me_head).wait_send()
        return 0

    lax.fori_loop(1, nh, sum_start, 0)
    pair = lax.fori_loop(1, nh, sum_finish, pair)
    full = HEADS * HS
    inv_rms = lax.rsqrt(pair[:, 0:1] / full + EPSILON)
    pull = inv_rms * inv_rms * inv_rms * pair[:, HS - 1 : HS] / full
    inv_rms = jnp.broadcast_to(inv_rms, (tok, HS))
    pull = jnp.broadcast_to(pull, (tok, HS))

    def own_reverse(head, at):
        scaled = gain_ref[:, at] * gn_ref[:, at].astype(F32)
        grad = (inv_rms * scaled - o_ref[:, at] * pull).astype(BF16)
        go_ref[:, at] = grad
        kept = jnp.where(first_mask, q_ref[:, at].astype(F32), 0.0).astype(BF16)
        rv_own[at, :] = dot(kept, grad, 0, 0).astype(BF16)

    each_head(own_reverse)
    start(3, rv_own, rv_in, chunk)
    rv_in[rows_at(me, chunk), :] = rv_own[rows_at(me, chunk), :]

    def grad_query(head, at):
        grad = go_ref[:, at]
        back = jnp.where(visible, dot(grad, v_ref[:, at], 1, 1), 0.0).astype(BF16)
        back_ref[at, :] = back
        add = dot(grad, fw_carry[at, :], 1, 1)
        result = dot(back, k_ref[:, at], 1, 0) + jnp.where(first_mask, add, 0.0)
        bq_send[:, at] = dot(pack_ref[...], result.astype(BF16), 1, 0).astype(BF16)

    each_head(grad_query)
    bq_in[rows_at(me, cap), :] = bq_send[rows_at(me, cap), :]
    start(5, bq_send, bq_in, cap)

    finish_recv(3, rv_own, rv_in, chunk)
    rv_send[rows_at(n - 1, chunk), :] = jnp.zeros((chunk, HS), BF16)

    def reverse_step(step, total):
        block = n - 1 - step
        total = rv_in[rows_at(block + 1, chunk), :].astype(F32) + total
        met = jnp.where(doc(block, 3) == doc(block + 1, 2), 1.0, 0.0)
        rv_send[rows_at(block, chunk), :] = (total * met).astype(BF16)
        return total * jnp.where(doc(block, 2) == doc(block + 1, 2), 1.0, 0.0)

    lax.fori_loop(1, n, reverse_step, jnp.zeros((chunk, HS), F32))
    start(4, rv_send, rv_carry, chunk)
    rv_carry[rows_at(me, chunk), :] = rv_send[rows_at(me, chunk), :]

    def inside_back(head, at):
        gk_ref[:, at] = dot(back_ref[at, :], q_ref[:, at], 0, 0)
        gv_ref[:, at] = dot(attn_ref[at, :], go_ref[:, at], 0, 0)

    each_head(inside_back)
    finish_recv(4, rv_send, rv_carry, chunk)

    def grad_pair(head, at):
        carry = rv_carry[at, :]
        key = gk_ref[:, at] + jnp.where(last_mask, dot(v_ref[:, at], carry, 1, 1), 0.0)
        value = gv_ref[:, at] + jnp.where(last_mask, dot(k_ref[:, at], carry, 1, 0), 0.0)
        bkv_send[:, at] = dot(pack_ref[...], key.astype(BF16), 1, 0).astype(BF16)
        bkv_send[:, rows_at(head + heads, HS)] = dot(
            pack_ref[...], value.astype(BF16), 1, 0
        ).astype(BF16)

    each_head(grad_pair)
    start(6, bkv_send, bkv_in, cap)
    bkv_in[rows_at(me, cap), :] = bkv_send[rows_at(me, cap), :]

    finish_recv(5, bq_send, bq_in, cap)

    def place_query(head, at):
        out_ref[:, at] = dot(unpack_ref[...], bq_in[:, at], 0, 0).astype(BF16)

    each_head(place_query)
    finish_recv(6, bkv_send, bkv_in, cap)

    def place_pair(head, at):
        for part in range(2):
            out_ref[:, rows_at(head + (part + 1) * heads, HS)] = dot(
                unpack_ref[...], bkv_in[:, rows_at(head + part * heads, HS)], 0, 0
            ).astype(BF16)

    each_head(place_pair)

    finish_send(0, meta_ref, metas, 8, True)
    finish_send(1, fw_own, fw_in, chunk)
    finish_send(2, fw_send, fw_carry, chunk)
    lax.fori_loop(1, nh, sum_sent, 0)
    finish_send(3, rv_own, rv_in, chunk)
    finish_send(4, rv_send, rv_carry, chunk)
    finish_send(5, bq_send, bq_in, cap)
    finish_send(6, bkv_send, bkv_in, cap)


def local(n, nh, query, keys, values, grad_normed, norm_gain, doc_ids, home):
    tok, width = query.shape
    heads = width // HS
    chunk = max(16, heads * HS // n)
    cap = max(16, 2 * tok // n)
    rows = jnp.stack(
        [
            home // tok,
            home % tok,
            jnp.broadcast_to(doc_ids[0], (tok,)),
            jnp.broadcast_to(doc_ids[-1], (tok,)),
            doc_ids,
        ]
    ).astype(F32)
    meta = jnp.concatenate([rows, jnp.zeros((3, tok), F32)], axis=0)
    states = pltpu.VMEM((n * chunk, HS), BF16)
    scores = pltpu.VMEM((heads * HS, HS), BF16)
    wide = pltpu.VMEM((tok, width), F32)
    vmem = pl.BlockSpec(memory_space=pltpu.VMEM)
    result = pl.pallas_call(
        functools.partial(kernel, n, nh, chunk, cap),
        out_shape=jax.ShapeDtypeStruct((tok, 3 * width), BF16),
        in_specs=[vmem] * 6,
        out_specs=vmem,
        scratch_shapes=[
            pltpu.VMEM((n * 8, tok), F32),
            states, states, states, states, states, states, states, states,
            scores, scores,
            wide,
            pltpu.VMEM((tok, width), BF16),
            wide, wide,
            pltpu.VMEM((tok, HS), F32),
            pltpu.VMEM((nh * tok, HS), F32),
            pltpu.VMEM((n * cap, tok), BF16),
            pltpu.VMEM((n * cap, tok), BF16),
            pltpu.VMEM((n * cap, width), BF16),
            pltpu.VMEM((n * cap, width), BF16),
            pltpu.VMEM((n * cap, 2 * width), BF16),
            pltpu.VMEM((n * cap, 2 * width), BF16),
            pltpu.SemaphoreType.DMA((7, n)),
            pltpu.SemaphoreType.DMA((7, n)),
            pltpu.SemaphoreType.DMA((nh,)),
            pltpu.SemaphoreType.DMA((nh,)),
        ],
        compiler_params=pltpu.CompilerParams(
            collective_id=0, has_side_effects=True, vmem_limit_bytes=48 * 1024 * 1024
        ),
    )(query, keys, values, grad_normed, norm_gain[None, :], meta)
    return result.reshape(tok, 3, width)


def solution(mesh):
    placed = (
        P("seq", "head"),
        P("seq", "head"),
        P("seq", "head"),
        P("seq", "head"),
        P("head"),
        P("seq"),
        P("seq"),
    )
    return jax.shard_map(
        functools.partial(local, mesh.shape["seq"], mesh.shape["head"]),
        mesh=mesh, in_specs=placed, out_specs=P("seq", None, "head"), check_vma=False,
    )
```

```python
import functools

import jax
import jax.numpy as jnp
from jax import lax
from jax.experimental import pallas as pl
from jax.experimental.pallas import tpu as pltpu
from jax.sharding import PartitionSpec as P

HEADS = 32
HS = 128
EPSILON = 1e-05
PLANE = 4
SUBS = 4
F32 = jnp.float32
BF16 = jnp.bfloat16


def dot(left, right, left_dim, right_dim):
    return lax.dot_general(
        left, right, (((left_dim,), (right_dim,)), ((), ())), preferred_element_type=F32
    )


def rows_at(index, size):
    return pl.ds(pl.multiple_of(index * size, size), size)


MESH = pl.DeviceIdType.MESH


def rows_from(offset, size):
    return pl.ds(pl.multiple_of(offset, size), size)


def same(left, right):
    return jnp.where(left == right, 1.0, 0.0)


def kernel(
    n, nh, cap,
    q_hbm, k_hbm, v_hbm, gn_hbm, gain_hbm, doc_hbm, home_hbm,
    out_ref,
    q_ref, k_ref, v_ref, gn_ref, gain_ref, doc_ref, home_ref,
    meta_ref, metas,
    fw_own, fw_in, fw_total, fw_far, fw_send, fw_carry,
    rv_own, rv_in, rv_total, rv_far, rv_send, rv_carry,
    attn_ref, back_ref, o_ref, go_ref, gk_ref, gv_ref, sums_out, sums_in,
    pack_ref, unpack_ref, bq_send, bq_in, bkv_send, bkv_in,
    in_sem, meta_sems, near_sems, far_sems, carry_sems, q_sems, kv_sems, sum_sems,
):
    tok, width = q_ref.shape
    heads = width // HS
    quarter = heads * HS // PLANE
    sub = quarter // SUBS
    aligned = sub == HS
    each = heads // SUBS
    planes = n // PLANE
    me = lax.axis_index("seq")
    me_head = lax.axis_index("head")
    plane, spot = me // PLANE, lax.rem(me, PLANE)

    loads = [
        pltpu.make_async_copy(src, dst, in_sem.at[index])
        for index, (src, dst) in enumerate(
            [
                (doc_hbm, doc_ref), (home_hbm, home_ref), (k_hbm, k_ref), (v_hbm, v_ref),
                (q_hbm, q_ref), (gn_hbm, gn_ref), (gain_hbm, gain_ref),
            ]
        )
    ]
    for load in loads:
        load.start()

    barrier = pltpu.get_barrier_semaphore()

    def greet(step, _):
        pl.semaphore_signal(
            barrier, inc=1, device_id={"seq": lax.rem(me + step, n)}, device_id_type=MESH
        )
        return 0

    def greet_head(step, _):
        pl.semaphore_signal(
            barrier, inc=1, device_id={"head": lax.rem(me_head + step, nh)}, device_id_type=MESH
        )
        return 0

    lax.fori_loop(1, n, greet, 0)
    lax.fori_loop(1, nh, greet_head, 0)

    loads[0].wait()
    loads[1].wait()
    homes = home_ref[...]
    owners = lax.div(homes, jnp.full_like(homes, tok))
    docs = doc_ref[...].astype(F32)
    meta_ref[0:1, :] = owners.astype(F32)
    meta_ref[1:2, :] = (homes - owners * tok).astype(F32)
    meta_ref[2:3, :] = jnp.broadcast_to(docs[:, 0:1], (1, tok))
    meta_ref[3:4, :] = jnp.broadcast_to(docs[:, tok - 1 : tok], (1, tok))
    meta_ref[4:5, :] = docs
    meta_ref[5:8, :] = jnp.zeros((3, tok), F32)

    doc_row = jnp.broadcast_to(docs, (tok, tok))
    doc_col = doc_row.T
    first_doc, last_doc = meta_ref[2:3, :], meta_ref[3:4, :]
    place_row = lax.broadcasted_iota(jnp.int32, (tok, tok), 0)
    place_col = lax.broadcasted_iota(jnp.int32, (tok, tok), 1)
    visible = (doc_col == doc_row) & (place_col <= place_row)
    first_mask = doc_col == first_doc
    last_mask = doc_col == last_doc
    before = jnp.where(place_row < place_col, 1.0, 0.0).astype(BF16)
    metas[rows_at(me, 8), :] = meta_ref[...]

    def copy_meta(to, slot):
        return pltpu.make_async_remote_copy(
            src_ref=meta_ref, dst_ref=metas.at[rows_at(slot, 8)],
            send_sem=meta_sems.at[0, to], recv_sem=meta_sems.at[1, slot],
            device_id={"seq": to}, device_id_type=MESH,
        )

    def copy_rows(src, dst, sems, group, to, slot):
        return pltpu.make_async_remote_copy(
            src_ref=src.at[rows_at(group * n + to, cap)],
            dst_ref=dst.at[rows_at(group * n + slot, cap)],
            send_sem=sems.at[0, group, to], recv_sem=sems.at[1, group, slot],
            device_id={"seq": to}, device_id_type=MESH,
        )

    def others(body):
        def step(index, _):
            body(lax.rem(me + index, n))
            return 0

        lax.fori_loop(1, n, step, 0)

    def loop(count, body):
        def step(index, _):
            body(index)
            return 0

        lax.fori_loop(0, count, step, 0)

    def at_sub(block, part):
        return rows_from(block * quarter + part * sub, sub)

    def copy_near(sems, scan, src, dst, part, to, slot):
        return pltpu.make_async_remote_copy(
            src_ref=src.at[at_sub(to, part)], dst_ref=dst.at[at_sub(slot, part)],
            send_sem=sems.at[0, scan, to * SUBS + part],
            recv_sem=sems.at[1, scan, slot * SUBS + part],
            device_id={"seq": plane * PLANE + to}, device_id_type=MESH,
        )

    peers = [lax.rem(spot + step, PLANE) for step in range(1, PLANE)]

    def send_near(sems, scan, src, dst, part):
        for peer in peers:
            copy_near(sems, scan, src, dst, part, peer, spot).start()
        dst[at_sub(spot, part), :] = src[at_sub(spot, part), :]

    def got_near(sems, scan, src, dst, part):
        for peer in peers:
            copy_near(sems, scan, src, dst, part, peer, peer).wait_recv()

    def sent_near(sems, scan, src, dst, part):
        for peer in peers:
            copy_near(sems, scan, src, dst, part, peer, spot).wait_send()

    def copy_far(scan, total, far, part, ahead):
        sign = 1 if scan == 0 else -1
        return pltpu.make_async_remote_copy(
            src_ref=total.at[at_sub(0, part)], dst_ref=far.at[at_sub(ahead - 1, part)],
            send_sem=far_sems.at[0, scan, (ahead - 1) * SUBS + part],
            recv_sem=far_sems.at[1, scan, (ahead - 1) * SUBS + part],
            device_id={"seq": me + sign * ahead * PLANE}, device_id_type=MESH,
        )

    def sends(scan, ahead):
        return plane + ahead < planes if scan == 0 else plane >= ahead

    def gets(scan, ahead):
        return plane >= ahead if scan == 0 else plane + ahead < planes

    def doc(block, which):
        return metas[pl.ds(block * 8 + which, 1), :]

    scans = [
        (fw_own, fw_in, fw_total, fw_far, fw_send, fw_carry, 3, 2, list(range(PLANE)), -1),
        (rv_own, rv_in, rv_total, rv_far, rv_send, rv_carry, 2, 3, list(range(PLANE))[::-1], 1),
    ]
    for scan in range(2):
        far = scans[scan][3]
        for ahead in (1, 2):
            @pl.when(jnp.logical_not(gets(scan, ahead)))
            def _():
                far[(ahead - 1) * quarter : ahead * quarter, :] = jnp.zeros((quarter, HS), BF16)

    def plane_total(scan, part):
        own, arrived, total_ref, far, _, _, leaving, _, order, toward = scans[scan]
        got_near(near_sems, scan, own, arrived, part)
        total = None
        for block in order:
            mine = arrived[at_sub(block, part), :].astype(F32)
            here = plane * PLANE + block
            if total is None:
                total = mine
            else:
                total = mine + total * same(doc(here, leaving), doc(here + toward, leaving))
        total_ref[at_sub(0, part), :] = total.astype(BF16)
        for ahead in (1, 2):
            @pl.when(sends(scan, ahead))
            def _():
                copy_far(scan, total_ref, far, part, ahead).start()

    def carries(scan, part):
        _, arrived, total_ref, far, send, carry, leaving, entering, order, toward = scans[scan]
        for ahead in (1, 2):
            @pl.when(gets(scan, ahead))
            def _():
                copy_far(scan, total_ref, far, part, ahead).wait_recv()

        def clamp(block):
            return jnp.clip(block, 0, n - 1)

        edge = plane * PLANE + order[0] + toward
        total = far[at_sub(0, part), :].astype(F32) + far[at_sub(1, part), :].astype(F32) * same(
            doc(clamp(edge), leaving), doc(clamp(edge + toward * PLANE), leaving)
        )
        for block in order:
            here = plane * PLANE + block
            prior = doc(clamp(here + toward), leaving)
            send[at_sub(block, part), :] = (total * same(doc(here, entering), prior)).astype(BF16)
            mine = arrived[at_sub(block, part), :].astype(F32)
            total = mine + total * same(doc(here, leaving), prior)
        send_near(carry_sems, scan, send, carry, part)

    def got_carry(scan, part):
        got_near(carry_sems, scan, scans[scan][4], scans[scan][5], part)

    def group_heads(part):
        return [(index, index * SUBS + part) for index in range(each)]

    def own_forward(part):
        for _, head in group_heads(part):
            at = rows_at(head, HS)
            kept = jnp.where(last_mask, k_ref[:, at].astype(F32), 0.0).astype(BF16)
            fw_own[at, :] = dot(kept, v_ref[:, at], 0, 0).astype(BF16)

    def inside(part):
        for _, head in group_heads(part):
            at = rows_at(head, HS)
            attn = jnp.where(visible, dot(q_ref[:, at], k_ref[:, at], 1, 1), 0.0).astype(BF16)
            attn_ref[at, :] = attn
            o_ref[:, at] = dot(attn, v_ref[:, at], 1, 0)

    loads[2].wait()
    loads[3].wait()
    own_forward(0)
    pl.semaphore_wait(barrier, (n - 1) + (nh - 1))
    others(lambda other: copy_meta(other, me).start())
    if aligned:
        send_near(near_sems, 0, fw_own, fw_in, 0)

        def own_step(index):
            own_forward(index + 1)
            send_near(near_sems, 0, fw_own, fw_in, index + 1)

        loop(SUBS - 1, own_step)
    else:
        loop(SUBS - 1, lambda index: own_forward(index + 1))
        loop(SUBS, lambda part: send_near(near_sems, 0, fw_own, fw_in, part))
    loads[4].wait()
    loop(SUBS // 2, inside)
    others(lambda other: copy_meta(other, other).wait_recv())
    loop(SUBS, lambda part: plane_total(0, part))
    loop(SUBS // 2, lambda part: inside(part + SUBS // 2))

    slots = lax.broadcasted_iota(jnp.int32, (cap, tok), 0).astype(F32)
    lanes = lax.broadcasted_iota(jnp.int32, (cap, tok), 1).astype(F32)

    def picks(owners, owner):
        chosen = jnp.broadcast_to(jnp.where(owners == owner, 1.0, 0.0), (cap, tok))
        rank = dot(chosen.astype(BF16), before, 1, 0)
        return jnp.where(rank == slots, chosen, 0.0)

    def pack(owner):
        pack_ref[rows_at(owner, cap), :] = picks(meta_ref[0:1, :], owner.astype(F32)).astype(BF16)

    def unpack(source):
        chosen = picks(metas[pl.ds(source * 8, 1), :], me.astype(F32))
        row = jnp.sum(chosen * metas[pl.ds(source * 8 + 1, 1), :], axis=1, keepdims=True)
        used = jnp.sum(chosen, axis=1, keepdims=True)
        unpack_ref[rows_at(source, cap), :] = (
            jnp.where(row == lanes, 1.0, 0.0) * used
        ).astype(BF16)

    loop(SUBS, lambda part: carries(0, part))
    loop(n, pack)
    loads[5].wait()
    loads[6].wait()
    if not aligned:
        loop(SUBS, lambda part: got_carry(0, part))

    def output_step(part, sums):
        squares, inner = sums
        if aligned:
            got_carry(0, part)
        for _, head in group_heads(part):
            at = rows_at(head, HS)
            add = dot(q_ref[:, at], fw_carry[at, :], 1, 0)
            total = o_ref[:, at] + jnp.where(first_mask, add, 0.0)
            o_ref[:, at] = total
            scaled = gain_ref[:, at] * gn_ref[:, at].astype(F32)
            squares, inner = squares + total * total, inner + scaled * total
        return squares, inner

    zero = jnp.zeros((tok, HS), F32)
    squares, inner = lax.fori_loop(0, SUBS, output_step, (zero, zero))
    squares = jnp.sum(squares, axis=1, keepdims=True)
    inner = jnp.sum(inner, axis=1, keepdims=True)
    pair = jnp.where(place_col < HS // 2, squares, inner)
    sums_out[...] = pair

    def sum_copy(to, slot):
        return pltpu.make_async_remote_copy(
            src_ref=sums_out, dst_ref=sums_in.at[rows_at(slot, tok)],
            send_sem=sum_sems.at[0, to], recv_sem=sum_sems.at[1, slot],
            device_id={"head": to}, device_id_type=MESH,
        )

    def sum_start(step, _):
        sum_copy(lax.rem(me_head + step, nh), me_head).start()
        return 0

    def sum_finish(step, total):
        other = lax.rem(me_head + step, nh)
        sum_copy(other, other).wait_recv()
        return total + sums_in[rows_at(other, tok), :]

    def sum_sent(step, _):
        sum_copy(lax.rem(me_head + step, nh), me_head).wait_send()
        return 0

    lax.fori_loop(1, nh, sum_start, 0)
    loop(n, unpack)
    pair = lax.fori_loop(1, nh, sum_finish, pair)
    full = HEADS * HS
    inv_rms = lax.rsqrt(pair[:, 0:1] / full + EPSILON)
    pull = inv_rms * inv_rms * inv_rms * pair[:, HS - 1 : HS] / full
    inv_rms = jnp.broadcast_to(inv_rms, (tok, HS))
    pull = jnp.broadcast_to(pull, (tok, HS))

    def own_reverse(part):
        for _, head in group_heads(part):
            at = rows_at(head, HS)
            scaled = gain_ref[:, at] * gn_ref[:, at].astype(F32)
            grad = (inv_rms * scaled - o_ref[:, at] * pull).astype(BF16)
            go_ref[:, at] = grad
            kept = jnp.where(first_mask, q_ref[:, at].astype(F32), 0.0).astype(BF16)
            rv_own[at, :] = dot(kept, grad, 0, 0).astype(BF16)
        if aligned:
            send_near(near_sems, 1, rv_own, rv_in, part)

    loop(SUBS, own_reverse)
    if not aligned:
        loop(SUBS, lambda part: send_near(near_sems, 1, rv_own, rv_in, part))

    half = SUBS // 2
    slots_all = n * cap

    def grad_query(group, part):
        for index, head in group_heads(group * half + part):
            at = rows_at(head, HS)
            grad = go_ref[:, at]
            back = jnp.where(visible, dot(grad, v_ref[:, at], 1, 1), 0.0).astype(BF16)
            back_ref[at, :] = back
            add = dot(grad, fw_carry[at, :], 1, 1)
            result = dot(back, k_ref[:, at], 1, 0) + jnp.where(first_mask, add, 0.0)
            bq_send[
                group * slots_all : (group + 1) * slots_all, rows_at(part * each + index, HS)
            ] = dot(pack_ref[...], result.astype(BF16), 1, 0).astype(BF16)

    def send_query(group):
        others(lambda other: copy_rows(bq_send, bq_in, q_sems, group, other, me).start())
        bq_in[rows_at(group * n + me, cap), :] = bq_send[rows_at(group * n + me, cap), :]

    loop(half, lambda part: grad_query(0, part))
    loop(SUBS, lambda part: plane_total(1, part))
    send_query(0)
    loop(half, lambda part: grad_query(1, part))
    send_query(1)

    def inside_back(part):
        for _, head in group_heads(part):
            at = rows_at(head, HS)
            gk_ref[:, at] = dot(back_ref[at, :], q_ref[:, at], 0, 0)
            gv_ref[:, at] = dot(attn_ref[at, :], go_ref[:, at], 0, 0)

    loop(SUBS, lambda part: carries(1, part))
    loop(SUBS, inside_back)
    if not aligned:
        loop(SUBS, lambda part: got_carry(1, part))

    def grad_pair(part):
        if aligned:
            got_carry(1, part)
        rows = rows_at(part, slots_all)
        for index, head in group_heads(part):
            at = rows_at(head, HS)
            carry = rv_carry[at, :]
            key = gk_ref[:, at] + jnp.where(last_mask, dot(v_ref[:, at], carry, 1, 1), 0.0)
            value = gv_ref[:, at] + jnp.where(last_mask, dot(k_ref[:, at], carry, 1, 0), 0.0)
            for which, result in enumerate((key, value)):
                column = (which * each + index) * HS
                bkv_send[rows, column : column + HS] = dot(
                    pack_ref[...], result.astype(BF16), 1, 0
                ).astype(BF16)
        others(lambda other: copy_rows(bkv_send, bkv_in, kv_sems, part, other, me).start())
        bkv_in[rows_at(part * n + me, cap), :] = bkv_send[rows_at(part * n + me, cap), :]

    loop(SUBS, grad_pair)

    def place_query(group, part):
        for index, head in group_heads(group * half + part):
            arrived = bq_in[
                group * slots_all : (group + 1) * slots_all, rows_at(part * each + index, HS)
            ]
            out_ref[:, rows_at(head, HS)] = dot(unpack_ref[...], arrived, 0, 0).astype(BF16)

    for group in range(2):
        others(lambda other: copy_rows(bq_send, bq_in, q_sems, group, other, other).wait_recv())
        loop(half, lambda part: place_query(group, part))

    def place_pair(part):
        others(lambda other: copy_rows(bkv_send, bkv_in, kv_sems, part, other, other).wait_recv())
        rows = rows_at(part, slots_all)
        for index, head in group_heads(part):
            for which in range(2):
                column = (which * each + index) * HS
                out_ref[:, rows_at((which + 1) * heads + head, HS)] = dot(
                    unpack_ref[...], bkv_in[rows, column : column + HS], 0, 0
                ).astype(BF16)

    loop(SUBS, place_pair)

    others(lambda other: copy_meta(other, me).wait_send())
    lax.fori_loop(1, nh, sum_sent, 0)
    for scan in range(2):
        own, arrived, total_ref, far, send, carry = scans[scan][:6]

        def drain(part):
            sent_near(near_sems, scan, own, arrived, part)
            sent_near(carry_sems, scan, send, carry, part)
            for ahead in (1, 2):
                @pl.when(sends(scan, ahead))
                def _():
                    copy_far(scan, total_ref, far, part, ahead).wait_send()

        loop(SUBS, drain)
    for group in range(2):
        others(lambda other: copy_rows(bq_send, bq_in, q_sems, group, other, me).wait_send())
    loop(
        SUBS,
        lambda part: others(
            lambda other: copy_rows(bkv_send, bkv_in, kv_sems, part, other, me).wait_send()
        ),
    )


def local(n, nh, query, keys, values, grad_normed, norm_gain, doc_ids, home):
    tok, width = query.shape
    heads = width // HS
    cap = max(16, 2 * tok // n)
    states = pltpu.VMEM((heads * HS, HS), BF16)
    total = pltpu.VMEM((heads * HS // PLANE, HS), BF16)
    far = pltpu.VMEM((2 * heads * HS // PLANE, HS), BF16)
    scan = [states, states, total, far, states, states]
    block = pltpu.VMEM((tok, width), BF16)
    wide = pltpu.VMEM((tok, width), F32)
    map_rows = pltpu.VMEM((n * cap, tok), BF16)
    query_rows = pltpu.VMEM((2 * n * cap, width // 2), BF16)
    pair_rows = pltpu.VMEM((SUBS * n * cap, 2 * width // SUBS), BF16)
    dma = pltpu.SemaphoreType.DMA
    result = pl.pallas_call(
        functools.partial(kernel, n, nh, cap),
        out_shape=jax.ShapeDtypeStruct((tok, 3 * width), BF16),
        in_specs=[pl.BlockSpec(memory_space=pl.ANY)] * 7,
        out_specs=pl.BlockSpec(memory_space=pltpu.VMEM),
        scratch_shapes=[
            block, block, block, block,
            pltpu.VMEM((1, width), F32),
            pltpu.VMEM((1, tok), jnp.int32),
            pltpu.VMEM((1, tok), jnp.int32),
            pltpu.VMEM((8, tok), F32),
            pltpu.VMEM((n * 8, tok), F32),
            *scan, *scan,
            states, states,
            wide, block, wide, wide,
            pltpu.VMEM((tok, HS), F32),
            pltpu.VMEM((nh * tok, HS), F32),
            map_rows, map_rows,
            query_rows, query_rows, pair_rows, pair_rows,
            dma((7,)),
            dma((2, n)),
            dma((2, 2, PLANE * SUBS)),
            dma((2, 2, 2 * SUBS)),
            dma((2, 2, PLANE * SUBS)),
            dma((2, 2, n)),
            dma((2, SUBS, n)),
            dma((2, nh)),
        ],
        compiler_params=pltpu.CompilerParams(
            collective_id=0, has_side_effects=True, vmem_limit_bytes=48 * 1024 * 1024
        ),
    )(query, keys, values, grad_normed, norm_gain[None, :], doc_ids[None, :], home[None, :])
    return result.reshape(tok, 3, width)


def solution(mesh):
    placed = (
        P("seq", "head"),
        P("seq", "head"),
        P("seq", "head"),
        P("seq", "head"),
        P("head"),
        P("seq"),
        P("seq"),
    )
    return jax.shard_map(
        functools.partial(local, mesh.shape["seq"], mesh.shape["head"]),
        mesh=mesh, in_specs=placed, out_specs=P("seq", None, "head"), check_vma=False,
    )
```

```python
import functools

import jax
import jax.numpy as jnp
from jax import lax
from jax.experimental import pallas as pl
from jax.experimental.pallas import tpu as pltpu
from jax.sharding import PartitionSpec as P

HEADS = 32
HS = 128
EPSILON = 1e-05
PLANE = 4
SUBS = 4
F32 = jnp.float32
BF16 = jnp.bfloat16


def dot(left, right, left_dim, right_dim):
    return lax.dot_general(
        left, right, (((left_dim,), (right_dim,)), ((), ())), preferred_element_type=F32
    )


def rows_at(index, size):
    return pl.ds(pl.multiple_of(index * size, size), size)


MESH = pl.DeviceIdType.MESH


def rows_from(offset, size):
    return pl.ds(pl.multiple_of(offset, size), size)


def same(left, right):
    return jnp.where(left == right, 1.0, 0.0)


def kernel(
    n, nh, cap,
    q_hbm, k_hbm, v_hbm, gn_hbm, gain_hbm, doc_hbm, home_hbm,
    out_ref,
    q_ref, k_ref, v_ref, gn_ref, gain_ref, doc_ref, home_ref,
    meta_ref, metas,
    fw_own, fw_in, fw_total, fw_far, fw_send, fw_carry,
    rv_own, rv_in, rv_total, rv_far, rv_send, rv_carry,
    attn_ref, back_ref, o_ref, go_ref, gk_ref, gv_ref, sums_out, sums_in,
    pack_ref, unpack_ref, bq_send, bq_in, bkv_send, bkv_in,
    in_sem, meta_sems, near_sems, far_sems, carry_sems, q_sems, kv_sems, sum_sems,
):
    tok, width = q_ref.shape
    heads = width // HS
    quarter = heads * HS // PLANE
    sub = quarter // SUBS
    aligned = sub == HS
    each = heads // SUBS
    planes = n // PLANE
    me = lax.axis_index("seq")
    me_head = lax.axis_index("head")
    plane, spot = me // PLANE, lax.rem(me, PLANE)

    loads = [
        pltpu.make_async_copy(src, dst, in_sem.at[index])
        for index, (src, dst) in enumerate(
            [
                (doc_hbm, doc_ref), (home_hbm, home_ref), (k_hbm, k_ref), (v_hbm, v_ref),
                (q_hbm, q_ref), (gn_hbm, gn_ref), (gain_hbm, gain_ref),
            ]
        )
    ]
    for load in loads:
        load.start()

    barrier = pltpu.get_barrier_semaphore()

    def greet(step, _):
        pl.semaphore_signal(
            barrier, inc=1, device_id={"seq": lax.rem(me + step, n)}, device_id_type=MESH
        )
        return 0

    def greet_head(step, _):
        pl.semaphore_signal(
            barrier, inc=1, device_id={"head": lax.rem(me_head + step, nh)}, device_id_type=MESH
        )
        return 0

    lax.fori_loop(1, n, greet, 0)
    lax.fori_loop(1, nh, greet_head, 0)

    loads[0].wait()
    loads[1].wait()
    homes = home_ref[...]
    owners = lax.div(homes, jnp.full_like(homes, tok))
    docs = doc_ref[...].astype(F32)
    meta_ref[0:1, :] = owners.astype(F32)
    meta_ref[1:2, :] = (homes - owners * tok).astype(F32)
    meta_ref[2:3, :] = jnp.broadcast_to(docs[:, 0:1], (1, tok))
    meta_ref[3:4, :] = jnp.broadcast_to(docs[:, tok - 1 : tok], (1, tok))
    meta_ref[4:5, :] = docs
    meta_ref[5:8, :] = jnp.zeros((3, tok), F32)

    doc_row = jnp.broadcast_to(docs, (tok, tok))
    doc_col = doc_row.T
    first_doc, last_doc = meta_ref[2:3, :], meta_ref[3:4, :]
    place_row = lax.broadcasted_iota(jnp.int32, (tok, tok), 0)
    place_col = lax.broadcasted_iota(jnp.int32, (tok, tok), 1)
    visible = (doc_col == doc_row) & (place_col <= place_row)
    first_mask = doc_col == first_doc
    last_mask = doc_col == last_doc
    before = jnp.where(place_row < place_col, 1.0, 0.0).astype(BF16)
    metas[rows_at(me, 8), :] = meta_ref[...]

    def copy_meta(to, slot):
        return pltpu.make_async_remote_copy(
            src_ref=meta_ref, dst_ref=metas.at[rows_at(slot, 8)],
            send_sem=meta_sems.at[0, to], recv_sem=meta_sems.at[1, slot],
            device_id={"seq": to}, device_id_type=MESH,
        )

    def copy_rows(src, dst, sems, group, to, slot):
        return pltpu.make_async_remote_copy(
            src_ref=src.at[rows_at(group * n + to, cap)],
            dst_ref=dst.at[rows_at(group * n + slot, cap)],
            send_sem=sems.at[0, group, to], recv_sem=sems.at[1, group, slot],
            device_id={"seq": to}, device_id_type=MESH,
        )

    def others(body):
        def step(index, _):
            away = (index + 1) // 2
            body(lax.rem(me + n // 2 + away * (1 - 2 * lax.rem(index, 2)), n))
            return 0

        lax.fori_loop(0, n - 1, step, 0)

    def loop(count, body):
        def step(index, _):
            body(index)
            return 0

        lax.fori_loop(0, count, step, 0)

    def at_sub(block, part):
        return rows_from(block * quarter + part * sub, sub)

    def copy_near(sems, scan, src, dst, part, to, slot):
        return pltpu.make_async_remote_copy(
            src_ref=src.at[at_sub(to, part)], dst_ref=dst.at[at_sub(slot, part)],
            send_sem=sems.at[0, scan, to * SUBS + part],
            recv_sem=sems.at[1, scan, slot * SUBS + part],
            device_id={"seq": plane * PLANE + to}, device_id_type=MESH,
        )

    peers = [lax.rem(spot + step, PLANE) for step in range(1, PLANE)]

    def send_near(sems, scan, src, dst, part):
        for peer in peers:
            copy_near(sems, scan, src, dst, part, peer, spot).start()
        dst[at_sub(spot, part), :] = src[at_sub(spot, part), :]

    def got_near(sems, scan, src, dst, part):
        for peer in peers:
            copy_near(sems, scan, src, dst, part, peer, peer).wait_recv()

    def sent_near(sems, scan, src, dst, part):
        for peer in peers:
            copy_near(sems, scan, src, dst, part, peer, spot).wait_send()

    def copy_far(scan, total, far, part, ahead):
        sign = 1 if scan == 0 else -1
        return pltpu.make_async_remote_copy(
            src_ref=total.at[at_sub(0, part)], dst_ref=far.at[at_sub(ahead - 1, part)],
            send_sem=far_sems.at[0, scan, (ahead - 1) * SUBS + part],
            recv_sem=far_sems.at[1, scan, (ahead - 1) * SUBS + part],
            device_id={"seq": me + sign * ahead * PLANE}, device_id_type=MESH,
        )

    def sends(scan, ahead):
        return plane + ahead < planes if scan == 0 else plane >= ahead

    def gets(scan, ahead):
        return plane >= ahead if scan == 0 else plane + ahead < planes

    def doc(block, which):
        return metas[pl.ds(block * 8 + which, 1), :]

    scans = [
        (fw_own, fw_in, fw_total, fw_far, fw_send, fw_carry, 3, 2, list(range(PLANE)), -1),
        (rv_own, rv_in, rv_total, rv_far, rv_send, rv_carry, 2, 3, list(range(PLANE))[::-1], 1),
    ]
    for scan in range(2):
        far = scans[scan][3]
        for ahead in (1, 2):
            @pl.when(jnp.logical_not(gets(scan, ahead)))
            def _():
                far[(ahead - 1) * quarter : ahead * quarter, :] = jnp.zeros((quarter, HS), BF16)

    def chain(scan, part):
        own, arrived, total_ref, far, send, carry, leaving, entering, order, toward = scans[scan]
        got_near(near_sems, scan, own, arrived, part)

        @pl.when(gets(scan, 1))
        def _():
            copy_far(scan, total_ref, far, part, 1).wait_recv()

        total = far[at_sub(0, part), :].astype(F32)
        for block in order:
            here = plane * PLANE + block
            prior = doc(jnp.clip(here + toward, 0, n - 1), leaving)
            send[at_sub(block, part), :] = (total * same(doc(here, entering), prior)).astype(BF16)
            mine = arrived[at_sub(block, part), :].astype(F32)
            total = mine + total * same(doc(here, leaving), prior)
        total_ref[at_sub(0, part), :] = total.astype(BF16)

        @pl.when(sends(scan, 1))
        def _():
            copy_far(scan, total_ref, far, part, 1).start()

        send_near(carry_sems, scan, send, carry, part)

    def plane_total(scan, part):
        own, arrived, total_ref, far, _, _, leaving, _, order, toward = scans[scan]
        got_near(near_sems, scan, own, arrived, part)
        total = None
        for block in order:
            mine = arrived[at_sub(block, part), :].astype(F32)
            here = plane * PLANE + block
            if total is None:
                total = mine
            else:
                total = mine + total * same(doc(here, leaving), doc(here + toward, leaving))
        total_ref[at_sub(0, part), :] = total.astype(BF16)
        for ahead in (1, 2):
            @pl.when(sends(scan, ahead))
            def _():
                copy_far(scan, total_ref, far, part, ahead).start()

    def carries(scan, part):
        _, arrived, total_ref, far, send, carry, leaving, entering, order, toward = scans[scan]
        for ahead in (1, 2):
            @pl.when(gets(scan, ahead))
            def _():
                copy_far(scan, total_ref, far, part, ahead).wait_recv()

        def clamp(block):
            return jnp.clip(block, 0, n - 1)

        edge = plane * PLANE + order[0] + toward
        total = far[at_sub(0, part), :].astype(F32) + far[at_sub(1, part), :].astype(F32) * same(
            doc(clamp(edge), leaving), doc(clamp(edge + toward * PLANE), leaving)
        )
        for block in order:
            here = plane * PLANE + block
            prior = doc(clamp(here + toward), leaving)
            send[at_sub(block, part), :] = (total * same(doc(here, entering), prior)).astype(BF16)
            mine = arrived[at_sub(block, part), :].astype(F32)
            total = mine + total * same(doc(here, leaving), prior)
        send_near(carry_sems, scan, send, carry, part)

    def got_carry(scan, part):
        got_near(carry_sems, scan, scans[scan][4], scans[scan][5], part)

    def group_heads(part):
        return [(index, index * SUBS + part) for index in range(each)]

    def own_forward(part):
        for _, head in group_heads(part):
            at = rows_at(head, HS)
            kept = jnp.where(last_mask, k_ref[:, at].astype(F32), 0.0).astype(BF16)
            fw_own[at, :] = dot(kept, v_ref[:, at], 0, 0).astype(BF16)

    def inside(part):
        for _, head in group_heads(part):
            at = rows_at(head, HS)
            attn = jnp.where(visible, dot(q_ref[:, at], k_ref[:, at], 1, 1), 0.0).astype(BF16)
            attn_ref[at, :] = attn
            o_ref[:, at] = dot(attn, v_ref[:, at], 1, 0)

    loads[2].wait()
    loads[3].wait()
    own_forward(0)
    pl.semaphore_wait(barrier, (n - 1) + (nh - 1))
    others(lambda other: copy_meta(other, me).start())
    if aligned:
        send_near(near_sems, 0, fw_own, fw_in, 0)

        def own_step(index):
            own_forward(index + 1)
            send_near(near_sems, 0, fw_own, fw_in, index + 1)

        loop(SUBS - 1, own_step)
    else:
        loop(SUBS - 1, lambda index: own_forward(index + 1))
        loop(SUBS, lambda part: send_near(near_sems, 0, fw_own, fw_in, part))
    loads[4].wait()
    loop(SUBS // 2, inside)
    others(lambda other: copy_meta(other, other).wait_recv())
    loop(SUBS, lambda part: chain(0, part))
    loop(SUBS // 2, lambda part: inside(part + SUBS // 2))

    slots = lax.broadcasted_iota(jnp.int32, (cap, tok), 0).astype(F32)
    lanes = lax.broadcasted_iota(jnp.int32, (cap, tok), 1).astype(F32)

    def picks(owners, owner):
        chosen = jnp.broadcast_to(jnp.where(owners == owner, 1.0, 0.0), (cap, tok))
        rank = dot(chosen.astype(BF16), before, 1, 0)
        return jnp.where(rank == slots, chosen, 0.0)

    def pack(owner):
        pack_ref[rows_at(owner, cap), :] = picks(meta_ref[0:1, :], owner.astype(F32)).astype(BF16)

    def unpack(source):
        chosen = picks(metas[pl.ds(source * 8, 1), :], me.astype(F32))
        row = jnp.sum(chosen * metas[pl.ds(source * 8 + 1, 1), :], axis=1, keepdims=True)
        used = jnp.sum(chosen, axis=1, keepdims=True)
        unpack_ref[rows_at(source, cap), :] = (
            jnp.where(row == lanes, 1.0, 0.0) * used
        ).astype(BF16)

    loop(n, pack)
    loads[5].wait()
    loads[6].wait()
    if not aligned:
        loop(SUBS, lambda part: got_carry(0, part))

    def output_step(part, sums):
        squares, inner = sums
        if aligned:
            got_carry(0, part)
        for _, head in group_heads(part):
            at = rows_at(head, HS)
            add = dot(q_ref[:, at], fw_carry[at, :], 1, 0)
            total = o_ref[:, at] + jnp.where(first_mask, add, 0.0)
            o_ref[:, at] = total
            scaled = gain_ref[:, at] * gn_ref[:, at].astype(F32)
            squares, inner = squares + total * total, inner + scaled * total
        return squares, inner

    zero = jnp.zeros((tok, HS), F32)
    squares, inner = lax.fori_loop(0, SUBS, output_step, (zero, zero))
    squares = jnp.sum(squares, axis=1, keepdims=True)
    inner = jnp.sum(inner, axis=1, keepdims=True)
    pair = jnp.where(place_col < HS // 2, squares, inner)
    sums_out[...] = pair

    def sum_copy(to, slot):
        return pltpu.make_async_remote_copy(
            src_ref=sums_out, dst_ref=sums_in.at[rows_at(slot, tok)],
            send_sem=sum_sems.at[0, to], recv_sem=sum_sems.at[1, slot],
            device_id={"head": to}, device_id_type=MESH,
        )

    def sum_start(step, _):
        sum_copy(lax.rem(me_head + step, nh), me_head).start()
        return 0

    def sum_finish(step, total):
        other = lax.rem(me_head + step, nh)
        sum_copy(other, other).wait_recv()
        return total + sums_in[rows_at(other, tok), :]

    def sum_sent(step, _):
        sum_copy(lax.rem(me_head + step, nh), me_head).wait_send()
        return 0

    lax.fori_loop(1, nh, sum_start, 0)
    loop(n, unpack)
    pair = lax.fori_loop(1, nh, sum_finish, pair)
    full = HEADS * HS
    inv_rms = lax.rsqrt(pair[:, 0:1] / full + EPSILON)
    pull = inv_rms * inv_rms * inv_rms * pair[:, HS - 1 : HS] / full
    inv_rms = jnp.broadcast_to(inv_rms, (tok, HS))
    pull = jnp.broadcast_to(pull, (tok, HS))

    def own_reverse(part):
        for _, head in group_heads(part):
            at = rows_at(head, HS)
            scaled = gain_ref[:, at] * gn_ref[:, at].astype(F32)
            grad = (inv_rms * scaled - o_ref[:, at] * pull).astype(BF16)
            go_ref[:, at] = grad
            kept = jnp.where(first_mask, q_ref[:, at].astype(F32), 0.0).astype(BF16)
            rv_own[at, :] = dot(kept, grad, 0, 0).astype(BF16)
        if aligned:
            send_near(near_sems, 1, rv_own, rv_in, part)

    loop(SUBS, own_reverse)
    if not aligned:
        loop(SUBS, lambda part: send_near(near_sems, 1, rv_own, rv_in, part))

    half = SUBS // 2
    slots_all = n * cap

    def grad_query(group, part):
        for index, head in group_heads(group * half + part):
            at = rows_at(head, HS)
            grad = go_ref[:, at]
            back = jnp.where(visible, dot(grad, v_ref[:, at], 1, 1), 0.0).astype(BF16)
            back_ref[at, :] = back
            add = dot(grad, fw_carry[at, :], 1, 1)
            result = dot(back, k_ref[:, at], 1, 0) + jnp.where(first_mask, add, 0.0)
            bq_send[
                group * slots_all : (group + 1) * slots_all, rows_at(part * each + index, HS)
            ] = dot(pack_ref[...], result.astype(BF16), 1, 0).astype(BF16)

    def send_query(group):
        others(lambda other: copy_rows(bq_send, bq_in, q_sems, group, other, me).start())
        bq_in[rows_at(group * n + me, cap), :] = bq_send[rows_at(group * n + me, cap), :]

    loop(half, lambda part: grad_query(0, part))
    loop(SUBS, lambda part: plane_total(1, part))
    send_query(0)
    loop(half, lambda part: grad_query(1, part))
    send_query(1)

    def inside_back(part):
        for _, head in group_heads(part):
            at = rows_at(head, HS)
            gk_ref[:, at] = dot(back_ref[at, :], q_ref[:, at], 0, 0)
            gv_ref[:, at] = dot(attn_ref[at, :], go_ref[:, at], 0, 0)

    loop(SUBS, lambda part: carries(1, part))
    loop(SUBS, inside_back)
    if not aligned:
        loop(SUBS, lambda part: got_carry(1, part))

    def grad_pair(part):
        if aligned:
            got_carry(1, part)
        rows = rows_at(part, slots_all)
        for index, head in group_heads(part):
            at = rows_at(head, HS)
            carry = rv_carry[at, :]
            key = gk_ref[:, at] + jnp.where(last_mask, dot(v_ref[:, at], carry, 1, 1), 0.0)
            value = gv_ref[:, at] + jnp.where(last_mask, dot(k_ref[:, at], carry, 1, 0), 0.0)
            for which, result in enumerate((key, value)):
                column = (which * each + index) * HS
                bkv_send[rows, column : column + HS] = dot(
                    pack_ref[...], result.astype(BF16), 1, 0
                ).astype(BF16)
        others(lambda other: copy_rows(bkv_send, bkv_in, kv_sems, part, other, me).start())
        bkv_in[rows_at(part * n + me, cap), :] = bkv_send[rows_at(part * n + me, cap), :]

    loop(SUBS, grad_pair)

    def place_query(group, part):
        for index, head in group_heads(group * half + part):
            arrived = bq_in[
                group * slots_all : (group + 1) * slots_all, rows_at(part * each + index, HS)
            ]
            out_ref[0, :, rows_at(head, HS)] = dot(unpack_ref[...], arrived, 0, 0).astype(BF16)

    for group in range(2):
        others(lambda other: copy_rows(bq_send, bq_in, q_sems, group, other, other).wait_recv())
        loop(half, lambda part: place_query(group, part))

    def place_pair(part):
        others(lambda other: copy_rows(bkv_send, bkv_in, kv_sems, part, other, other).wait_recv())
        rows = rows_at(part, slots_all)
        for index, head in group_heads(part):
            for which in range(2):
                column = (which * each + index) * HS
                out_ref[which + 1, :, rows_at(head, HS)] = dot(
                    unpack_ref[...], bkv_in[rows, column : column + HS], 0, 0
                ).astype(BF16)

    loop(SUBS, place_pair)

    others(lambda other: copy_meta(other, me).wait_send())
    lax.fori_loop(1, nh, sum_sent, 0)
    for scan in range(2):
        own, arrived, total_ref, far, send, carry = scans[scan][:6]

        def drain(part):
            sent_near(near_sems, scan, own, arrived, part)
            sent_near(carry_sems, scan, send, carry, part)
            for ahead in (1, 2)[: scan + 1]:
                @pl.when(sends(scan, ahead))
                def _():
                    copy_far(scan, total_ref, far, part, ahead).wait_send()

        loop(SUBS, drain)
    for group in range(2):
        others(lambda other: copy_rows(bq_send, bq_in, q_sems, group, other, me).wait_send())
    loop(
        SUBS,
        lambda part: others(
            lambda other: copy_rows(bkv_send, bkv_in, kv_sems, part, other, me).wait_send()
        ),
    )


def local(n, nh, query, keys, values, grad_normed, norm_gain, doc_ids, home):
    tok, width = query.shape
    heads = width // HS
    cap = max(16, 2 * tok // n)
    states = pltpu.VMEM((heads * HS, HS), BF16)
    total = pltpu.VMEM((heads * HS // PLANE, HS), BF16)
    far = pltpu.VMEM((2 * heads * HS // PLANE, HS), BF16)
    scan = [states, states, total, far, states, states]
    block = pltpu.VMEM((tok, width), BF16)
    wide = pltpu.VMEM((tok, width), F32)
    map_rows = pltpu.VMEM((n * cap, tok), BF16)
    query_rows = pltpu.VMEM((2 * n * cap, width // 2), BF16)
    pair_rows = pltpu.VMEM((SUBS * n * cap, 2 * width // SUBS), BF16)
    dma = pltpu.SemaphoreType.DMA
    result = pl.pallas_call(
        functools.partial(kernel, n, nh, cap),
        out_shape=jax.ShapeDtypeStruct((3, tok, width), BF16),
        in_specs=[pl.BlockSpec(memory_space=pltpu.HBM)] * 7,
        out_specs=pl.BlockSpec(memory_space=pltpu.VMEM),
        scratch_shapes=[
            block, block, block, block,
            pltpu.VMEM((1, width), F32),
            pltpu.VMEM((1, tok), jnp.int32),
            pltpu.VMEM((1, tok), jnp.int32),
            pltpu.VMEM((8, tok), F32),
            pltpu.VMEM((n * 8, tok), F32),
            *scan, *scan,
            states, states,
            wide, block, wide, wide,
            pltpu.VMEM((tok, HS), F32),
            pltpu.VMEM((nh * tok, HS), F32),
            map_rows, map_rows,
            query_rows, query_rows, pair_rows, pair_rows,
            dma((7,)),
            dma((2, n)),
            dma((2, 2, PLANE * SUBS)),
            dma((2, 2, 2 * SUBS)),
            dma((2, 2, PLANE * SUBS)),
            dma((2, 2, n)),
            dma((2, SUBS, n)),
            dma((2, nh)),
        ],
        compiler_params=pltpu.CompilerParams(
            collective_id=0, has_side_effects=True, vmem_limit_bytes=56 * 1024 * 1024
        ),
    )(query, keys, values, grad_normed, norm_gain[None, :], doc_ids[None, :], home[None, :])
    return jnp.transpose(result, (1, 0, 2))


def solution(mesh):
    placed = (
        P("seq", "head"),
        P("seq", "head"),
        P("seq", "head"),
        P("seq", "head"),
        P("head"),
        P("seq"),
        P("seq"),
    )
    return jax.shard_map(
        functools.partial(local, mesh.shape["seq"], mesh.shape["head"]),
        mesh=mesh, in_specs=placed, out_specs=P("seq", None, "head"), check_vma=False,
    )
```

```python
import functools

import jax
import jax.numpy as jnp
from jax import lax
from jax.experimental import pallas as pl
from jax.experimental.pallas import tpu as pltpu
from jax.sharding import PartitionSpec as P

HEADS = 32
HS = 128
EPSILON = 1e-05
PLANE = 4
SUBS = 4
F32 = jnp.float32
BF16 = jnp.bfloat16


def dot(left, right, left_dim, right_dim):
    return lax.dot_general(
        left, right, (((left_dim,), (right_dim,)), ((), ())), preferred_element_type=F32
    )


def rows_at(index, size):
    return pl.ds(pl.multiple_of(index * size, size), size)


MESH = pl.DeviceIdType.MESH


def rows_from(offset, size):
    return pl.ds(pl.multiple_of(offset, size), size)


def same(left, right):
    return jnp.where(left == right, 1.0, 0.0)


def kernel(
    n, nh, cap,
    q_hbm, k_hbm, v_hbm, gn_hbm, gain_hbm, doc_hbm, home_hbm,
    out_ref,
    q_ref, k_ref, v_ref, gn_ref, gain_ref, doc_ref, home_ref,
    meta_ref, metas,
    fw_own, fw_in, fw_total, fw_far, fw_send, fw_carry,
    rv_own, rv_in, rv_total, rv_far, rv_send, rv_carry,
    attn_ref, back_ref, o_ref, go_ref, gk_ref, gv_ref, sums_out, sums_in,
    rank_ref, pack_ref, unpack_ref, place_ref, bq_send, bq_in, bkv_send, bkv_in,
    in_sem, meta_sems, near_sems, far_sems, carry_sems, q_sems, kv_sems, sum_sems,
):
    tok, width = q_ref.shape
    heads = width // HS
    quarter = heads * HS // PLANE
    sub = quarter // SUBS
    aligned = sub == HS
    each = heads // SUBS
    planes = n // PLANE
    me = lax.axis_index("seq")
    me_head = lax.axis_index("head")
    plane, spot = me // PLANE, lax.rem(me, PLANE)

    loads = [
        pltpu.make_async_copy(src, dst, in_sem.at[index])
        for index, (src, dst) in enumerate(
            [
                (doc_hbm, doc_ref), (home_hbm, home_ref), (k_hbm, k_ref), (v_hbm, v_ref),
                (q_hbm, q_ref), (gn_hbm, gn_ref), (gain_hbm, gain_ref),
            ]
        )
    ]
    for load in loads:
        load.start()

    barrier = pltpu.get_barrier_semaphore()

    def greet(step, _):
        pl.semaphore_signal(
            barrier, inc=1, device_id={"seq": lax.rem(me + step, n)}, device_id_type=MESH
        )
        return 0

    def greet_head(step, _):
        pl.semaphore_signal(
            barrier, inc=1, device_id={"head": lax.rem(me_head + step, nh)}, device_id_type=MESH
        )
        return 0

    lax.fori_loop(1, n, greet, 0)
    lax.fori_loop(1, nh, greet_head, 0)

    loads[0].wait()
    loads[1].wait()
    homes = home_ref[...]
    owners = lax.div(homes, jnp.full_like(homes, tok))
    docs = doc_ref[...].astype(F32)
    meta_ref[0:1, :] = owners.astype(F32)
    meta_ref[1:2, :] = (homes - owners * tok).astype(F32)
    meta_ref[2:3, :] = jnp.broadcast_to(docs[:, 0:1], (1, tok))
    meta_ref[3:4, :] = jnp.broadcast_to(docs[:, tok - 1 : tok], (1, tok))
    meta_ref[4:5, :] = docs
    meta_ref[5:8, :] = jnp.zeros((3, tok), F32)

    doc_row = jnp.broadcast_to(docs, (tok, tok))
    doc_col = doc_row.T
    first_doc, last_doc = meta_ref[2:3, :], meta_ref[3:4, :]
    place_row = lax.broadcasted_iota(jnp.int32, (tok, tok), 0)
    place_col = lax.broadcasted_iota(jnp.int32, (tok, tok), 1)
    visible = (doc_col == doc_row) & (place_col <= place_row)
    first_mask = doc_col == first_doc
    last_mask = doc_col == last_doc
    before = jnp.where(place_row < place_col, 1.0, 0.0).astype(BF16)
    metas[rows_at(me, 8), :] = meta_ref[...]

    def copy_meta(to, slot):
        return pltpu.make_async_remote_copy(
            src_ref=meta_ref, dst_ref=metas.at[rows_at(slot, 8)],
            send_sem=meta_sems.at[0, to], recv_sem=meta_sems.at[1, slot],
            device_id={"seq": to}, device_id_type=MESH,
        )

    def copy_rows(src, dst, sems, group, to, slot):
        return pltpu.make_async_remote_copy(
            src_ref=src.at[rows_at(group * n + to, cap)],
            dst_ref=dst.at[rows_at(group * n + slot, cap)],
            send_sem=sems.at[0, group, to], recv_sem=sems.at[1, group, slot],
            device_id={"seq": to}, device_id_type=MESH,
        )

    def others(body):
        def step(index, _):
            body(lax.rem(me + index, n))
            return 0

        lax.fori_loop(1, n, step, 0)

    def loop(count, body):
        def step(index, _):
            body(index)
            return 0

        lax.fori_loop(0, count, step, 0)

    def at_sub(block, part):
        return rows_from(block * quarter + part * sub, sub)

    def copy_near(sems, scan, src, dst, part, to, slot):
        return pltpu.make_async_remote_copy(
            src_ref=src.at[at_sub(to, part)], dst_ref=dst.at[at_sub(slot, part)],
            send_sem=sems.at[0, scan, to * SUBS + part],
            recv_sem=sems.at[1, scan, slot * SUBS + part],
            device_id={"seq": plane * PLANE + to}, device_id_type=MESH,
        )

    peers = [lax.rem(spot + step, PLANE) for step in range(1, PLANE)]

    def send_near(sems, scan, src, dst, part):
        for peer in peers:
            copy_near(sems, scan, src, dst, part, peer, spot).start()
        dst[at_sub(spot, part), :] = src[at_sub(spot, part), :]

    def got_near(sems, scan, src, dst, part):
        for peer in peers:
            copy_near(sems, scan, src, dst, part, peer, peer).wait_recv()

    def sent_near(sems, scan, src, dst, part):
        for peer in peers:
            copy_near(sems, scan, src, dst, part, peer, spot).wait_send()

    def copy_far(scan, total, far, part, ahead):
        sign = 1 if scan == 0 else -1
        return pltpu.make_async_remote_copy(
            src_ref=total.at[at_sub(0, part)], dst_ref=far.at[at_sub(ahead - 1, part)],
            send_sem=far_sems.at[0, scan, (ahead - 1) * SUBS + part],
            recv_sem=far_sems.at[1, scan, (ahead - 1) * SUBS + part],
            device_id={"seq": me + sign * ahead * PLANE}, device_id_type=MESH,
        )

    def sends(scan, ahead):
        return plane + ahead < planes if scan == 0 else plane >= ahead

    def gets(scan, ahead):
        return plane >= ahead if scan == 0 else plane + ahead < planes

    def doc(block, which):
        return metas[pl.ds(block * 8 + which, 1), :]

    scans = [
        (fw_own, fw_in, fw_total, fw_far, fw_send, fw_carry, 3, 2, list(range(PLANE)), -1),
        (rv_own, rv_in, rv_total, rv_far, rv_send, rv_carry, 2, 3, list(range(PLANE))[::-1], 1),
    ]
    for scan in range(2):
        far = scans[scan][3]
        for ahead in (1, 2):
            @pl.when(jnp.logical_not(gets(scan, ahead)))
            def _():
                far[(ahead - 1) * quarter : ahead * quarter, :] = jnp.zeros((quarter, HS), BF16)

    def chain(scan, part):
        own, arrived, total_ref, far, send, carry, leaving, entering, order, toward = scans[scan]
        got_near(near_sems, scan, own, arrived, part)

        @pl.when(gets(scan, 1))
        def _():
            copy_far(scan, total_ref, far, part, 1).wait_recv()

        total = far[at_sub(0, part), :].astype(F32)
        for block in order:
            here = plane * PLANE + block
            prior = doc(jnp.clip(here + toward, 0, n - 1), leaving)
            send[at_sub(block, part), :] = (total * same(doc(here, entering), prior)).astype(BF16)
            mine = arrived[at_sub(block, part), :].astype(F32)
            total = mine + total * same(doc(here, leaving), prior)
        total_ref[at_sub(0, part), :] = total.astype(BF16)

        @pl.when(sends(scan, 1))
        def _():
            copy_far(scan, total_ref, far, part, 1).start()

        send_near(carry_sems, scan, send, carry, part)

    def plane_total(scan, part):
        own, arrived, total_ref, far, _, _, leaving, _, order, toward = scans[scan]
        got_near(near_sems, scan, own, arrived, part)
        total = None
        for block in order:
            mine = arrived[at_sub(block, part), :].astype(F32)
            here = plane * PLANE + block
            if total is None:
                total = mine
            else:
                total = mine + total * same(doc(here, leaving), doc(here + toward, leaving))
        total_ref[at_sub(0, part), :] = total.astype(BF16)
        for ahead in (1, 2):
            @pl.when(sends(scan, ahead))
            def _():
                copy_far(scan, total_ref, far, part, ahead).start()

    def carries(scan, part):
        _, arrived, total_ref, far, send, carry, leaving, entering, order, toward = scans[scan]
        for ahead in (1, 2):
            @pl.when(gets(scan, ahead))
            def _():
                copy_far(scan, total_ref, far, part, ahead).wait_recv()

        def clamp(block):
            return jnp.clip(block, 0, n - 1)

        edge = plane * PLANE + order[0] + toward
        total = far[at_sub(0, part), :].astype(F32) + far[at_sub(1, part), :].astype(F32) * same(
            doc(clamp(edge), leaving), doc(clamp(edge + toward * PLANE), leaving)
        )
        for block in order:
            here = plane * PLANE + block
            prior = doc(clamp(here + toward), leaving)
            send[at_sub(block, part), :] = (total * same(doc(here, entering), prior)).astype(BF16)
            mine = arrived[at_sub(block, part), :].astype(F32)
            total = mine + total * same(doc(here, leaving), prior)
        send_near(carry_sems, scan, send, carry, part)

    def got_carry(scan, part):
        got_near(carry_sems, scan, scans[scan][4], scans[scan][5], part)

    def group_heads(part):
        return [(index, index * SUBS + part) for index in range(each)]

    def own_forward(part):
        for _, head in group_heads(part):
            at = rows_at(head, HS)
            kept = jnp.where(last_mask, k_ref[:, at].astype(F32), 0.0).astype(BF16)
            fw_own[at, :] = dot(kept, v_ref[:, at], 0, 0).astype(BF16)

    def inside(part):
        for _, head in group_heads(part):
            at = rows_at(head, HS)
            attn = jnp.where(visible, dot(q_ref[:, at], k_ref[:, at], 1, 1), 0.0).astype(BF16)
            attn_ref[at, :] = attn
            o_ref[:, at] = dot(attn, v_ref[:, at], 1, 0)

    loads[2].wait()
    loads[3].wait()
    own_forward(0)
    pl.semaphore_wait(barrier, (n - 1) + (nh - 1))
    if aligned:
        send_near(near_sems, 0, fw_own, fw_in, 0)

        def own_step(index):
            own_forward(index + 1)
            send_near(near_sems, 0, fw_own, fw_in, index + 1)

        loop(SUBS - 1, own_step)
    else:
        loop(SUBS - 1, lambda index: own_forward(index + 1))
        loop(SUBS, lambda part: send_near(near_sems, 0, fw_own, fw_in, part))
    others(lambda other: copy_meta(other, me).start())
    slots = lax.broadcasted_iota(jnp.int32, (cap, tok), 0).astype(F32)
    lanes = lax.broadcasted_iota(jnp.int32, (cap, tok), 1).astype(F32)

    def picks(owners, owner):
        chosen = jnp.broadcast_to(jnp.where(owners == owner, 1.0, 0.0), (cap, tok))
        rank = dot(chosen.astype(BF16), before, 1, 0)
        return jnp.where(rank == slots, chosen, 0.0)

    owner_row = meta_ref[0:1, :]
    owner_of = lax.broadcasted_iota(jnp.int32, (n, tok), 0).astype(F32)
    rank_ref[...] = dot(same(owner_row, owner_of).astype(BF16), before, 1, 0)

    def pack(owner):
        rank = rank_ref[pl.ds(owner, 1), :]
        chosen = same(owner_row, owner.astype(F32))
        pack_ref[rows_at(owner, cap), :] = (same(rank, slots) * chosen).astype(BF16)

    loads[4].wait()
    loop(SUBS // 2, inside)
    loop(n, pack)
    others(lambda other: copy_meta(other, other).wait_recv())
    loop(SUBS, lambda part: chain(0, part))
    loop(SUBS // 2, lambda part: inside(part + SUBS // 2))

    def unpack(source):
        chosen = picks(metas[pl.ds(source * 8, 1), :], me.astype(F32))
        row = jnp.sum(chosen * metas[pl.ds(source * 8 + 1, 1), :], axis=1, keepdims=True)
        used = jnp.sum(chosen, axis=1, keepdims=True)
        unpack_ref[rows_at(source, cap), :] = (
            jnp.where(row == lanes, 1.0, 0.0) * used
        ).astype(BF16)

    loads[5].wait()
    loads[6].wait()
    if not aligned:
        loop(SUBS, lambda part: got_carry(0, part))

    def output_step(part, sums):
        squares, inner = sums
        if aligned:
            got_carry(0, part)
        for _, head in group_heads(part):
            at = rows_at(head, HS)
            add = dot(q_ref[:, at], fw_carry[at, :], 1, 0)
            total = o_ref[:, at] + jnp.where(first_mask, add, 0.0)
            o_ref[:, at] = total
            scaled = gain_ref[:, at] * gn_ref[:, at].astype(F32)
            squares, inner = squares + total * total, inner + scaled * total
        return squares, inner

    zero = jnp.zeros((tok, HS), F32)
    squares, inner = lax.fori_loop(0, SUBS, output_step, (zero, zero))
    squares = jnp.sum(squares, axis=1, keepdims=True)
    inner = jnp.sum(inner, axis=1, keepdims=True)
    pair = jnp.where(place_col < HS // 2, squares, inner)
    sums_out[...] = pair

    def sum_copy(to, slot):
        return pltpu.make_async_remote_copy(
            src_ref=sums_out, dst_ref=sums_in.at[rows_at(slot, tok)],
            send_sem=sum_sems.at[0, to], recv_sem=sum_sems.at[1, slot],
            device_id={"head": to}, device_id_type=MESH,
        )

    def sum_start(step, _):
        sum_copy(lax.rem(me_head + step, nh), me_head).start()
        return 0

    def sum_finish(step, total):
        other = lax.rem(me_head + step, nh)
        sum_copy(other, other).wait_recv()
        return total + sums_in[rows_at(other, tok), :]

    def sum_sent(step, _):
        sum_copy(lax.rem(me_head + step, nh), me_head).wait_send()
        return 0

    lax.fori_loop(1, nh, sum_start, 0)
    pair = lax.fori_loop(1, nh, sum_finish, pair)
    full = HEADS * HS
    inv_rms = lax.rsqrt(pair[:, 0:1] / full + EPSILON)
    pull = inv_rms * inv_rms * inv_rms * pair[:, HS - 1 : HS] / full
    inv_rms = jnp.broadcast_to(inv_rms, (tok, HS))
    pull = jnp.broadcast_to(pull, (tok, HS))

    def own_reverse(part):
        for _, head in group_heads(part):
            at = rows_at(head, HS)
            scaled = gain_ref[:, at] * gn_ref[:, at].astype(F32)
            grad = (inv_rms * scaled - o_ref[:, at] * pull).astype(BF16)
            go_ref[:, at] = grad
            kept = jnp.where(first_mask, q_ref[:, at].astype(F32), 0.0).astype(BF16)
            rv_own[at, :] = dot(kept, grad, 0, 0).astype(BF16)
        if aligned:
            send_near(near_sems, 1, rv_own, rv_in, part)

    loop(SUBS, own_reverse)
    if not aligned:
        loop(SUBS, lambda part: send_near(near_sems, 1, rv_own, rv_in, part))

    half = SUBS // 2
    slots_all = n * cap

    def grad_query(group, part):
        made = []
        for index, head in group_heads(group * half + part):
            at = rows_at(head, HS)
            grad = go_ref[:, at]
            back = jnp.where(visible, dot(grad, v_ref[:, at], 1, 1), 0.0).astype(BF16)
            back_ref[at, :] = back
            add = dot(grad, fw_carry[at, :], 1, 1)
            result = dot(back, k_ref[:, at], 1, 0) + jnp.where(first_mask, add, 0.0)
            made.append(result.astype(BF16))
        bq_send[group * slots_all : (group + 1) * slots_all, rows_at(part, each * HS)] = dot(
            pack_ref[...], jnp.concatenate(made, axis=1), 1, 0
        ).astype(BF16)

    def send_query(group):
        others(lambda other: copy_rows(bq_send, bq_in, q_sems, group, other, me).start())
        bq_in[rows_at(group * n + me, cap), :] = bq_send[rows_at(group * n + me, cap), :]

    loop(half, lambda part: grad_query(0, part))
    loop(SUBS, lambda part: plane_total(1, part))
    send_query(0)
    loop(half, lambda part: grad_query(1, part))
    send_query(1)

    def inside_back(part):
        for _, head in group_heads(part):
            at = rows_at(head, HS)
            gk_ref[:, at] = dot(back_ref[at, :], q_ref[:, at], 0, 0)
            gv_ref[:, at] = dot(attn_ref[at, :], go_ref[:, at], 0, 0)

    loop(SUBS, lambda part: carries(1, part))
    loop(SUBS, inside_back)
    if not aligned:
        loop(SUBS, lambda part: got_carry(1, part))

    def grad_pair(part):
        if aligned:
            got_carry(1, part)
        made = [[], []]
        for index, head in group_heads(part):
            at = rows_at(head, HS)
            carry = rv_carry[at, :]
            key = gk_ref[:, at] + jnp.where(last_mask, dot(v_ref[:, at], carry, 1, 1), 0.0)
            value = gv_ref[:, at] + jnp.where(last_mask, dot(k_ref[:, at], carry, 1, 0), 0.0)
            made[0].append(key.astype(BF16))
            made[1].append(value.astype(BF16))
        bkv_send[rows_at(part, slots_all), :] = dot(
            pack_ref[...], jnp.concatenate(made[0] + made[1], axis=1), 1, 0
        ).astype(BF16)
        others(lambda other: copy_rows(bkv_send, bkv_in, kv_sems, part, other, me).start())
        bkv_in[rows_at(part * n + me, cap), :] = bkv_send[rows_at(part * n + me, cap), :]

    loop(SUBS, grad_pair)

    loop(n, unpack)
    place_ref[...] = unpack_ref[...].T

    def place_query(group, part):
        arrived = bq_in[group * slots_all : (group + 1) * slots_all, rows_at(part, each * HS)]
        placed = dot(place_ref[...], arrived, 1, 0).astype(BF16)
        for index, head in group_heads(group * half + part):
            out_ref[0, :, rows_at(head, HS)] = placed[:, index * HS : (index + 1) * HS]

    for group in range(2):
        others(lambda other: copy_rows(bq_send, bq_in, q_sems, group, other, other).wait_recv())
        loop(half, lambda part: place_query(group, part))

    def place_pair(part):
        others(lambda other: copy_rows(bkv_send, bkv_in, kv_sems, part, other, other).wait_recv())
        placed = dot(place_ref[...], bkv_in[rows_at(part, slots_all), :], 1, 0).astype(BF16)
        for index, head in group_heads(part):
            for which in range(2):
                column = (which * each + index) * HS
                out_ref[which + 1, :, rows_at(head, HS)] = placed[:, column : column + HS]

    loop(SUBS, place_pair)

    others(lambda other: copy_meta(other, me).wait_send())
    lax.fori_loop(1, nh, sum_sent, 0)
    for scan in range(2):
        own, arrived, total_ref, far, send, carry = scans[scan][:6]

        def drain(part):
            sent_near(near_sems, scan, own, arrived, part)
            sent_near(carry_sems, scan, send, carry, part)
            for ahead in (1, 2)[: scan + 1]:
                @pl.when(sends(scan, ahead))
                def _():
                    copy_far(scan, total_ref, far, part, ahead).wait_send()

        loop(SUBS, drain)
    for group in range(2):
        others(lambda other: copy_rows(bq_send, bq_in, q_sems, group, other, me).wait_send())
    loop(
        SUBS,
        lambda part: others(
            lambda other: copy_rows(bkv_send, bkv_in, kv_sems, part, other, me).wait_send()
        ),
    )


def local(n, nh, query, keys, values, grad_normed, norm_gain, doc_ids, home):
    tok, width = query.shape
    heads = width // HS
    cap = max(16, 2 * tok // n)
    states = pltpu.VMEM((heads * HS, HS), BF16)
    total = pltpu.VMEM((heads * HS // PLANE, HS), BF16)
    far = pltpu.VMEM((2 * heads * HS // PLANE, HS), BF16)
    scan = [states, states, total, far, states, states]
    block = pltpu.VMEM((tok, width), BF16)
    wide = pltpu.VMEM((tok, width), F32)
    map_rows = pltpu.VMEM((n * cap, tok), BF16)
    query_rows = pltpu.VMEM((2 * n * cap, width // 2), BF16)
    pair_rows = pltpu.VMEM((SUBS * n * cap, 2 * width // SUBS), BF16)
    dma = pltpu.SemaphoreType.DMA
    result = pl.pallas_call(
        functools.partial(kernel, n, nh, cap),
        out_shape=jax.ShapeDtypeStruct((3, tok, width), BF16),
        in_specs=[pl.BlockSpec(memory_space=pltpu.HBM)] * 7,
        out_specs=pl.BlockSpec(memory_space=pltpu.VMEM),
        scratch_shapes=[
            block, block, block, block,
            pltpu.VMEM((1, width), F32),
            pltpu.VMEM((1, tok), jnp.int32),
            pltpu.VMEM((1, tok), jnp.int32),
            pltpu.VMEM((8, tok), F32),
            pltpu.VMEM((n * 8, tok), F32),
            *scan, *scan,
            states, states,
            wide, block, wide, wide,
            pltpu.VMEM((tok, HS), F32),
            pltpu.VMEM((nh * tok, HS), F32),
            pltpu.VMEM((n, tok), F32),
            map_rows, map_rows,
            pltpu.VMEM((tok, n * cap), BF16),
            query_rows, query_rows, pair_rows, pair_rows,
            dma((7,)),
            dma((2, n)),
            dma((2, 2, PLANE * SUBS)),
            dma((2, 2, 2 * SUBS)),
            dma((2, 2, PLANE * SUBS)),
            dma((2, 2, n)),
            dma((2, SUBS, n)),
            dma((2, nh)),
        ],
        compiler_params=pltpu.CompilerParams(
            collective_id=0, has_side_effects=True, vmem_limit_bytes=56 * 1024 * 1024
        ),
    )(query, keys, values, grad_normed, norm_gain[None, :], doc_ids[None, :], home[None, :])
    return jnp.transpose(result, (1, 0, 2))


def solution(mesh):
    placed = (
        P("seq", "head"),
        P("seq", "head"),
        P("seq", "head"),
        P("seq", "head"),
        P("head"),
        P("seq"),
        P("seq"),
    )
    return jax.shard_map(
        functools.partial(local, mesh.shape["seq"], mesh.shape["head"]),
        mesh=mesh, in_specs=placed, out_specs=P("seq", None, "head"), check_vma=False,
    )
```

```python
import functools

import jax
import jax.numpy as jnp
from jax import lax
from jax.experimental import pallas as pl
from jax.experimental.pallas import tpu as pltpu
from jax.sharding import PartitionSpec as P

HEADS = 32
HS = 128
EPSILON = 1e-05
PLANE = 4
SUBS = 4
F32 = jnp.float32
BF16 = jnp.bfloat16


def dot(left, right, left_dim, right_dim):
    return lax.dot_general(
        left, right, (((left_dim,), (right_dim,)), ((), ())), preferred_element_type=F32
    )


def rows_at(index, size):
    return pl.ds(pl.multiple_of(index * size, size), size)


MESH = pl.DeviceIdType.MESH


def rows_from(offset, size):
    return pl.ds(pl.multiple_of(offset, size), size)


def same(left, right):
    return jnp.where(left == right, 1.0, 0.0)


def kernel(
    n, nh, cap,
    q_hbm, k_hbm, v_hbm, gn_hbm, gain_hbm, doc_hbm, home_hbm,
    out_ref,
    q_ref, k_ref, v_ref, gn_ref, gain_ref, doc_ref, home_ref,
    meta_ref, metas,
    fw_own, fw_in, fw_total, fw_far, fw_send, fw_carry,
    rv_own, rv_in, rv_total, rv_far, rv_send, rv_carry,
    attn_ref, back_ref, o_ref, go_ref, gk_ref, gv_ref, sums_out, sums_in,
    rank_ref, pack_ref, unpack_ref, place_ref, bq_send, bq_in, bkv_send, bkv_in,
    in_sem, meta_sems, near_sems, far_sems, carry_sems, q_sems, kv_sems, sum_sems,
):
    tok, width = q_ref.shape
    heads = width // HS
    quarter = heads * HS // PLANE
    sub = quarter // SUBS
    aligned = sub == HS
    each = heads // SUBS
    planes = n // PLANE
    me = lax.axis_index("seq")
    me_head = lax.axis_index("head")
    plane, spot = me // PLANE, lax.rem(me, PLANE)

    loads = [
        pltpu.make_async_copy(src, dst, in_sem.at[index])
        for index, (src, dst) in enumerate(
            [
                (doc_hbm, doc_ref), (home_hbm, home_ref), (k_hbm, k_ref), (v_hbm, v_ref),
                (q_hbm, q_ref), (gn_hbm, gn_ref), (gain_hbm, gain_ref),
            ]
        )
    ]
    for load in loads:
        load.start()

    barrier = pltpu.get_barrier_semaphore()

    def greet(step, _):
        pl.semaphore_signal(
            barrier, inc=1, device_id={"seq": lax.rem(me + step, n)}, device_id_type=MESH
        )
        return 0

    def greet_head(step, _):
        pl.semaphore_signal(
            barrier, inc=1, device_id={"head": lax.rem(me_head + step, nh)}, device_id_type=MESH
        )
        return 0

    lax.fori_loop(1, n, greet, 0)
    lax.fori_loop(1, nh, greet_head, 0)

    loads[0].wait()
    loads[1].wait()
    homes = home_ref[...]
    owners = lax.div(homes, jnp.full_like(homes, tok))
    docs = doc_ref[...].astype(F32)
    meta_ref[0:1, :] = owners.astype(F32)
    meta_ref[1:2, :] = (homes - owners * tok).astype(F32)
    meta_ref[2:3, :] = jnp.broadcast_to(docs[:, 0:1], (1, tok))
    meta_ref[3:4, :] = jnp.broadcast_to(docs[:, tok - 1 : tok], (1, tok))
    meta_ref[4:5, :] = docs
    meta_ref[5:8, :] = jnp.zeros((3, tok), F32)

    doc_row = jnp.broadcast_to(docs, (tok, tok))
    doc_col = doc_row.T
    first_doc, last_doc = meta_ref[2:3, :], meta_ref[3:4, :]
    place_row = lax.broadcasted_iota(jnp.int32, (tok, tok), 0)
    place_col = lax.broadcasted_iota(jnp.int32, (tok, tok), 1)
    visible = (doc_col == doc_row) & (place_col <= place_row)
    first_mask = doc_col == first_doc
    last_mask = doc_col == last_doc
    before = jnp.where(place_row < place_col, 1.0, 0.0).astype(BF16)
    metas[rows_at(me, 8), :] = meta_ref[...]

    def copy_meta(to, slot):
        return pltpu.make_async_remote_copy(
            src_ref=meta_ref, dst_ref=metas.at[rows_at(slot, 8)],
            send_sem=meta_sems.at[0, to], recv_sem=meta_sems.at[1, slot],
            device_id={"seq": to}, device_id_type=MESH,
        )

    def copy_rows(src, dst, sems, group, to, slot):
        return pltpu.make_async_remote_copy(
            src_ref=src.at[rows_at(group * n + to, cap)],
            dst_ref=dst.at[rows_at(group * n + slot, cap)],
            send_sem=sems.at[0, group, to], recv_sem=sems.at[1, group, slot],
            device_id={"seq": to}, device_id_type=MESH,
        )

    def others(body):
        def step(index, _):
            body(lax.rem(me + index, n))
            return 0

        lax.fori_loop(1, n, step, 0)

    def loop(count, body):
        def step(index, _):
            body(index)
            return 0

        lax.fori_loop(0, count, step, 0)

    def at_sub(block, part):
        return rows_from(block * quarter + part * sub, sub)

    def copy_near(sems, scan, src, dst, part, to, slot):
        return pltpu.make_async_remote_copy(
            src_ref=src.at[at_sub(to, part)], dst_ref=dst.at[at_sub(slot, part)],
            send_sem=sems.at[0, scan, to * SUBS + part],
            recv_sem=sems.at[1, scan, slot * SUBS + part],
            device_id={"seq": plane * PLANE + to}, device_id_type=MESH,
        )

    peers = [lax.rem(spot + step, PLANE) for step in range(1, PLANE)]

    def send_near(sems, scan, src, dst, part):
        for peer in peers:
            copy_near(sems, scan, src, dst, part, peer, spot).start()
        dst[at_sub(spot, part), :] = src[at_sub(spot, part), :]

    def got_near(sems, scan, src, dst, part):
        for peer in peers:
            copy_near(sems, scan, src, dst, part, peer, peer).wait_recv()

    def sent_near(sems, scan, src, dst, part):
        for peer in peers:
            copy_near(sems, scan, src, dst, part, peer, spot).wait_send()

    def copy_far(scan, total, far, part):
        sign = 1 if scan == 0 else -1
        return pltpu.make_async_remote_copy(
            src_ref=total.at[at_sub(0, part)], dst_ref=far.at[at_sub(0, part)],
            send_sem=far_sems.at[0, scan, part], recv_sem=far_sems.at[1, scan, part],
            device_id={"seq": me + sign * PLANE}, device_id_type=MESH,
        )

    def sends(scan):
        return plane + 1 < planes if scan == 0 else plane >= 1

    def gets(scan):
        return plane >= 1 if scan == 0 else plane + 1 < planes

    def doc(block, which):
        return metas[pl.ds(block * 8 + which, 1), :]

    scans = [
        (fw_own, fw_in, fw_total, fw_far, fw_send, fw_carry, 3, 2, list(range(PLANE)), -1),
        (rv_own, rv_in, rv_total, rv_far, rv_send, rv_carry, 2, 3, list(range(PLANE))[::-1], 1),
    ]
    for scan in range(2):
        far = scans[scan][3]

        @pl.when(jnp.logical_not(gets(scan)))
        def _():
            far[...] = jnp.zeros((quarter, HS), BF16)

    def chain(scan, part):
        own, arrived, total_ref, far, send, carry, leaving, entering, order, toward = scans[scan]
        got_near(near_sems, scan, own, arrived, part)

        @pl.when(gets(scan))
        def _():
            copy_far(scan, total_ref, far, part).wait_recv()

        total = far[at_sub(0, part), :].astype(F32)
        for block in order:
            here = plane * PLANE + block
            prior = doc(jnp.clip(here + toward, 0, n - 1), leaving)
            send[at_sub(block, part), :] = (total * same(doc(here, entering), prior)).astype(BF16)
            mine = arrived[at_sub(block, part), :].astype(F32)
            total = mine + total * same(doc(here, leaving), prior)
        total_ref[at_sub(0, part), :] = total.astype(BF16)

        @pl.when(sends(scan))
        def _():
            copy_far(scan, total_ref, far, part).start()

        send_near(carry_sems, scan, send, carry, part)

    def got_carry(scan, part):
        got_near(carry_sems, scan, scans[scan][4], scans[scan][5], part)

    def group_heads(part):
        return [(index, index * SUBS + part) for index in range(each)]

    def own_forward(part):
        for _, head in group_heads(part):
            at = rows_at(head, HS)
            kept = jnp.where(last_mask, k_ref[:, at].astype(F32), 0.0).astype(BF16)
            fw_own[at, :] = dot(kept, v_ref[:, at], 0, 0).astype(BF16)

    def inside(part):
        for _, head in group_heads(part):
            at = rows_at(head, HS)
            attn = jnp.where(visible, dot(q_ref[:, at], k_ref[:, at], 1, 1), 0.0).astype(BF16)
            attn_ref[at, :] = attn
            o_ref[:, at] = dot(attn, v_ref[:, at], 1, 0)

    loads[2].wait()
    loads[3].wait()
    own_forward(0)
    pl.semaphore_wait(barrier, (n - 1) + (nh - 1))
    if aligned:
        send_near(near_sems, 0, fw_own, fw_in, 0)

        def own_step(index):
            own_forward(index + 1)
            send_near(near_sems, 0, fw_own, fw_in, index + 1)

        loop(SUBS - 1, own_step)
    else:
        loop(SUBS - 1, lambda index: own_forward(index + 1))
        loop(SUBS, lambda part: send_near(near_sems, 0, fw_own, fw_in, part))
    others(lambda other: copy_meta(other, me).start())
    slots = lax.broadcasted_iota(jnp.int32, (cap, tok), 0).astype(F32)
    lanes = lax.broadcasted_iota(jnp.int32, (cap, tok), 1).astype(F32)

    def picks(owners, owner):
        chosen = jnp.broadcast_to(jnp.where(owners == owner, 1.0, 0.0), (cap, tok))
        rank = dot(chosen.astype(BF16), before, 1, 0)
        return jnp.where(rank == slots, chosen, 0.0)

    owner_row = meta_ref[0:1, :]
    owner_of = lax.broadcasted_iota(jnp.int32, (n, tok), 0).astype(F32)
    rank_ref[...] = dot(same(owner_row, owner_of).astype(BF16), before, 1, 0)

    def pack(owner):
        rank = rank_ref[pl.ds(owner, 1), :]
        chosen = same(owner_row, owner.astype(F32))
        pack_ref[rows_at(owner, cap), :] = (same(rank, slots) * chosen).astype(BF16)

    loads[4].wait()
    loop(SUBS // 2, inside)
    loop(n, pack)
    others(lambda other: copy_meta(other, other).wait_recv())
    loop(SUBS, lambda part: chain(0, part))
    loop(SUBS // 2, lambda part: inside(part + SUBS // 2))

    def unpack(source):
        chosen = picks(metas[pl.ds(source * 8, 1), :], me.astype(F32))
        row = jnp.sum(chosen * metas[pl.ds(source * 8 + 1, 1), :], axis=1, keepdims=True)
        used = jnp.sum(chosen, axis=1, keepdims=True)
        unpack_ref[rows_at(source, cap), :] = (
            jnp.where(row == lanes, 1.0, 0.0) * used
        ).astype(BF16)

    loads[5].wait()
    loads[6].wait()
    if not aligned:
        loop(SUBS, lambda part: got_carry(0, part))

    def output_step(part, sums):
        squares, inner = sums
        if aligned:
            got_carry(0, part)
        for _, head in group_heads(part):
            at = rows_at(head, HS)
            add = dot(q_ref[:, at], fw_carry[at, :], 1, 0)
            total = o_ref[:, at] + jnp.where(first_mask, add, 0.0)
            o_ref[:, at] = total
            scaled = gain_ref[:, at] * gn_ref[:, at].astype(F32)
            squares, inner = squares + total * total, inner + scaled * total
        return squares, inner

    zero = jnp.zeros((tok, HS), F32)
    squares, inner = lax.fori_loop(0, SUBS, output_step, (zero, zero))
    squares = jnp.sum(squares, axis=1, keepdims=True)
    inner = jnp.sum(inner, axis=1, keepdims=True)
    pair = jnp.where(place_col < HS // 2, squares, inner)
    sums_out[...] = pair

    def sum_copy(to, slot):
        return pltpu.make_async_remote_copy(
            src_ref=sums_out, dst_ref=sums_in.at[rows_at(slot, tok)],
            send_sem=sum_sems.at[0, to], recv_sem=sum_sems.at[1, slot],
            device_id={"head": to}, device_id_type=MESH,
        )

    def sum_start(step, _):
        sum_copy(lax.rem(me_head + step, nh), me_head).start()
        return 0

    def sum_finish(step, total):
        other = lax.rem(me_head + step, nh)
        sum_copy(other, other).wait_recv()
        return total + sums_in[rows_at(other, tok), :]

    def sum_sent(step, _):
        sum_copy(lax.rem(me_head + step, nh), me_head).wait_send()
        return 0

    lax.fori_loop(1, nh, sum_start, 0)
    pair = lax.fori_loop(1, nh, sum_finish, pair)
    full = HEADS * HS
    inv_rms = lax.rsqrt(pair[:, 0:1] / full + EPSILON)
    pull = inv_rms * inv_rms * inv_rms * pair[:, HS - 1 : HS] / full
    inv_rms = jnp.broadcast_to(inv_rms, (tok, HS))
    pull = jnp.broadcast_to(pull, (tok, HS))

    def own_reverse(part):
        for _, head in group_heads(part):
            at = rows_at(head, HS)
            scaled = gain_ref[:, at] * gn_ref[:, at].astype(F32)
            grad = (inv_rms * scaled - o_ref[:, at] * pull).astype(BF16)
            go_ref[:, at] = grad
            kept = jnp.where(first_mask, q_ref[:, at].astype(F32), 0.0).astype(BF16)
            rv_own[at, :] = dot(kept, grad, 0, 0).astype(BF16)
        if aligned:
            send_near(near_sems, 1, rv_own, rv_in, part)

    loop(SUBS, own_reverse)
    if not aligned:
        loop(SUBS, lambda part: send_near(near_sems, 1, rv_own, rv_in, part))

    half = SUBS // 2
    slots_all = n * cap

    def grad_query(group, part):
        made = []
        for index, head in group_heads(group * half + part):
            at = rows_at(head, HS)
            grad = go_ref[:, at]
            back = jnp.where(visible, dot(grad, v_ref[:, at], 1, 1), 0.0).astype(BF16)
            back_ref[at, :] = back
            add = dot(grad, fw_carry[at, :], 1, 1)
            result = dot(back, k_ref[:, at], 1, 0) + jnp.where(first_mask, add, 0.0)
            made.append(result.astype(BF16))
        bq_send[group * slots_all : (group + 1) * slots_all, rows_at(part, each * HS)] = dot(
            pack_ref[...], jnp.concatenate(made, axis=1), 1, 0
        ).astype(BF16)

    def send_query(group):
        others(lambda other: copy_rows(bq_send, bq_in, q_sems, group, other, me).start())
        bq_in[rows_at(group * n + me, cap), :] = bq_send[rows_at(group * n + me, cap), :]

    for group in range(2):
        loop(half, lambda part: grad_query(group, part))
    loop(SUBS, lambda part: chain(1, part))
    for group in range(2):
        send_query(group)

    def inside_back(part):
        for _, head in group_heads(part):
            at = rows_at(head, HS)
            gk_ref[:, at] = dot(back_ref[at, :], q_ref[:, at], 0, 0)
            gv_ref[:, at] = dot(attn_ref[at, :], go_ref[:, at], 0, 0)

    loop(SUBS, inside_back)
    if not aligned:
        loop(SUBS, lambda part: got_carry(1, part))

    def grad_pair(part):
        if aligned:
            got_carry(1, part)
        made = [[], []]
        for index, head in group_heads(part):
            at = rows_at(head, HS)
            carry = rv_carry[at, :]
            key = gk_ref[:, at] + jnp.where(last_mask, dot(v_ref[:, at], carry, 1, 1), 0.0)
            value = gv_ref[:, at] + jnp.where(last_mask, dot(k_ref[:, at], carry, 1, 0), 0.0)
            made[0].append(key.astype(BF16))
            made[1].append(value.astype(BF16))
        bkv_send[rows_at(part, slots_all), :] = dot(
            pack_ref[...], jnp.concatenate(made[0] + made[1], axis=1), 1, 0
        ).astype(BF16)
        others(lambda other: copy_rows(bkv_send, bkv_in, kv_sems, part, other, me).start())
        bkv_in[rows_at(part * n + me, cap), :] = bkv_send[rows_at(part * n + me, cap), :]

    loop(SUBS, grad_pair)

    loop(n, unpack)
    place_ref[...] = unpack_ref[...].T

    def place_query(group, part):
        arrived = bq_in[group * slots_all : (group + 1) * slots_all, rows_at(part, each * HS)]
        placed = dot(place_ref[...], arrived, 1, 0).astype(BF16)
        for index, head in group_heads(group * half + part):
            out_ref[0, :, rows_at(head, HS)] = placed[:, index * HS : (index + 1) * HS]

    for group in range(2):
        others(lambda other: copy_rows(bq_send, bq_in, q_sems, group, other, other).wait_recv())
        loop(half, lambda part: place_query(group, part))

    def place_pair(part):
        others(lambda other: copy_rows(bkv_send, bkv_in, kv_sems, part, other, other).wait_recv())
        placed = dot(place_ref[...], bkv_in[rows_at(part, slots_all), :], 1, 0).astype(BF16)
        for index, head in group_heads(part):
            for which in range(2):
                column = (which * each + index) * HS
                out_ref[which + 1, :, rows_at(head, HS)] = placed[:, column : column + HS]

    loop(SUBS, place_pair)

    others(lambda other: copy_meta(other, me).wait_send())
    lax.fori_loop(1, nh, sum_sent, 0)
    for scan in range(2):
        own, arrived, total_ref, far, send, carry = scans[scan][:6]

        def drain(part):
            sent_near(near_sems, scan, own, arrived, part)
            sent_near(carry_sems, scan, send, carry, part)

            @pl.when(sends(scan))
            def _():
                copy_far(scan, total_ref, far, part).wait_send()

        loop(SUBS, drain)
    for group in range(2):
        others(lambda other: copy_rows(bq_send, bq_in, q_sems, group, other, me).wait_send())
    loop(
        SUBS,
        lambda part: others(
            lambda other: copy_rows(bkv_send, bkv_in, kv_sems, part, other, me).wait_send()
        ),
    )


def local(n, nh, query, keys, values, grad_normed, norm_gain, doc_ids, home):
    tok, width = query.shape
    heads = width // HS
    cap = max(16, 2 * tok // n)
    states = pltpu.VMEM((heads * HS, HS), BF16)
    total = pltpu.VMEM((heads * HS // PLANE, HS), BF16)
    far = pltpu.VMEM((heads * HS // PLANE, HS), BF16)
    scan = [states, states, total, far, states, states]
    block = pltpu.VMEM((tok, width), BF16)
    wide = pltpu.VMEM((tok, width), F32)
    map_rows = pltpu.VMEM((n * cap, tok), BF16)
    query_rows = pltpu.VMEM((2 * n * cap, width // 2), BF16)
    pair_rows = pltpu.VMEM((SUBS * n * cap, 2 * width // SUBS), BF16)
    dma = pltpu.SemaphoreType.DMA
    result = pl.pallas_call(
        functools.partial(kernel, n, nh, cap),
        out_shape=jax.ShapeDtypeStruct((3, tok, width), BF16),
        in_specs=[pl.BlockSpec(memory_space=pltpu.HBM)] * 7,
        out_specs=pl.BlockSpec(memory_space=pltpu.VMEM),
        scratch_shapes=[
            block, block, block, block,
            pltpu.VMEM((1, width), F32),
            pltpu.VMEM((1, tok), jnp.int32),
            pltpu.VMEM((1, tok), jnp.int32),
            pltpu.VMEM((8, tok), F32),
            pltpu.VMEM((n * 8, tok), F32),
            *scan, *scan,
            states, states,
            wide, block, wide, wide,
            pltpu.VMEM((tok, HS), F32),
            pltpu.VMEM((nh * tok, HS), F32),
            pltpu.VMEM((n, tok), F32),
            map_rows, map_rows,
            pltpu.VMEM((tok, n * cap), BF16),
            query_rows, query_rows, pair_rows, pair_rows,
            dma((7,)),
            dma((2, n)),
            dma((2, 2, PLANE * SUBS)),
            dma((2, 2, SUBS)),
            dma((2, 2, PLANE * SUBS)),
            dma((2, 2, n)),
            dma((2, SUBS, n)),
            dma((2, nh)),
        ],
        compiler_params=pltpu.CompilerParams(
            collective_id=0, has_side_effects=True, vmem_limit_bytes=56 * 1024 * 1024
        ),
    )(query, keys, values, grad_normed, norm_gain[None, :], doc_ids[None, :], home[None, :])
    return jnp.transpose(result, (1, 0, 2))


def solution(mesh):
    placed = (
        P("seq", "head"),
        P("seq", "head"),
        P("seq", "head"),
        P("seq", "head"),
        P("head"),
        P("seq"),
        P("seq"),
    )
    return jax.shard_map(
        functools.partial(local, mesh.shape["seq"], mesh.shape["head"]),
        mesh=mesh, in_specs=placed, out_specs=P("seq", None, "head"), check_vma=False,
    )
```

```python
import functools

import jax
import jax.numpy as jnp
from jax import lax
from jax.experimental import pallas as pl
from jax.experimental.pallas import tpu as pltpu
from jax.sharding import PartitionSpec as P

HEADS = 32
HS = 128
EPSILON = 1e-05
PLANE = 4
SUBS = 4
F32 = jnp.float32
BF16 = jnp.bfloat16


def dot(left, right, left_dim, right_dim):
    return lax.dot_general(
        left, right, (((left_dim,), (right_dim,)), ((), ())), preferred_element_type=F32
    )


def rows_at(index, size):
    return pl.ds(pl.multiple_of(index * size, size), size)


MESH = pl.DeviceIdType.MESH


def rows_from(offset, size):
    return pl.ds(pl.multiple_of(offset, size), size)


def same(left, right):
    return jnp.where(left == right, 1.0, 0.0)


def kernel(
    n, nh, cap,
    q_hbm, k_hbm, v_hbm, gn_hbm, gain_hbm, doc_hbm, home_hbm,
    out_ref,
    q_ref, k_ref, v_ref, gn_ref, gain_ref, doc_ref, home_ref,
    meta_ref, metas,
    fw_own, fw_in, fw_total, fw_far, fw_send, fw_carry,
    rv_own, rv_in, rv_total, rv_far, rv_send, rv_carry,
    attn_ref, back_ref, o_ref, go_ref, gk_ref, gv_ref, sums_out, sums_in,
    rank_ref, pack_ref, unpack_ref, place_ref, bq_send, bq_in, bkv_send, bkv_in,
    in_sem, meta_sems, near_sems, far_sems, carry_sems, q_sems, kv_sems, sum_sems,
):
    tok, width = q_ref.shape
    heads = width // HS
    quarter = heads * HS // PLANE
    sub = quarter // SUBS
    aligned = sub == HS
    each = heads // SUBS
    planes = n // PLANE
    me = lax.axis_index("seq")
    me_head = lax.axis_index("head")
    plane, spot = me // PLANE, lax.rem(me, PLANE)

    loads = [
        pltpu.make_async_copy(src, dst, in_sem.at[index])
        for index, (src, dst) in enumerate(
            [
                (doc_hbm, doc_ref), (home_hbm, home_ref), (k_hbm, k_ref), (v_hbm, v_ref),
                (q_hbm, q_ref), (gn_hbm, gn_ref), (gain_hbm, gain_ref),
            ]
        )
    ]
    for load in loads:
        load.start()

    barrier = pltpu.get_barrier_semaphore()

    def greet(step, _):
        pl.semaphore_signal(
            barrier, inc=1, device_id={"seq": lax.rem(me + step, n)}, device_id_type=MESH
        )
        return 0

    def greet_head(step, _):
        pl.semaphore_signal(
            barrier, inc=1, device_id={"head": lax.rem(me_head + step, nh)}, device_id_type=MESH
        )
        return 0

    lax.fori_loop(1, n, greet, 0)
    lax.fori_loop(1, nh, greet_head, 0)

    loads[0].wait()
    loads[1].wait()
    homes = home_ref[...]
    owners = lax.div(homes, jnp.full_like(homes, tok))
    docs = doc_ref[...].astype(F32)
    meta_ref[0:1, :] = owners.astype(F32)
    meta_ref[1:2, :] = (homes - owners * tok).astype(F32)
    meta_ref[2:3, :] = jnp.broadcast_to(docs[:, 0:1], (1, tok))
    meta_ref[3:4, :] = jnp.broadcast_to(docs[:, tok - 1 : tok], (1, tok))
    meta_ref[4:5, :] = docs
    meta_ref[5:8, :] = jnp.zeros((3, tok), F32)

    doc_row = jnp.broadcast_to(docs, (tok, tok))
    doc_col = doc_row.T
    first_doc, last_doc = meta_ref[2:3, :], meta_ref[3:4, :]
    place_row = lax.broadcasted_iota(jnp.int32, (tok, tok), 0)
    place_col = lax.broadcasted_iota(jnp.int32, (tok, tok), 1)
    visible = (doc_col == doc_row) & (place_col <= place_row)
    first_mask = doc_col == first_doc
    last_mask = doc_col == last_doc
    before = jnp.where(place_row < place_col, 1.0, 0.0).astype(BF16)
    metas[rows_at(me, 8), :] = meta_ref[...]

    def copy_meta(to, slot):
        return pltpu.make_async_remote_copy(
            src_ref=meta_ref, dst_ref=metas.at[rows_at(slot, 8)],
            send_sem=meta_sems.at[0, to], recv_sem=meta_sems.at[1, slot],
            device_id={"seq": to}, device_id_type=MESH,
        )

    def copy_rows(src, dst, sems, group, to, slot):
        return pltpu.make_async_remote_copy(
            src_ref=src.at[rows_at(group * n + to, cap)],
            dst_ref=dst.at[rows_at(group * n + slot, cap)],
            send_sem=sems.at[0, group, to], recv_sem=sems.at[1, group, slot],
            device_id={"seq": to}, device_id_type=MESH,
        )

    def others(body):
        def step(index, _):
            body(lax.rem(me + index, n))
            return 0

        lax.fori_loop(1, n, step, 0)

    def loop(count, body):
        def step(index, _):
            body(index)
            return 0

        lax.fori_loop(0, count, step, 0)

    def at_sub(block, part):
        return rows_from(block * quarter + part * sub, sub)

    def copy_near(sems, scan, src, dst, part, to, slot):
        return pltpu.make_async_remote_copy(
            src_ref=src.at[at_sub(to, part)], dst_ref=dst.at[at_sub(slot, part)],
            send_sem=sems.at[0, scan, to * SUBS + part],
            recv_sem=sems.at[1, scan, slot * SUBS + part],
            device_id={"seq": plane * PLANE + to}, device_id_type=MESH,
        )

    peers = [lax.rem(spot + step, PLANE) for step in range(1, PLANE)]

    def send_near(sems, scan, src, dst, part):
        for peer in peers:
            copy_near(sems, scan, src, dst, part, peer, spot).start()
        dst[at_sub(spot, part), :] = src[at_sub(spot, part), :]

    def got_near(sems, scan, src, dst, part):
        for peer in peers:
            copy_near(sems, scan, src, dst, part, peer, peer).wait_recv()

    def sent_near(sems, scan, src, dst, part):
        for peer in peers:
            copy_near(sems, scan, src, dst, part, peer, spot).wait_send()

    def copy_far(scan, total, far, part, ahead):
        sign = 1 if scan == 0 else -1
        return pltpu.make_async_remote_copy(
            src_ref=total.at[at_sub(0, part)], dst_ref=far.at[at_sub(ahead - 1, part)],
            send_sem=far_sems.at[0, scan, (ahead - 1) * SUBS + part],
            recv_sem=far_sems.at[1, scan, (ahead - 1) * SUBS + part],
            device_id={"seq": me + sign * ahead * PLANE}, device_id_type=MESH,
        )

    def sends(scan, ahead):
        return plane + ahead < planes if scan == 0 else plane >= ahead

    def gets(scan, ahead):
        return plane >= ahead if scan == 0 else plane + ahead < planes

    def doc(block, which):
        return metas[pl.ds(block * 8 + which, 1), :]

    scans = [
        (fw_own, fw_in, fw_total, fw_far, fw_send, fw_carry, 3, 2, list(range(PLANE)), -1),
        (rv_own, rv_in, rv_total, rv_far, rv_send, rv_carry, 2, 3, list(range(PLANE))[::-1], 1),
    ]
    for scan in range(2):
        far = scans[scan][3]
        for ahead in (1, 2):
            @pl.when(jnp.logical_not(gets(scan, ahead)))
            def _():
                far[(ahead - 1) * quarter : ahead * quarter, :] = jnp.zeros((quarter, HS), BF16)

    def plane_total(scan, part):
        own, arrived, total_ref, far, _, _, leaving, _, order, toward = scans[scan]
        got_near(near_sems, scan, own, arrived, part)
        total = None
        for block in order:
            mine = arrived[at_sub(block, part), :].astype(F32)
            here = plane * PLANE + block
            if total is None:
                total = mine
            else:
                total = mine + total * same(doc(here, leaving), doc(here + toward, leaving))
        total_ref[at_sub(0, part), :] = total.astype(BF16)
        for ahead in (1, 2):
            @pl.when(sends(scan, ahead))
            def _():
                copy_far(scan, total_ref, far, part, ahead).start()

    def carries(scan, part):
        _, arrived, total_ref, far, send, carry, leaving, entering, order, toward = scans[scan]
        for ahead in (1, 2):
            @pl.when(gets(scan, ahead))
            def _():
                copy_far(scan, total_ref, far, part, ahead).wait_recv()

        def clamp(block):
            return jnp.clip(block, 0, n - 1)

        edge = plane * PLANE + order[0] + toward
        total = far[at_sub(0, part), :].astype(F32) + far[at_sub(1, part), :].astype(F32) * same(
            doc(clamp(edge), leaving), doc(clamp(edge + toward * PLANE), leaving)
        )
        for block in order:
            here = plane * PLANE + block
            prior = doc(clamp(here + toward), leaving)
            send[at_sub(block, part), :] = (total * same(doc(here, entering), prior)).astype(BF16)
            mine = arrived[at_sub(block, part), :].astype(F32)
            total = mine + total * same(doc(here, leaving), prior)
        send_near(carry_sems, scan, send, carry, part)

    def got_carry(scan, part):
        got_near(carry_sems, scan, scans[scan][4], scans[scan][5], part)

    def group_heads(part):
        return [(index, index * SUBS + part) for index in range(each)]

    def own_forward(part):
        for _, head in group_heads(part):
            at = rows_at(head, HS)
            kept = jnp.where(last_mask, k_ref[:, at].astype(F32), 0.0).astype(BF16)
            fw_own[at, :] = dot(kept, v_ref[:, at], 0, 0).astype(BF16)

    def inside(part):
        for _, head in group_heads(part):
            at = rows_at(head, HS)
            attn = jnp.where(visible, dot(q_ref[:, at], k_ref[:, at], 1, 1), 0.0).astype(BF16)
            attn_ref[at, :] = attn
            o_ref[:, at] = dot(attn, v_ref[:, at], 1, 0)

    loads[2].wait()
    loads[3].wait()
    own_forward(0)
    pl.semaphore_wait(barrier, (n - 1) + (nh - 1))
    if aligned:
        send_near(near_sems, 0, fw_own, fw_in, 0)

        def own_step(index):
            own_forward(index + 1)
            send_near(near_sems, 0, fw_own, fw_in, index + 1)

        loop(SUBS - 1, own_step)
    else:
        loop(SUBS - 1, lambda index: own_forward(index + 1))
        loop(SUBS, lambda part: send_near(near_sems, 0, fw_own, fw_in, part))
    others(lambda other: copy_meta(other, me).start())
    slots = lax.broadcasted_iota(jnp.int32, (cap, tok), 0).astype(F32)
    lanes = lax.broadcasted_iota(jnp.int32, (cap, tok), 1).astype(F32)

    def picks(owners, owner):
        chosen = jnp.broadcast_to(jnp.where(owners == owner, 1.0, 0.0), (cap, tok))
        rank = dot(chosen.astype(BF16), before, 1, 0)
        return jnp.where(rank == slots, chosen, 0.0)

    owner_row = meta_ref[0:1, :]
    owner_of = lax.broadcasted_iota(jnp.int32, (n, tok), 0).astype(F32)
    rank_ref[...] = dot(same(owner_row, owner_of).astype(BF16), before, 1, 0)

    def pack(owner):
        rank = rank_ref[pl.ds(owner, 1), :]
        chosen = same(owner_row, owner.astype(F32))
        pack_ref[rows_at(owner, cap), :] = (same(rank, slots) * chosen).astype(BF16)

    loads[4].wait()
    loop(SUBS // 2, inside)
    loop(n, pack)
    others(lambda other: copy_meta(other, other).wait_recv())
    loop(SUBS, lambda part: plane_total(0, part))
    loop(SUBS // 2, lambda part: inside(part + SUBS // 2))

    def unpack(source):
        chosen = picks(metas[pl.ds(source * 8, 1), :], me.astype(F32))
        row = jnp.sum(chosen * metas[pl.ds(source * 8 + 1, 1), :], axis=1, keepdims=True)
        used = jnp.sum(chosen, axis=1, keepdims=True)
        unpack_ref[rows_at(source, cap), :] = (
            jnp.where(row == lanes, 1.0, 0.0) * used
        ).astype(BF16)

    loop(SUBS, lambda part: carries(0, part))
    loads[5].wait()
    loads[6].wait()
    if not aligned:
        loop(SUBS, lambda part: got_carry(0, part))

    def output_step(part, sums):
        squares, inner = sums
        if aligned:
            got_carry(0, part)
        for _, head in group_heads(part):
            at = rows_at(head, HS)
            add = dot(q_ref[:, at], fw_carry[at, :], 1, 0)
            total = o_ref[:, at] + jnp.where(first_mask, add, 0.0)
            o_ref[:, at] = total
            scaled = gain_ref[:, at] * gn_ref[:, at].astype(F32)
            squares, inner = squares + total * total, inner + scaled * total
        return squares, inner

    zero = jnp.zeros((tok, HS), F32)
    squares, inner = lax.fori_loop(0, SUBS, output_step, (zero, zero))
    squares = jnp.sum(squares, axis=1, keepdims=True)
    inner = jnp.sum(inner, axis=1, keepdims=True)
    pair = jnp.where(place_col < HS // 2, squares, inner)
    sums_out[...] = pair

    def sum_copy(to, slot):
        return pltpu.make_async_remote_copy(
            src_ref=sums_out, dst_ref=sums_in.at[rows_at(slot, tok)],
            send_sem=sum_sems.at[0, to], recv_sem=sum_sems.at[1, slot],
            device_id={"head": to}, device_id_type=MESH,
        )

    def sum_start(step, _):
        sum_copy(lax.rem(me_head + step, nh), me_head).start()
        return 0

    def sum_finish(step, total):
        other = lax.rem(me_head + step, nh)
        sum_copy(other, other).wait_recv()
        return total + sums_in[rows_at(other, tok), :]

    def sum_sent(step, _):
        sum_copy(lax.rem(me_head + step, nh), me_head).wait_send()
        return 0

    lax.fori_loop(1, nh, sum_start, 0)
    pair = lax.fori_loop(1, nh, sum_finish, pair)
    full = HEADS * HS
    inv_rms = lax.rsqrt(pair[:, 0:1] / full + EPSILON)
    pull = inv_rms * inv_rms * inv_rms * pair[:, HS - 1 : HS] / full
    inv_rms = jnp.broadcast_to(inv_rms, (tok, HS))
    pull = jnp.broadcast_to(pull, (tok, HS))

    def own_reverse(part):
        for _, head in group_heads(part):
            at = rows_at(head, HS)
            scaled = gain_ref[:, at] * gn_ref[:, at].astype(F32)
            grad = (inv_rms * scaled - o_ref[:, at] * pull).astype(BF16)
            go_ref[:, at] = grad
            kept = jnp.where(first_mask, q_ref[:, at].astype(F32), 0.0).astype(BF16)
            rv_own[at, :] = dot(kept, grad, 0, 0).astype(BF16)
        if aligned:
            send_near(near_sems, 1, rv_own, rv_in, part)

    loop(SUBS, own_reverse)
    if not aligned:
        loop(SUBS, lambda part: send_near(near_sems, 1, rv_own, rv_in, part))

    half = SUBS // 2
    slots_all = n * cap

    def grad_query(group, part):
        made = []
        for index, head in group_heads(group * half + part):
            at = rows_at(head, HS)
            grad = go_ref[:, at]
            back = jnp.where(visible, dot(grad, v_ref[:, at], 1, 1), 0.0).astype(BF16)
            back_ref[at, :] = back
            add = dot(grad, fw_carry[at, :], 1, 1)
            result = dot(back, k_ref[:, at], 1, 0) + jnp.where(first_mask, add, 0.0)
            made.append(result.astype(BF16))
        bq_send[group * slots_all : (group + 1) * slots_all, rows_at(part, each * HS)] = dot(
            pack_ref[...], jnp.concatenate(made, axis=1), 1, 0
        ).astype(BF16)

    def send_query(group):
        others(lambda other: copy_rows(bq_send, bq_in, q_sems, group, other, me).start())
        bq_in[rows_at(group * n + me, cap), :] = bq_send[rows_at(group * n + me, cap), :]

    loop(half, lambda part: grad_query(0, part))
    send_query(0)
    loop(SUBS, lambda part: plane_total(1, part))
    loop(half, lambda part: grad_query(1, part))
    send_query(1)

    def inside_back(part):
        for _, head in group_heads(part):
            at = rows_at(head, HS)
            gk_ref[:, at] = dot(back_ref[at, :], q_ref[:, at], 0, 0)
            gv_ref[:, at] = dot(attn_ref[at, :], go_ref[:, at], 0, 0)

    loop(SUBS, lambda part: carries(1, part))
    loop(SUBS, inside_back)
    if not aligned:
        loop(SUBS, lambda part: got_carry(1, part))

    def grad_pair(part):
        if aligned:
            got_carry(1, part)
        made = [[], []]
        for index, head in group_heads(part):
            at = rows_at(head, HS)
            carry = rv_carry[at, :]
            key = gk_ref[:, at] + jnp.where(last_mask, dot(v_ref[:, at], carry, 1, 1), 0.0)
            value = gv_ref[:, at] + jnp.where(last_mask, dot(k_ref[:, at], carry, 1, 0), 0.0)
            made[0].append(key.astype(BF16))
            made[1].append(value.astype(BF16))
        bkv_send[rows_at(part, slots_all), :] = dot(
            pack_ref[...], jnp.concatenate(made[0] + made[1], axis=1), 1, 0
        ).astype(BF16)
        others(lambda other: copy_rows(bkv_send, bkv_in, kv_sems, part, other, me).start())
        bkv_in[rows_at(part * n + me, cap), :] = bkv_send[rows_at(part * n + me, cap), :]

    loop(SUBS, grad_pair)

    loop(n, unpack)
    place_ref[...] = unpack_ref[...].T

    def place_query(group, part):
        arrived = bq_in[group * slots_all : (group + 1) * slots_all, rows_at(part, each * HS)]
        placed = dot(place_ref[...], arrived, 1, 0).astype(BF16)
        for index, head in group_heads(group * half + part):
            out_ref[0, :, rows_at(head, HS)] = placed[:, index * HS : (index + 1) * HS]

    for group in range(2):
        others(lambda other: copy_rows(bq_send, bq_in, q_sems, group, other, other).wait_recv())
        loop(half, lambda part: place_query(group, part))

    def place_pair(part):
        others(lambda other: copy_rows(bkv_send, bkv_in, kv_sems, part, other, other).wait_recv())
        placed = dot(place_ref[...], bkv_in[rows_at(part, slots_all), :], 1, 0).astype(BF16)
        for index, head in group_heads(part):
            for which in range(2):
                column = (which * each + index) * HS
                out_ref[which + 1, :, rows_at(head, HS)] = placed[:, column : column + HS]

    loop(SUBS, place_pair)

    others(lambda other: copy_meta(other, me).wait_send())
    lax.fori_loop(1, nh, sum_sent, 0)
    for scan in range(2):
        own, arrived, total_ref, far, send, carry = scans[scan][:6]

        def drain(part):
            sent_near(near_sems, scan, own, arrived, part)
            sent_near(carry_sems, scan, send, carry, part)
            for ahead in (1, 2):
                @pl.when(sends(scan, ahead))
                def _():
                    copy_far(scan, total_ref, far, part, ahead).wait_send()

        loop(SUBS, drain)
    for group in range(2):
        others(lambda other: copy_rows(bq_send, bq_in, q_sems, group, other, me).wait_send())
    loop(
        SUBS,
        lambda part: others(
            lambda other: copy_rows(bkv_send, bkv_in, kv_sems, part, other, me).wait_send()
        ),
    )


def local(n, nh, query, keys, values, grad_normed, norm_gain, doc_ids, home):
    tok, width = query.shape
    heads = width // HS
    cap = max(16, 2 * tok // n)
    states = pltpu.VMEM((heads * HS, HS), BF16)
    total = pltpu.VMEM((heads * HS // PLANE, HS), BF16)
    far = pltpu.VMEM((2 * heads * HS // PLANE, HS), BF16)
    scan = [states, states, total, far, states, states]
    block = pltpu.VMEM((tok, width), BF16)
    wide = pltpu.VMEM((tok, width), F32)
    map_rows = pltpu.VMEM((n * cap, tok), BF16)
    query_rows = pltpu.VMEM((2 * n * cap, width // 2), BF16)
    pair_rows = pltpu.VMEM((SUBS * n * cap, 2 * width // SUBS), BF16)
    dma = pltpu.SemaphoreType.DMA
    result = pl.pallas_call(
        functools.partial(kernel, n, nh, cap),
        out_shape=jax.ShapeDtypeStruct((3, tok, width), BF16),
        in_specs=[pl.BlockSpec(memory_space=pltpu.HBM)] * 7,
        out_specs=pl.BlockSpec(memory_space=pltpu.VMEM),
        scratch_shapes=[
            block, block, block, block,
            pltpu.VMEM((1, width), F32),
            pltpu.VMEM((1, tok), jnp.int32),
            pltpu.VMEM((1, tok), jnp.int32),
            pltpu.VMEM((8, tok), F32),
            pltpu.VMEM((n * 8, tok), F32),
            *scan, *scan,
            states, states,
            wide, block, wide, wide,
            pltpu.VMEM((tok, HS), F32),
            pltpu.VMEM((nh * tok, HS), F32),
            pltpu.VMEM((n, tok), F32),
            map_rows, map_rows,
            pltpu.VMEM((tok, n * cap), BF16),
            query_rows, query_rows, pair_rows, pair_rows,
            dma((7,)),
            dma((2, n)),
            dma((2, 2, PLANE * SUBS)),
            dma((2, 2, 2 * SUBS)),
            dma((2, 2, PLANE * SUBS)),
            dma((2, 2, n)),
            dma((2, SUBS, n)),
            dma((2, nh)),
        ],
        compiler_params=pltpu.CompilerParams(
            collective_id=0, has_side_effects=True, vmem_limit_bytes=56 * 1024 * 1024
        ),
    )(query, keys, values, grad_normed, norm_gain[None, :], doc_ids[None, :], home[None, :])
    return jnp.transpose(result, (1, 0, 2))


def solution(mesh):
    placed = (
        P("seq", "head"),
        P("seq", "head"),
        P("seq", "head"),
        P("seq", "head"),
        P("head"),
        P("seq"),
        P("seq"),
    )
    return jax.shard_map(
        functools.partial(local, mesh.shape["seq"], mesh.shape["head"]),
        mesh=mesh, in_specs=placed, out_specs=P("seq", None, "head"), check_vma=False,
    )
```

```python
import functools

import jax
import jax.numpy as jnp
from jax import lax
from jax.experimental import pallas as pl
from jax.experimental.pallas import tpu as pltpu
from jax.sharding import PartitionSpec as P

HEADS = 32
HS = 128
EPSILON = 1e-05
PLANE = 4
SUBS = 4
F32 = jnp.float32
BF16 = jnp.bfloat16


def dot(left, right, left_dim, right_dim):
    return lax.dot_general(
        left, right, (((left_dim,), (right_dim,)), ((), ())), preferred_element_type=F32
    )


def rows_at(index, size):
    return pl.ds(pl.multiple_of(index * size, size), size)


MESH = pl.DeviceIdType.MESH


def rows_from(offset, size):
    return pl.ds(pl.multiple_of(offset, size), size)


def same(left, right):
    return jnp.where(left == right, 1.0, 0.0)


def kernel(
    n, nh, cap,
    q_hbm, k_hbm, v_hbm, gn_hbm, gain_hbm, doc_hbm, home_hbm,
    out_ref,
    q_ref, k_ref, v_ref, gn_ref, gain_ref, doc_ref, home_ref,
    meta_ref, metas,
    fw_own, fw_in, fw_total, fw_far, fw_send, fw_carry,
    rv_own, rv_in, rv_total, rv_far, rv_send, rv_carry,
    attn_ref, back_ref, o_ref, go_ref, gk_ref, gv_ref, sums_out, sums_in,
    rank_ref, pack_ref, unpack_ref, place_ref, bq_send, bq_in, bkv_send, bkv_in,
    in_sem, meta_sems, near_sems, far_sems, carry_sems, q_sems, kv_sems, sum_sems,
):
    tok, width = q_ref.shape
    heads = width // HS
    quarter = heads * HS // PLANE
    sub = quarter // SUBS
    aligned = sub == HS
    each = heads // SUBS
    planes = n // PLANE
    me = lax.axis_index("seq")
    me_head = lax.axis_index("head")
    plane, spot = me // PLANE, lax.rem(me, PLANE)

    loads = [
        pltpu.make_async_copy(src, dst, in_sem.at[index])
        for index, (src, dst) in enumerate(
            [
                (doc_hbm, doc_ref), (home_hbm, home_ref), (k_hbm, k_ref), (v_hbm, v_ref),
                (q_hbm, q_ref), (gn_hbm, gn_ref), (gain_hbm, gain_ref),
            ]
        )
    ]
    for load in loads:
        load.start()

    barrier = pltpu.get_barrier_semaphore()

    def greet(step, _):
        pl.semaphore_signal(
            barrier, inc=1, device_id={"seq": lax.rem(me + step, n)}, device_id_type=MESH
        )
        return 0

    def greet_head(step, _):
        pl.semaphore_signal(
            barrier, inc=1, device_id={"head": lax.rem(me_head + step, nh)}, device_id_type=MESH
        )
        return 0

    lax.fori_loop(1, n, greet, 0)
    lax.fori_loop(1, nh, greet_head, 0)

    loads[0].wait()
    loads[1].wait()
    homes = home_ref[...]
    owners = lax.div(homes, jnp.full_like(homes, tok))
    docs = doc_ref[...].astype(F32)
    meta_ref[0:1, :] = owners.astype(F32)
    meta_ref[1:2, :] = (homes - owners * tok).astype(F32)
    meta_ref[2:3, :] = jnp.broadcast_to(docs[:, 0:1], (1, tok))
    meta_ref[3:4, :] = jnp.broadcast_to(docs[:, tok - 1 : tok], (1, tok))
    meta_ref[4:5, :] = docs
    meta_ref[5:8, :] = jnp.zeros((3, tok), F32)

    doc_row = jnp.broadcast_to(docs, (tok, tok))
    doc_col = doc_row.T
    first_doc, last_doc = meta_ref[2:3, :], meta_ref[3:4, :]
    place_row = lax.broadcasted_iota(jnp.int32, (tok, tok), 0)
    place_col = lax.broadcasted_iota(jnp.int32, (tok, tok), 1)
    visible = (doc_col == doc_row) & (place_col <= place_row)
    first_mask = doc_col == first_doc
    last_mask = doc_col == last_doc
    before = jnp.where(place_row < place_col, 1.0, 0.0).astype(BF16)
    metas[rows_at(me, 8), :] = meta_ref[...]

    def copy_meta(to, slot):
        return pltpu.make_async_remote_copy(
            src_ref=meta_ref, dst_ref=metas.at[rows_at(slot, 8)],
            send_sem=meta_sems.at[0, to], recv_sem=meta_sems.at[1, slot],
            device_id={"seq": to}, device_id_type=MESH,
        )

    def copy_rows(src, dst, sems, group, to, slot):
        return pltpu.make_async_remote_copy(
            src_ref=src.at[rows_at(group * n + to, cap)],
            dst_ref=dst.at[rows_at(group * n + slot, cap)],
            send_sem=sems.at[0, group, to], recv_sem=sems.at[1, group, slot],
            device_id={"seq": to}, device_id_type=MESH,
        )

    def others(body):
        def step(index, _):
            body(lax.rem(me + index, n))
            return 0

        lax.fori_loop(1, n, step, 0)

    def loop(count, body):
        def step(index, _):
            body(index)
            return 0

        lax.fori_loop(0, count, step, 0)

    def at_sub(block, part):
        return rows_from(block * quarter + part * sub, sub)

    def copy_near(sems, scan, src, dst, part, to, slot):
        return pltpu.make_async_remote_copy(
            src_ref=src.at[at_sub(to, part)], dst_ref=dst.at[at_sub(slot, part)],
            send_sem=sems.at[0, scan, to * SUBS + part],
            recv_sem=sems.at[1, scan, slot * SUBS + part],
            device_id={"seq": plane * PLANE + to}, device_id_type=MESH,
        )

    peers = [lax.rem(spot + step, PLANE) for step in range(1, PLANE)]

    def send_near(sems, scan, src, dst, part):
        for peer in peers:
            copy_near(sems, scan, src, dst, part, peer, spot).start()
        dst[at_sub(spot, part), :] = src[at_sub(spot, part), :]

    def got_near(sems, scan, src, dst, part):
        for peer in peers:
            copy_near(sems, scan, src, dst, part, peer, peer).wait_recv()

    def sent_near(sems, scan, src, dst, part):
        for peer in peers:
            copy_near(sems, scan, src, dst, part, peer, spot).wait_send()

    def copy_far(scan, total, far, part, ahead):
        sign = 1 if scan == 0 else -1
        return pltpu.make_async_remote_copy(
            src_ref=total.at[at_sub(0, part)], dst_ref=far.at[at_sub(ahead - 1, part)],
            send_sem=far_sems.at[0, scan, (ahead - 1) * SUBS + part],
            recv_sem=far_sems.at[1, scan, (ahead - 1) * SUBS + part],
            device_id={"seq": me + sign * ahead * PLANE}, device_id_type=MESH,
        )

    def sends(scan, ahead):
        return plane + ahead < planes if scan == 0 else plane >= ahead

    def gets(scan, ahead):
        return plane >= ahead if scan == 0 else plane + ahead < planes

    def doc(block, which):
        return metas[pl.ds(block * 8 + which, 1), :]

    scans = [
        (fw_own, fw_in, fw_total, fw_far, fw_send, fw_carry, 3, 2, list(range(PLANE)), -1),
        (rv_own, rv_in, rv_total, rv_far, rv_send, rv_carry, 2, 3, list(range(PLANE))[::-1], 1),
    ]
    for scan in range(2):
        far = scans[scan][3]
        for ahead in (1, 2):
            @pl.when(jnp.logical_not(gets(scan, ahead)))
            def _():
                far[(ahead - 1) * quarter : ahead * quarter, :] = jnp.zeros((quarter, HS), BF16)

    def plane_total(scan, part):
        own, arrived, total_ref, far, _, _, leaving, _, order, toward = scans[scan]
        got_near(near_sems, scan, own, arrived, part)
        total = None
        for block in order:
            mine = arrived[at_sub(block, part), :].astype(F32)
            here = plane * PLANE + block
            if total is None:
                total = mine
            else:
                total = mine + total * same(doc(here, leaving), doc(here + toward, leaving))
        total_ref[at_sub(0, part), :] = total.astype(BF16)
        for ahead in (1, 2):
            @pl.when(sends(scan, ahead))
            def _():
                copy_far(scan, total_ref, far, part, ahead).start()

    def carries(scan, part):
        _, arrived, total_ref, far, send, carry, leaving, entering, order, toward = scans[scan]
        for ahead in (1, 2):
            @pl.when(gets(scan, ahead))
            def _():
                copy_far(scan, total_ref, far, part, ahead).wait_recv()

        def clamp(block):
            return jnp.clip(block, 0, n - 1)

        edge = plane * PLANE + order[0] + toward
        total = far[at_sub(0, part), :].astype(F32) + far[at_sub(1, part), :].astype(F32) * same(
            doc(clamp(edge), leaving), doc(clamp(edge + toward * PLANE), leaving)
        )
        for block in order:
            here = plane * PLANE + block
            prior = doc(clamp(here + toward), leaving)
            send[at_sub(block, part), :] = (total * same(doc(here, entering), prior)).astype(BF16)
            mine = arrived[at_sub(block, part), :].astype(F32)
            total = mine + total * same(doc(here, leaving), prior)
        send_near(carry_sems, scan, send, carry, part)

    def got_carry(scan, part):
        got_near(carry_sems, scan, scans[scan][4], scans[scan][5], part)

    def group_heads(part):
        return [(index, index * SUBS + part) for index in range(each)]

    def own_forward(part):
        for _, head in group_heads(part):
            at = rows_at(head, HS)
            kept = jnp.where(last_mask, k_ref[:, at].astype(F32), 0.0).astype(BF16)
            fw_own[at, :] = dot(kept, v_ref[:, at], 0, 0).astype(BF16)

    def inside(part):
        for _, head in group_heads(part):
            at = rows_at(head, HS)
            attn = jnp.where(visible, dot(q_ref[:, at], k_ref[:, at], 1, 1), 0.0).astype(BF16)
            attn_ref[at, :] = attn
            o_ref[:, at] = dot(attn, v_ref[:, at], 1, 0)

    loads[2].wait()
    loads[3].wait()
    own_forward(0)
    pl.semaphore_wait(barrier, (n - 1) + (nh - 1))
    if aligned:
        send_near(near_sems, 0, fw_own, fw_in, 0)

        def own_step(index):
            own_forward(index + 1)
            send_near(near_sems, 0, fw_own, fw_in, index + 1)

        loop(SUBS - 1, own_step)
    else:
        loop(SUBS - 1, lambda index: own_forward(index + 1))
        loop(SUBS, lambda part: send_near(near_sems, 0, fw_own, fw_in, part))
    others(lambda other: copy_meta(other, me).start())
    slots = lax.broadcasted_iota(jnp.int32, (cap, tok), 0).astype(F32)
    lanes = lax.broadcasted_iota(jnp.int32, (cap, tok), 1).astype(F32)

    def picks(owners, owner):
        chosen = jnp.broadcast_to(jnp.where(owners == owner, 1.0, 0.0), (cap, tok))
        rank = dot(chosen.astype(BF16), before, 1, 0)
        return jnp.where(rank == slots, chosen, 0.0)

    owner_row = meta_ref[0:1, :]
    owner_of = lax.broadcasted_iota(jnp.int32, (n, tok), 0).astype(F32)
    rank_ref[...] = dot(same(owner_row, owner_of).astype(BF16), before, 1, 0)

    def pack(owner):
        rank = rank_ref[pl.ds(owner, 1), :]
        chosen = same(owner_row, owner.astype(F32))
        pack_ref[rows_at(owner, cap), :] = (same(rank, slots) * chosen).astype(BF16)

    loads[4].wait()
    loop(SUBS // 2, inside)
    loop(n, pack)
    others(lambda other: copy_meta(other, other).wait_recv())
    loop(SUBS, lambda part: plane_total(0, part))
    loop(SUBS // 2, lambda part: inside(part + SUBS // 2))

    def unpack(source):
        chosen = picks(metas[pl.ds(source * 8, 1), :], me.astype(F32))
        row = jnp.sum(chosen * metas[pl.ds(source * 8 + 1, 1), :], axis=1, keepdims=True)
        used = jnp.sum(chosen, axis=1, keepdims=True)
        unpack_ref[rows_at(source, cap), :] = (
            jnp.where(row == lanes, 1.0, 0.0) * used
        ).astype(BF16)

    loop(SUBS, lambda part: carries(0, part))
    loads[5].wait()
    loads[6].wait()
    if not aligned:
        loop(SUBS, lambda part: got_carry(0, part))

    def output_step(part, sums):
        squares, inner = sums
        if aligned:
            got_carry(0, part)
        for _, head in group_heads(part):
            at = rows_at(head, HS)
            add = dot(q_ref[:, at], fw_carry[at, :], 1, 0)
            total = o_ref[:, at] + jnp.where(first_mask, add, 0.0)
            o_ref[:, at] = total
            scaled = gain_ref[:, at] * gn_ref[:, at].astype(F32)
            squares, inner = squares + total * total, inner + scaled * total
        return squares, inner

    zero = jnp.zeros((tok, HS), F32)
    squares, inner = lax.fori_loop(0, SUBS, output_step, (zero, zero))
    squares = jnp.sum(squares, axis=1, keepdims=True)
    inner = jnp.sum(inner, axis=1, keepdims=True)
    pair = jnp.where(place_col < HS // 2, squares, inner)
    sums_out[...] = pair

    def sum_copy(to, slot):
        return pltpu.make_async_remote_copy(
            src_ref=sums_out, dst_ref=sums_in.at[rows_at(slot, tok)],
            send_sem=sum_sems.at[0, to], recv_sem=sum_sems.at[1, slot],
            device_id={"head": to}, device_id_type=MESH,
        )

    def sum_start(step, _):
        sum_copy(lax.rem(me_head + step, nh), me_head).start()
        return 0

    def sum_finish(step, total):
        other = lax.rem(me_head + step, nh)
        sum_copy(other, other).wait_recv()
        return total + sums_in[rows_at(other, tok), :]

    def sum_sent(step, _):
        sum_copy(lax.rem(me_head + step, nh), me_head).wait_send()
        return 0

    lax.fori_loop(1, nh, sum_start, 0)
    pair = lax.fori_loop(1, nh, sum_finish, pair)
    full = HEADS * HS
    inv_rms = lax.rsqrt(pair[:, 0:1] / full + EPSILON)
    pull = inv_rms * inv_rms * inv_rms * pair[:, HS - 1 : HS] / full
    inv_rms = jnp.broadcast_to(inv_rms, (tok, HS))
    pull = jnp.broadcast_to(pull, (tok, HS))

    def own_reverse(part):
        for _, head in group_heads(part):
            at = rows_at(head, HS)
            scaled = gain_ref[:, at] * gn_ref[:, at].astype(F32)
            grad = (inv_rms * scaled - o_ref[:, at] * pull).astype(BF16)
            go_ref[:, at] = grad
            kept = jnp.where(first_mask, q_ref[:, at].astype(F32), 0.0).astype(BF16)
            rv_own[at, :] = dot(kept, grad, 0, 0).astype(BF16)
        if aligned:
            send_near(near_sems, 1, rv_own, rv_in, part)

    loop(SUBS, own_reverse)
    if not aligned:
        loop(SUBS, lambda part: send_near(near_sems, 1, rv_own, rv_in, part))

    half = SUBS // 2
    slots_all = n * cap

    def grad_query(group, part):
        made = []
        for index, head in group_heads(group * half + part):
            at = rows_at(head, HS)
            grad = go_ref[:, at]
            back = jnp.where(visible, dot(grad, v_ref[:, at], 1, 1), 0.0).astype(BF16)
            back_ref[at, :] = back
            add = dot(grad, fw_carry[at, :], 1, 1)
            result = dot(back, k_ref[:, at], 1, 0) + jnp.where(first_mask, add, 0.0)
            made.append(result.astype(BF16))
        bq_send[group * slots_all : (group + 1) * slots_all, rows_at(part, each * HS)] = dot(
            pack_ref[...], jnp.concatenate(made, axis=1), 1, 0
        ).astype(BF16)

    def send_query(group):
        others(lambda other: copy_rows(bq_send, bq_in, q_sems, group, other, me).start())
        bq_in[rows_at(group * n + me, cap), :] = bq_send[rows_at(group * n + me, cap), :]

    loop(half, lambda part: grad_query(0, part))
    loop(SUBS, lambda part: plane_total(1, part))
    send_query(0)
    loop(half, lambda part: grad_query(1, part))
    send_query(1)

    def inside_back(part):
        for _, head in group_heads(part):
            at = rows_at(head, HS)
            gk_ref[:, at] = dot(back_ref[at, :], q_ref[:, at], 0, 0)
            gv_ref[:, at] = dot(attn_ref[at, :], go_ref[:, at], 0, 0)

    loop(SUBS, lambda part: carries(1, part))
    loop(SUBS, inside_back)
    if not aligned:
        loop(SUBS, lambda part: got_carry(1, part))

    def grad_pair(part):
        if aligned:
            got_carry(1, part)
        made = [[], []]
        for index, head in group_heads(part):
            at = rows_at(head, HS)
            carry = rv_carry[at, :]
            key = gk_ref[:, at] + jnp.where(last_mask, dot(v_ref[:, at], carry, 1, 1), 0.0)
            value = gv_ref[:, at] + jnp.where(last_mask, dot(k_ref[:, at], carry, 1, 0), 0.0)
            made[0].append(key.astype(BF16))
            made[1].append(value.astype(BF16))
        bkv_send[rows_at(part, slots_all), :] = dot(
            pack_ref[...], jnp.concatenate(made[0] + made[1], axis=1), 1, 0
        ).astype(BF16)
        others(lambda other: copy_rows(bkv_send, bkv_in, kv_sems, part, other, me).start())
        bkv_in[rows_at(part * n + me, cap), :] = bkv_send[rows_at(part * n + me, cap), :]

    loop(SUBS, grad_pair)

    loop(n, unpack)
    place_ref[...] = unpack_ref[...].T

    def place_query(group, part):
        arrived = bq_in[group * slots_all : (group + 1) * slots_all, rows_at(part, each * HS)]
        placed = dot(place_ref[...], arrived, 1, 0).astype(BF16)
        for index, head in group_heads(group * half + part):
            out_ref[0, :, rows_at(head, HS)] = placed[:, index * HS : (index + 1) * HS]

    for group in range(2):
        others(lambda other: copy_rows(bq_send, bq_in, q_sems, group, other, other).wait_recv())
        loop(half, lambda part: place_query(group, part))

    def place_pair(part):
        others(lambda other: copy_rows(bkv_send, bkv_in, kv_sems, part, other, other).wait_recv())
        placed = dot(place_ref[...], bkv_in[rows_at(part, slots_all), :], 1, 0).astype(BF16)
        for index, head in group_heads(part):
            for which in range(2):
                column = (which * each + index) * HS
                out_ref[which + 1, :, rows_at(head, HS)] = placed[:, column : column + HS]

    loop(SUBS, place_pair)

    others(lambda other: copy_meta(other, me).wait_send())
    lax.fori_loop(1, nh, sum_sent, 0)
    for scan in range(2):
        own, arrived, total_ref, far, send, carry = scans[scan][:6]

        def drain(part):
            sent_near(near_sems, scan, own, arrived, part)
            sent_near(carry_sems, scan, send, carry, part)
            for ahead in (1, 2):
                @pl.when(sends(scan, ahead))
                def _():
                    copy_far(scan, total_ref, far, part, ahead).wait_send()

        loop(SUBS, drain)
    for group in range(2):
        others(lambda other: copy_rows(bq_send, bq_in, q_sems, group, other, me).wait_send())
    loop(
        SUBS,
        lambda part: others(
            lambda other: copy_rows(bkv_send, bkv_in, kv_sems, part, other, me).wait_send()
        ),
    )


def local(n, nh, query, keys, values, grad_normed, norm_gain, doc_ids, home):
    tok, width = query.shape
    heads = width // HS
    cap = max(16, 2 * tok // n)
    states = pltpu.VMEM((heads * HS, HS), BF16)
    total = pltpu.VMEM((heads * HS // PLANE, HS), BF16)
    far = pltpu.VMEM((2 * heads * HS // PLANE, HS), BF16)
    scan = [states, states, total, far, states, states]
    block = pltpu.VMEM((tok, width), BF16)
    wide = pltpu.VMEM((tok, width), F32)
    map_rows = pltpu.VMEM((n * cap, tok), BF16)
    query_rows = pltpu.VMEM((2 * n * cap, width // 2), BF16)
    pair_rows = pltpu.VMEM((SUBS * n * cap, 2 * width // SUBS), BF16)
    dma = pltpu.SemaphoreType.DMA
    result = pl.pallas_call(
        functools.partial(kernel, n, nh, cap),
        out_shape=jax.ShapeDtypeStruct((3, tok, width), BF16),
        in_specs=[pl.BlockSpec(memory_space=pltpu.HBM)] * 7,
        out_specs=pl.BlockSpec(memory_space=pltpu.VMEM),
        scratch_shapes=[
            block, block, block, block,
            pltpu.VMEM((1, width), F32),
            pltpu.VMEM((1, tok), jnp.int32),
            pltpu.VMEM((1, tok), jnp.int32),
            pltpu.VMEM((8, tok), F32),
            pltpu.VMEM((n * 8, tok), F32),
            *scan, *scan,
            states, states,
            wide, block, wide, wide,
            pltpu.VMEM((tok, HS), F32),
            pltpu.VMEM((nh * tok, HS), F32),
            pltpu.VMEM((n, tok), F32),
            map_rows, map_rows,
            pltpu.VMEM((tok, n * cap), BF16),
            query_rows, query_rows, pair_rows, pair_rows,
            dma((7,)),
            dma((2, n)),
            dma((2, 2, PLANE * SUBS)),
            dma((2, 2, 2 * SUBS)),
            dma((2, 2, PLANE * SUBS)),
            dma((2, 2, n)),
            dma((2, SUBS, n)),
            dma((2, nh)),
        ],
        compiler_params=pltpu.CompilerParams(
            collective_id=0, has_side_effects=True, vmem_limit_bytes=56 * 1024 * 1024
        ),
    )(query, keys, values, grad_normed, norm_gain[None, :], doc_ids[None, :], home[None, :])
    return jnp.transpose(result, (1, 0, 2))


def solution(mesh):
    placed = (
        P("seq", "head"),
        P("seq", "head"),
        P("seq", "head"),
        P("seq", "head"),
        P("head"),
        P("seq"),
        P("seq"),
    )
    return jax.shard_map(
        functools.partial(local, mesh.shape["seq"], mesh.shape["head"]),
        mesh=mesh, in_specs=placed, out_specs=P("seq", None, "head"), check_vma=False,
    )
```

```python
import functools

import jax
import jax.numpy as jnp
from jax import lax
from jax.experimental import pallas as pl
from jax.experimental.pallas import tpu as pltpu
from jax.sharding import PartitionSpec as P

HEADS = 32
HS = 128
EPSILON = 1e-05
PLANE = 4
SUBS = 4
STRIDE = 7
F32 = jnp.float32
BF16 = jnp.bfloat16


def dot(left, right, left_dim, right_dim):
    return lax.dot_general(
        left, right, (((left_dim,), (right_dim,)), ((), ())), preferred_element_type=F32
    )


def rows_at(index, size):
    return pl.ds(pl.multiple_of(index * size, size), size)


MESH = pl.DeviceIdType.MESH


def rows_from(offset, size):
    return pl.ds(pl.multiple_of(offset, size), size)


def same(left, right):
    return jnp.where(left == right, 1.0, 0.0)


def kernel(
    n, nh, cap,
    q_hbm, k_hbm, v_hbm, gn_hbm, gain_hbm, doc_hbm, home_hbm,
    out_ref,
    q_ref, k_ref, v_ref, gn_ref, gain_ref, doc_ref, home_ref,
    meta_ref, metas,
    fw_own, fw_in, fw_total, fw_far, fw_send, fw_carry,
    rv_own, rv_in, rv_total, rv_far, rv_send, rv_carry,
    attn_ref, back_ref, o_ref, go_ref, gk_ref, gv_ref, sums_out, sums_in,
    rank_ref, pack_ref, unpack_ref, place_ref, bq_send, bq_in, bkv_send, bkv_in,
    in_sem, meta_sems, near_sems, far_sems, carry_sems, q_sems, kv_sems, sum_sems,
):
    tok, width = q_ref.shape
    heads = width // HS
    quarter = heads * HS // PLANE
    sub = quarter // SUBS
    aligned = sub == HS
    each = heads // SUBS
    planes = n // PLANE
    me = lax.axis_index("seq")
    me_head = lax.axis_index("head")
    plane, spot = me // PLANE, lax.rem(me, PLANE)

    loads = [
        pltpu.make_async_copy(src, dst, in_sem.at[index])
        for index, (src, dst) in enumerate(
            [
                (doc_hbm, doc_ref), (home_hbm, home_ref), (k_hbm, k_ref), (v_hbm, v_ref),
                (q_hbm, q_ref), (gn_hbm, gn_ref), (gain_hbm, gain_ref),
            ]
        )
    ]
    for load in loads:
        load.start()

    barrier = pltpu.get_barrier_semaphore()

    def greet(step, _):
        pl.semaphore_signal(
            barrier, inc=1, device_id={"seq": lax.rem(me + step, n)}, device_id_type=MESH
        )
        return 0

    def greet_head(step, _):
        pl.semaphore_signal(
            barrier, inc=1, device_id={"head": lax.rem(me_head + step, nh)}, device_id_type=MESH
        )
        return 0

    lax.fori_loop(1, n, greet, 0)
    lax.fori_loop(1, nh, greet_head, 0)

    loads[0].wait()
    loads[1].wait()
    homes = home_ref[...]
    owners = lax.div(homes, jnp.full_like(homes, tok))
    docs = doc_ref[...].astype(F32)
    meta_ref[0:1, :] = owners.astype(F32)
    meta_ref[1:2, :] = (homes - owners * tok).astype(F32)
    meta_ref[2:3, :] = jnp.broadcast_to(docs[:, 0:1], (1, tok))
    meta_ref[3:4, :] = jnp.broadcast_to(docs[:, tok - 1 : tok], (1, tok))
    meta_ref[4:5, :] = docs
    meta_ref[5:8, :] = jnp.zeros((3, tok), F32)

    doc_row = jnp.broadcast_to(docs, (tok, tok))
    doc_col = doc_row.T
    first_doc, last_doc = meta_ref[2:3, :], meta_ref[3:4, :]
    place_row = lax.broadcasted_iota(jnp.int32, (tok, tok), 0)
    place_col = lax.broadcasted_iota(jnp.int32, (tok, tok), 1)
    visible = (doc_col == doc_row) & (place_col <= place_row)
    first_mask = doc_col == first_doc
    last_mask = doc_col == last_doc
    before = jnp.where(place_row < place_col, 1.0, 0.0).astype(BF16)
    metas[rows_at(me, 8), :] = meta_ref[...]

    def copy_meta(to, slot):
        return pltpu.make_async_remote_copy(
            src_ref=meta_ref, dst_ref=metas.at[rows_at(slot, 8)],
            send_sem=meta_sems.at[0, to], recv_sem=meta_sems.at[1, slot],
            device_id={"seq": to}, device_id_type=MESH,
        )

    def copy_rows(src, dst, sems, group, to, slot):
        return pltpu.make_async_remote_copy(
            src_ref=src.at[rows_at(group * n + to, cap)],
            dst_ref=dst.at[rows_at(group * n + slot, cap)],
            send_sem=sems.at[0, group, to], recv_sem=sems.at[1, group, slot],
            device_id={"seq": to}, device_id_type=MESH,
        )

    def others(body):
        def step(index, _):
            body(lax.rem(me + STRIDE * index, n))
            return 0

        lax.fori_loop(1, n, step, 0)

    def loop(count, body):
        def step(index, _):
            body(index)
            return 0

        lax.fori_loop(0, count, step, 0)

    def at_sub(block, part):
        return rows_from(block * quarter + part * sub, sub)

    def copy_near(sems, scan, src, dst, part, to, slot):
        return pltpu.make_async_remote_copy(
            src_ref=src.at[at_sub(to, part)], dst_ref=dst.at[at_sub(slot, part)],
            send_sem=sems.at[0, scan, to * SUBS + part],
            recv_sem=sems.at[1, scan, slot * SUBS + part],
            device_id={"seq": plane * PLANE + to}, device_id_type=MESH,
        )

    peers = [lax.rem(spot + step, PLANE) for step in range(1, PLANE)]

    def send_near(sems, scan, src, dst, part):
        for peer in peers:
            copy_near(sems, scan, src, dst, part, peer, spot).start()
        dst[at_sub(spot, part), :] = src[at_sub(spot, part), :]

    def got_near(sems, scan, src, dst, part):
        for peer in peers:
            copy_near(sems, scan, src, dst, part, peer, peer).wait_recv()

    def sent_near(sems, scan, src, dst, part):
        for peer in peers:
            copy_near(sems, scan, src, dst, part, peer, spot).wait_send()

    def copy_far(scan, total, far, part, ahead):
        sign = 1 if scan == 0 else -1
        return pltpu.make_async_remote_copy(
            src_ref=total.at[at_sub(0, part)], dst_ref=far.at[at_sub(ahead - 1, part)],
            send_sem=far_sems.at[0, scan, (ahead - 1) * SUBS + part],
            recv_sem=far_sems.at[1, scan, (ahead - 1) * SUBS + part],
            device_id={"seq": me + sign * ahead * PLANE}, device_id_type=MESH,
        )

    def sends(scan, ahead):
        return plane + ahead < planes if scan == 0 else plane >= ahead

    def gets(scan, ahead):
        return plane >= ahead if scan == 0 else plane + ahead < planes

    def doc(block, which):
        return metas[pl.ds(block * 8 + which, 1), :]

    scans = [
        (fw_own, fw_in, fw_total, fw_far, fw_send, fw_carry, 3, 2, list(range(PLANE)), -1),
        (rv_own, rv_in, rv_total, rv_far, rv_send, rv_carry, 2, 3, list(range(PLANE))[::-1], 1),
    ]
    for scan in range(2):
        far = scans[scan][3]
        for ahead in (1, 2):
            @pl.when(jnp.logical_not(gets(scan, ahead)))
            def _():
                far[(ahead - 1) * quarter : ahead * quarter, :] = jnp.zeros((quarter, HS), BF16)

    def chain(scan, part):
        own, arrived, total_ref, far, send, carry, leaving, entering, order, toward = scans[scan]
        got_near(near_sems, scan, own, arrived, part)

        @pl.when(gets(scan, 1))
        def _():
            copy_far(scan, total_ref, far, part, 1).wait_recv()

        total = far[at_sub(0, part), :].astype(F32)
        for block in order:
            here = plane * PLANE + block
            prior = doc(jnp.clip(here + toward, 0, n - 1), leaving)
            send[at_sub(block, part), :] = (total * same(doc(here, entering), prior)).astype(BF16)
            mine = arrived[at_sub(block, part), :].astype(F32)
            total = mine + total * same(doc(here, leaving), prior)
        total_ref[at_sub(0, part), :] = total.astype(BF16)

        @pl.when(sends(scan, 1))
        def _():
            copy_far(scan, total_ref, far, part, 1).start()

        send_near(carry_sems, scan, send, carry, part)

    def plane_total(scan, part):
        own, arrived, total_ref, far, _, _, leaving, _, order, toward = scans[scan]
        got_near(near_sems, scan, own, arrived, part)
        total = None
        for block in order:
            mine = arrived[at_sub(block, part), :].astype(F32)
            here = plane * PLANE + block
            if total is None:
                total = mine
            else:
                total = mine + total * same(doc(here, leaving), doc(here + toward, leaving))
        total_ref[at_sub(0, part), :] = total.astype(BF16)
        for ahead in (1, 2):
            @pl.when(sends(scan, ahead))
            def _():
                copy_far(scan, total_ref, far, part, ahead).start()

    def carries(scan, part):
        _, arrived, total_ref, far, send, carry, leaving, entering, order, toward = scans[scan]
        for ahead in (1, 2):
            @pl.when(gets(scan, ahead))
            def _():
                copy_far(scan, total_ref, far, part, ahead).wait_recv()

        def clamp(block):
            return jnp.clip(block, 0, n - 1)

        edge = plane * PLANE + order[0] + toward
        total = far[at_sub(0, part), :].astype(F32) + far[at_sub(1, part), :].astype(F32) * same(
            doc(clamp(edge), leaving), doc(clamp(edge + toward * PLANE), leaving)
        )
        for block in order:
            here = plane * PLANE + block
            prior = doc(clamp(here + toward), leaving)
            send[at_sub(block, part), :] = (total * same(doc(here, entering), prior)).astype(BF16)
            mine = arrived[at_sub(block, part), :].astype(F32)
            total = mine + total * same(doc(here, leaving), prior)
        send_near(carry_sems, scan, send, carry, part)

    def got_carry(scan, part):
        got_near(carry_sems, scan, scans[scan][4], scans[scan][5], part)

    def group_heads(part):
        return [(index, index * SUBS + part) for index in range(each)]

    def own_forward(part):
        for _, head in group_heads(part):
            at = rows_at(head, HS)
            kept = jnp.where(last_mask, k_ref[:, at].astype(F32), 0.0).astype(BF16)
            fw_own[at, :] = dot(kept, v_ref[:, at], 0, 0).astype(BF16)

    def inside(part):
        for _, head in group_heads(part):
            at = rows_at(head, HS)
            attn = jnp.where(visible, dot(q_ref[:, at], k_ref[:, at], 1, 1), 0.0).astype(BF16)
            attn_ref[at, :] = attn
            o_ref[:, at] = dot(attn, v_ref[:, at], 1, 0)

    loads[2].wait()
    loads[3].wait()
    own_forward(0)
    pl.semaphore_wait(barrier, (n - 1) + (nh - 1))
    if aligned:
        send_near(near_sems, 0, fw_own, fw_in, 0)

        def own_step(index):
            own_forward(index + 1)
            send_near(near_sems, 0, fw_own, fw_in, index + 1)

        loop(SUBS - 1, own_step)
    else:
        loop(SUBS - 1, lambda index: own_forward(index + 1))
        loop(SUBS, lambda part: send_near(near_sems, 0, fw_own, fw_in, part))
    others(lambda other: copy_meta(other, me).start())
    slots = lax.broadcasted_iota(jnp.int32, (cap, tok), 0).astype(F32)
    lanes = lax.broadcasted_iota(jnp.int32, (cap, tok), 1).astype(F32)

    def picks(owners, owner):
        chosen = jnp.broadcast_to(jnp.where(owners == owner, 1.0, 0.0), (cap, tok))
        rank = dot(chosen.astype(BF16), before, 1, 0)
        return jnp.where(rank == slots, chosen, 0.0)

    owner_row = meta_ref[0:1, :]
    owner_of = lax.broadcasted_iota(jnp.int32, (n, tok), 0).astype(F32)
    rank_ref[...] = dot(same(owner_row, owner_of).astype(BF16), before, 1, 0)

    def pack(owner):
        rank = rank_ref[pl.ds(owner, 1), :]
        chosen = same(owner_row, owner.astype(F32))
        pack_ref[rows_at(owner, cap), :] = (same(rank, slots) * chosen).astype(BF16)

    loads[4].wait()
    loop(SUBS // 2, inside)
    loop(n, pack)
    others(lambda other: copy_meta(other, other).wait_recv())
    loop(SUBS, lambda part: chain(0, part))
    loop(SUBS // 2, lambda part: inside(part + SUBS // 2))

    def unpack(source):
        chosen = picks(metas[pl.ds(source * 8, 1), :], me.astype(F32))
        row = jnp.sum(chosen * metas[pl.ds(source * 8 + 1, 1), :], axis=1, keepdims=True)
        used = jnp.sum(chosen, axis=1, keepdims=True)
        unpack_ref[rows_at(source, cap), :] = (
            jnp.where(row == lanes, 1.0, 0.0) * used
        ).astype(BF16)

    loads[5].wait()
    loads[6].wait()
    if not aligned:
        loop(SUBS, lambda part: got_carry(0, part))

    def output_step(part, sums):
        squares, inner = sums
        if aligned:
            got_carry(0, part)
        for _, head in group_heads(part):
            at = rows_at(head, HS)
            add = dot(q_ref[:, at], fw_carry[at, :], 1, 0)
            total = o_ref[:, at] + jnp.where(first_mask, add, 0.0)
            o_ref[:, at] = total
            scaled = gain_ref[:, at] * gn_ref[:, at].astype(F32)
            squares, inner = squares + total * total, inner + scaled * total
        return squares, inner

    zero = jnp.zeros((tok, HS), F32)
    squares, inner = lax.fori_loop(0, SUBS, output_step, (zero, zero))
    squares = jnp.sum(squares, axis=1, keepdims=True)
    inner = jnp.sum(inner, axis=1, keepdims=True)
    pair = jnp.where(place_col < HS // 2, squares, inner)
    sums_out[...] = pair

    def sum_copy(to, slot):
        return pltpu.make_async_remote_copy(
            src_ref=sums_out, dst_ref=sums_in.at[rows_at(slot, tok)],
            send_sem=sum_sems.at[0, to], recv_sem=sum_sems.at[1, slot],
            device_id={"head": to}, device_id_type=MESH,
        )

    def sum_start(step, _):
        sum_copy(lax.rem(me_head + step, nh), me_head).start()
        return 0

    def sum_finish(step, total):
        other = lax.rem(me_head + step, nh)
        sum_copy(other, other).wait_recv()
        return total + sums_in[rows_at(other, tok), :]

    def sum_sent(step, _):
        sum_copy(lax.rem(me_head + step, nh), me_head).wait_send()
        return 0

    lax.fori_loop(1, nh, sum_start, 0)
    pair = lax.fori_loop(1, nh, sum_finish, pair)
    full = HEADS * HS
    inv_rms = lax.rsqrt(pair[:, 0:1] / full + EPSILON)
    pull = inv_rms * inv_rms * inv_rms * pair[:, HS - 1 : HS] / full
    inv_rms = jnp.broadcast_to(inv_rms, (tok, HS))
    pull = jnp.broadcast_to(pull, (tok, HS))

    def own_reverse(part):
        for _, head in group_heads(part):
            at = rows_at(head, HS)
            scaled = gain_ref[:, at] * gn_ref[:, at].astype(F32)
            grad = (inv_rms * scaled - o_ref[:, at] * pull).astype(BF16)
            go_ref[:, at] = grad
            kept = jnp.where(first_mask, q_ref[:, at].astype(F32), 0.0).astype(BF16)
            rv_own[at, :] = dot(kept, grad, 0, 0).astype(BF16)
        if aligned:
            send_near(near_sems, 1, rv_own, rv_in, part)

    loop(SUBS, own_reverse)
    if not aligned:
        loop(SUBS, lambda part: send_near(near_sems, 1, rv_own, rv_in, part))

    half = SUBS // 2
    slots_all = n * cap

    def grad_query(group, part):
        made = []
        for index, head in group_heads(group * half + part):
            at = rows_at(head, HS)
            grad = go_ref[:, at]
            back = jnp.where(visible, dot(grad, v_ref[:, at], 1, 1), 0.0).astype(BF16)
            back_ref[at, :] = back
            add = dot(grad, fw_carry[at, :], 1, 1)
            result = dot(back, k_ref[:, at], 1, 0) + jnp.where(first_mask, add, 0.0)
            made.append(result.astype(BF16))
        bq_send[group * slots_all : (group + 1) * slots_all, rows_at(part, each * HS)] = dot(
            pack_ref[...], jnp.concatenate(made, axis=1), 1, 0
        ).astype(BF16)

    def send_query(group):
        others(lambda other: copy_rows(bq_send, bq_in, q_sems, group, other, me).start())
        bq_in[rows_at(group * n + me, cap), :] = bq_send[rows_at(group * n + me, cap), :]

    loop(half, lambda part: grad_query(0, part))
    loop(SUBS, lambda part: plane_total(1, part))
    send_query(0)
    loop(half, lambda part: grad_query(1, part))
    send_query(1)

    def inside_back(part):
        for _, head in group_heads(part):
            at = rows_at(head, HS)
            gk_ref[:, at] = dot(back_ref[at, :], q_ref[:, at], 0, 0)
            gv_ref[:, at] = dot(attn_ref[at, :], go_ref[:, at], 0, 0)

    loop(SUBS, lambda part: carries(1, part))
    loop(SUBS, inside_back)
    if not aligned:
        loop(SUBS, lambda part: got_carry(1, part))

    def grad_pair(part):
        if aligned:
            got_carry(1, part)
        made = [[], []]
        for index, head in group_heads(part):
            at = rows_at(head, HS)
            carry = rv_carry[at, :]
            key = gk_ref[:, at] + jnp.where(last_mask, dot(v_ref[:, at], carry, 1, 1), 0.0)
            value = gv_ref[:, at] + jnp.where(last_mask, dot(k_ref[:, at], carry, 1, 0), 0.0)
            made[0].append(key.astype(BF16))
            made[1].append(value.astype(BF16))
        bkv_send[rows_at(part, slots_all), :] = dot(
            pack_ref[...], jnp.concatenate(made[0] + made[1], axis=1), 1, 0
        ).astype(BF16)
        others(lambda other: copy_rows(bkv_send, bkv_in, kv_sems, part, other, me).start())
        bkv_in[rows_at(part * n + me, cap), :] = bkv_send[rows_at(part * n + me, cap), :]

    loop(SUBS, grad_pair)

    loop(n, unpack)
    place_ref[...] = unpack_ref[...].T

    def place_query(group, part):
        arrived = bq_in[group * slots_all : (group + 1) * slots_all, rows_at(part, each * HS)]
        placed = dot(place_ref[...], arrived, 1, 0).astype(BF16)
        for index, head in group_heads(group * half + part):
            out_ref[0, :, rows_at(head, HS)] = placed[:, index * HS : (index + 1) * HS]

    for group in range(2):
        others(lambda other: copy_rows(bq_send, bq_in, q_sems, group, other, other).wait_recv())
        loop(half, lambda part: place_query(group, part))

    def place_pair(part):
        others(lambda other: copy_rows(bkv_send, bkv_in, kv_sems, part, other, other).wait_recv())
        placed = dot(place_ref[...], bkv_in[rows_at(part, slots_all), :], 1, 0).astype(BF16)
        for index, head in group_heads(part):
            for which in range(2):
                column = (which * each + index) * HS
                out_ref[which + 1, :, rows_at(head, HS)] = placed[:, column : column + HS]

    loop(SUBS, place_pair)

    others(lambda other: copy_meta(other, me).wait_send())
    lax.fori_loop(1, nh, sum_sent, 0)
    for scan in range(2):
        own, arrived, total_ref, far, send, carry = scans[scan][:6]

        def drain(part):
            sent_near(near_sems, scan, own, arrived, part)
            sent_near(carry_sems, scan, send, carry, part)
            for ahead in (1, 2)[: scan + 1]:
                @pl.when(sends(scan, ahead))
                def _():
                    copy_far(scan, total_ref, far, part, ahead).wait_send()

        loop(SUBS, drain)
    for group in range(2):
        others(lambda other: copy_rows(bq_send, bq_in, q_sems, group, other, me).wait_send())
    loop(
        SUBS,
        lambda part: others(
            lambda other: copy_rows(bkv_send, bkv_in, kv_sems, part, other, me).wait_send()
        ),
    )


def local(n, nh, query, keys, values, grad_normed, norm_gain, doc_ids, home):
    tok, width = query.shape
    heads = width // HS
    cap = max(16, 2 * tok // n)
    states = pltpu.VMEM((heads * HS, HS), BF16)
    total = pltpu.VMEM((heads * HS // PLANE, HS), BF16)
    far = pltpu.VMEM((2 * heads * HS // PLANE, HS), BF16)
    scan = [states, states, total, far, states, states]
    block = pltpu.VMEM((tok, width), BF16)
    wide = pltpu.VMEM((tok, width), F32)
    map_rows = pltpu.VMEM((n * cap, tok), BF16)
    query_rows = pltpu.VMEM((2 * n * cap, width // 2), BF16)
    pair_rows = pltpu.VMEM((SUBS * n * cap, 2 * width // SUBS), BF16)
    dma = pltpu.SemaphoreType.DMA
    result = pl.pallas_call(
        functools.partial(kernel, n, nh, cap),
        out_shape=jax.ShapeDtypeStruct((3, tok, width), BF16),
        in_specs=[pl.BlockSpec(memory_space=pltpu.HBM)] * 7,
        out_specs=pl.BlockSpec(memory_space=pltpu.VMEM),
        scratch_shapes=[
            block, block, block, block,
            pltpu.VMEM((1, width), F32),
            pltpu.VMEM((1, tok), jnp.int32),
            pltpu.VMEM((1, tok), jnp.int32),
            pltpu.VMEM((8, tok), F32),
            pltpu.VMEM((n * 8, tok), F32),
            *scan, *scan,
            states, states,
            wide, block, wide, wide,
            pltpu.VMEM((tok, HS), F32),
            pltpu.VMEM((nh * tok, HS), F32),
            pltpu.VMEM((n, tok), F32),
            map_rows, map_rows,
            pltpu.VMEM((tok, n * cap), BF16),
            query_rows, query_rows, pair_rows, pair_rows,
            dma((7,)),
            dma((2, n)),
            dma((2, 2, PLANE * SUBS)),
            dma((2, 2, 2 * SUBS)),
            dma((2, 2, PLANE * SUBS)),
            dma((2, 2, n)),
            dma((2, SUBS, n)),
            dma((2, nh)),
        ],
        compiler_params=pltpu.CompilerParams(
            collective_id=0, has_side_effects=True, vmem_limit_bytes=56 * 1024 * 1024
        ),
    )(query, keys, values, grad_normed, norm_gain[None, :], doc_ids[None, :], home[None, :])
    return jnp.transpose(result, (1, 0, 2))


def solution(mesh):
    placed = (
        P("seq", "head"),
        P("seq", "head"),
        P("seq", "head"),
        P("seq", "head"),
        P("head"),
        P("seq"),
        P("seq"),
    )
    return jax.shard_map(
        functools.partial(local, mesh.shape["seq"], mesh.shape["head"]),
        mesh=mesh, in_specs=placed, out_specs=P("seq", None, "head"), check_vma=False,
    )
```

```python
import functools

import jax
import jax.numpy as jnp
from jax import lax
from jax.experimental import pallas as pl
from jax.experimental.pallas import tpu as pltpu
from jax.sharding import PartitionSpec as P

HEADS = 32
HS = 128
EPSILON = 1e-05
PLANE = 4
SUBS = 4
F32 = jnp.float32
BF16 = jnp.bfloat16


def dot(left, right, left_dim, right_dim):
    return lax.dot_general(
        left, right, (((left_dim,), (right_dim,)), ((), ())), preferred_element_type=F32
    )


def rows_at(index, size):
    return pl.ds(pl.multiple_of(index * size, size), size)


MESH = pl.DeviceIdType.MESH


def rows_from(offset, size):
    return pl.ds(pl.multiple_of(offset, size), size)


def same(left, right):
    return jnp.where(left == right, 1.0, 0.0)


def kernel(
    n, nh, cap,
    q_hbm, k_hbm, v_hbm, gn_hbm, gain_hbm, doc_hbm, home_hbm,
    out_ref,
    q_ref, k_ref, v_ref, gn_ref, gain_ref, doc_ref, home_ref,
    meta_ref, metas,
    fw_own, fw_in, fw_total, fw_far, fw_send, fw_carry,
    rv_own, rv_in, rv_total, rv_far, rv_send, rv_carry,
    attn_ref, back_ref, o_ref, go_ref, gk_ref, gv_ref, sums_out, sums_in,
    rank_ref, pack_ref, unpack_ref, place_ref, bq_send, bq_in, bkv_send, bkv_in,
    in_sem, meta_sems, near_sems, far_sems, carry_sems, q_sems, kv_sems, sum_sems,
):
    tok, width = q_ref.shape
    heads = width // HS
    quarter = heads * HS // PLANE
    sub = quarter // SUBS
    aligned = sub == HS
    each = heads // SUBS
    planes = n // PLANE
    me = lax.axis_index("seq")
    me_head = lax.axis_index("head")
    plane, spot = me // PLANE, lax.rem(me, PLANE)

    loads = [
        pltpu.make_async_copy(src, dst, in_sem.at[index])
        for index, (src, dst) in enumerate(
            [
                (doc_hbm, doc_ref), (home_hbm, home_ref), (k_hbm, k_ref), (v_hbm, v_ref),
                (q_hbm, q_ref), (gn_hbm, gn_ref), (gain_hbm, gain_ref),
            ]
        )
    ]
    for load in loads:
        load.start()

    barrier = pltpu.get_barrier_semaphore()

    def greet(step, _):
        pl.semaphore_signal(
            barrier, inc=1, device_id={"seq": lax.rem(me + step, n)}, device_id_type=MESH
        )
        return 0

    def greet_head(step, _):
        pl.semaphore_signal(
            barrier, inc=1, device_id={"head": lax.rem(me_head + step, nh)}, device_id_type=MESH
        )
        return 0

    lax.fori_loop(1, n, greet, 0)
    lax.fori_loop(1, nh, greet_head, 0)

    loads[0].wait()
    loads[1].wait()
    homes = home_ref[...]
    owners = lax.div(homes, jnp.full_like(homes, tok))
    docs = doc_ref[...].astype(F32)
    meta_ref[0:1, :] = owners.astype(F32)
    meta_ref[1:2, :] = (homes - owners * tok).astype(F32)
    meta_ref[2:3, :] = jnp.broadcast_to(docs[:, 0:1], (1, tok))
    meta_ref[3:4, :] = jnp.broadcast_to(docs[:, tok - 1 : tok], (1, tok))
    meta_ref[4:5, :] = docs
    meta_ref[5:8, :] = jnp.zeros((3, tok), F32)

    doc_row = jnp.broadcast_to(docs, (tok, tok))
    doc_col = doc_row.T
    first_doc, last_doc = meta_ref[2:3, :], meta_ref[3:4, :]
    place_row = lax.broadcasted_iota(jnp.int32, (tok, tok), 0)
    place_col = lax.broadcasted_iota(jnp.int32, (tok, tok), 1)
    visible = (doc_col == doc_row) & (place_col <= place_row)
    first_mask = doc_col == first_doc
    last_mask = doc_col == last_doc
    before = jnp.where(place_row < place_col, 1.0, 0.0).astype(BF16)
    metas[rows_at(me, 8), :] = meta_ref[...]

    def copy_meta(to, slot):
        return pltpu.make_async_remote_copy(
            src_ref=meta_ref, dst_ref=metas.at[rows_at(slot, 8)],
            send_sem=meta_sems.at[0, to], recv_sem=meta_sems.at[1, slot],
            device_id={"seq": to}, device_id_type=MESH,
        )

    def copy_rows(src, dst, sems, group, to, slot):
        return pltpu.make_async_remote_copy(
            src_ref=src.at[rows_at(group * n + to, cap)],
            dst_ref=dst.at[rows_at(group * n + slot, cap)],
            send_sem=sems.at[0, group, to], recv_sem=sems.at[1, group, slot],
            device_id={"seq": to}, device_id_type=MESH,
        )

    def others(body):
        def step(index, _):
            body(lax.rem(me + index, n))
            return 0

        lax.fori_loop(1, n, step, 0)

    def loop(count, body):
        def step(index, _):
            body(index)
            return 0

        lax.fori_loop(0, count, step, 0)

    def at_sub(block, part):
        return rows_from(block * quarter + part * sub, sub)

    def copy_near(sems, scan, src, dst, part, to, slot):
        return pltpu.make_async_remote_copy(
            src_ref=src.at[at_sub(to, part)], dst_ref=dst.at[at_sub(slot, part)],
            send_sem=sems.at[0, scan, to * SUBS + part],
            recv_sem=sems.at[1, scan, slot * SUBS + part],
            device_id={"seq": plane * PLANE + to}, device_id_type=MESH,
        )

    peers = [lax.rem(spot + step, PLANE) for step in range(1, PLANE)]

    def send_near(sems, scan, src, dst, part):
        for peer in peers:
            copy_near(sems, scan, src, dst, part, peer, spot).start()
        dst[at_sub(spot, part), :] = src[at_sub(spot, part), :]

    def got_near(sems, scan, src, dst, part):
        for peer in peers:
            copy_near(sems, scan, src, dst, part, peer, peer).wait_recv()

    def sent_near(sems, scan, src, dst, part):
        for peer in peers:
            copy_near(sems, scan, src, dst, part, peer, spot).wait_send()

    def copy_far(scan, total, far, part, ahead):
        sign = 1 if scan == 0 else -1
        return pltpu.make_async_remote_copy(
            src_ref=total.at[at_sub(0, part)], dst_ref=far.at[at_sub(ahead - 1, part)],
            send_sem=far_sems.at[0, scan, (ahead - 1) * SUBS + part],
            recv_sem=far_sems.at[1, scan, (ahead - 1) * SUBS + part],
            device_id={"seq": me + sign * ahead * PLANE}, device_id_type=MESH,
        )

    def sends(scan, ahead):
        return plane + ahead < planes if scan == 0 else plane >= ahead

    def gets(scan, ahead):
        return plane >= ahead if scan == 0 else plane + ahead < planes

    def doc(block, which):
        return metas[pl.ds(block * 8 + which, 1), :]

    scans = [
        (fw_own, fw_in, fw_total, fw_far, fw_send, fw_carry, 3, 2, list(range(PLANE)), -1),
        (rv_own, rv_in, rv_total, rv_far, rv_send, rv_carry, 2, 3, list(range(PLANE))[::-1], 1),
    ]
    for scan in range(2):
        far = scans[scan][3]
        for ahead in (1, 2):
            @pl.when(jnp.logical_not(gets(scan, ahead)))
            def _():
                far[(ahead - 1) * quarter : ahead * quarter, :] = jnp.zeros((quarter, HS), BF16)

    def chain(scan, part):
        own, arrived, total_ref, far, send, carry, leaving, entering, order, toward = scans[scan]
        got_near(near_sems, scan, own, arrived, part)

        @pl.when(gets(scan, 1))
        def _():
            copy_far(scan, total_ref, far, part, 1).wait_recv()

        total = far[at_sub(0, part), :].astype(F32)
        for block in order:
            here = plane * PLANE + block
            prior = doc(jnp.clip(here + toward, 0, n - 1), leaving)
            send[at_sub(block, part), :] = (total * same(doc(here, entering), prior)).astype(BF16)
            mine = arrived[at_sub(block, part), :].astype(F32)
            total = mine + total * same(doc(here, leaving), prior)
        total_ref[at_sub(0, part), :] = total.astype(BF16)

        @pl.when(sends(scan, 1))
        def _():
            copy_far(scan, total_ref, far, part, 1).start()

        send_near(carry_sems, scan, send, carry, part)

    def plane_total(scan, part):
        own, arrived, total_ref, far, _, _, leaving, _, order, toward = scans[scan]
        got_near(near_sems, scan, own, arrived, part)
        total = None
        for block in order:
            mine = arrived[at_sub(block, part), :].astype(F32)
            here = plane * PLANE + block
            if total is None:
                total = mine
            else:
                total = mine + total * same(doc(here, leaving), doc(here + toward, leaving))
        total_ref[at_sub(0, part), :] = total.astype(BF16)
        for ahead in (1, 2):
            @pl.when(sends(scan, ahead))
            def _():
                copy_far(scan, total_ref, far, part, ahead).start()

    def carries(scan, part):
        _, arrived, total_ref, far, send, carry, leaving, entering, order, toward = scans[scan]
        for ahead in (1, 2):
            @pl.when(gets(scan, ahead))
            def _():
                copy_far(scan, total_ref, far, part, ahead).wait_recv()

        def clamp(block):
            return jnp.clip(block, 0, n - 1)

        edge = plane * PLANE + order[0] + toward
        total = far[at_sub(0, part), :].astype(F32) + far[at_sub(1, part), :].astype(F32) * same(
            doc(clamp(edge), leaving), doc(clamp(edge + toward * PLANE), leaving)
        )
        for block in order:
            here = plane * PLANE + block
            prior = doc(clamp(here + toward), leaving)
            send[at_sub(block, part), :] = (total * same(doc(here, entering), prior)).astype(BF16)
            mine = arrived[at_sub(block, part), :].astype(F32)
            total = mine + total * same(doc(here, leaving), prior)
        send_near(carry_sems, scan, send, carry, part)

    def got_carry(scan, part):
        got_near(carry_sems, scan, scans[scan][4], scans[scan][5], part)

    def group_heads(part):
        return [(index, index * SUBS + part) for index in range(each)]

    def own_forward(part):
        for _, head in group_heads(part):
            at = rows_at(head, HS)
            kept = jnp.where(last_mask, k_ref[:, at].astype(F32), 0.0).astype(BF16)
            fw_own[at, :] = dot(kept, v_ref[:, at], 0, 0).astype(BF16)

    def inside(part):
        for _, head in group_heads(part):
            at = rows_at(head, HS)
            attn = jnp.where(visible, dot(q_ref[:, at], k_ref[:, at], 1, 1), 0.0).astype(BF16)
            attn_ref[at, :] = attn
            o_ref[:, at] = dot(attn, v_ref[:, at], 1, 0)

    loads[2].wait()
    loads[3].wait()
    own_forward(0)
    pl.semaphore_wait(barrier, (n - 1) + (nh - 1))
    if aligned:
        send_near(near_sems, 0, fw_own, fw_in, 0)

        def own_step(index):
            own_forward(index + 1)
            send_near(near_sems, 0, fw_own, fw_in, index + 1)

        loop(SUBS - 1, own_step)
    else:
        loop(SUBS - 1, lambda index: own_forward(index + 1))
        loop(SUBS, lambda part: send_near(near_sems, 0, fw_own, fw_in, part))
    others(lambda other: copy_meta(other, me).start())
    slots = lax.broadcasted_iota(jnp.int32, (cap, tok), 0).astype(F32)
    lanes = lax.broadcasted_iota(jnp.int32, (cap, tok), 1).astype(F32)

    def picks(owners, owner):
        chosen = jnp.broadcast_to(jnp.where(owners == owner, 1.0, 0.0), (cap, tok))
        rank = dot(chosen.astype(BF16), before, 1, 0)
        return jnp.where(rank == slots, chosen, 0.0)

    owner_row = meta_ref[0:1, :]
    owner_of = lax.broadcasted_iota(jnp.int32, (n, tok), 0).astype(F32)
    rank_ref[...] = dot(same(owner_row, owner_of).astype(BF16), before, 1, 0)

    def pack(owner):
        rank = rank_ref[pl.ds(owner, 1), :]
        chosen = same(owner_row, owner.astype(F32))
        pack_ref[rows_at(owner, cap), :] = (same(rank, slots) * chosen).astype(BF16)

    loads[4].wait()
    loop(SUBS // 2, inside)
    loop(n, pack)
    others(lambda other: copy_meta(other, other).wait_recv())
    loop(SUBS, lambda part: chain(0, part))
    loop(SUBS // 2, lambda part: inside(part + SUBS // 2))

    def unpack(source):
        chosen = picks(metas[pl.ds(source * 8, 1), :], me.astype(F32))
        row = jnp.sum(chosen * metas[pl.ds(source * 8 + 1, 1), :], axis=1, keepdims=True)
        used = jnp.sum(chosen, axis=1, keepdims=True)
        unpack_ref[rows_at(source, cap), :] = (
            jnp.where(row == lanes, 1.0, 0.0) * used
        ).astype(BF16)

    loads[5].wait()
    loads[6].wait()
    if not aligned:
        loop(SUBS, lambda part: got_carry(0, part))

    def output_step(part, sums):
        squares, inner = sums
        if aligned:
            got_carry(0, part)
        for _, head in group_heads(part):
            at = rows_at(head, HS)
            add = dot(q_ref[:, at], fw_carry[at, :], 1, 0)
            total = o_ref[:, at] + jnp.where(first_mask, add, 0.0)
            o_ref[:, at] = total
            scaled = gain_ref[:, at] * gn_ref[:, at].astype(F32)
            squares, inner = squares + total * total, inner + scaled * total
        return squares, inner

    zero = jnp.zeros((tok, HS), F32)
    squares, inner = lax.fori_loop(0, SUBS, output_step, (zero, zero))
    squares = jnp.sum(squares, axis=1, keepdims=True)
    inner = jnp.sum(inner, axis=1, keepdims=True)
    pair = jnp.where(place_col < HS // 2, squares, inner)
    sums_out[...] = pair

    def sum_copy(to, slot):
        return pltpu.make_async_remote_copy(
            src_ref=sums_out, dst_ref=sums_in.at[rows_at(slot, tok)],
            send_sem=sum_sems.at[0, to], recv_sem=sum_sems.at[1, slot],
            device_id={"head": to}, device_id_type=MESH,
        )

    def sum_start(step, _):
        sum_copy(lax.rem(me_head + step, nh), me_head).start()
        return 0

    def sum_finish(step, total):
        other = lax.rem(me_head + step, nh)
        sum_copy(other, other).wait_recv()
        return total + sums_in[rows_at(other, tok), :]

    def sum_sent(step, _):
        sum_copy(lax.rem(me_head + step, nh), me_head).wait_send()
        return 0

    lax.fori_loop(1, nh, sum_start, 0)
    pair = lax.fori_loop(1, nh, sum_finish, pair)
    full = HEADS * HS
    inv_rms = lax.rsqrt(pair[:, 0:1] / full + EPSILON)
    pull = inv_rms * inv_rms * inv_rms * pair[:, HS - 1 : HS] / full
    inv_rms = jnp.broadcast_to(inv_rms, (tok, HS))
    pull = jnp.broadcast_to(pull, (tok, HS))

    def own_reverse(part):
        for _, head in group_heads(part):
            at = rows_at(head, HS)
            scaled = gain_ref[:, at] * gn_ref[:, at].astype(F32)
            grad = (inv_rms * scaled - o_ref[:, at] * pull).astype(BF16)
            go_ref[:, at] = grad
            kept = jnp.where(first_mask, q_ref[:, at].astype(F32), 0.0).astype(BF16)
            rv_own[at, :] = dot(kept, grad, 0, 0).astype(BF16)
        if aligned:
            send_near(near_sems, 1, rv_own, rv_in, part)

    loop(SUBS, own_reverse)
    if not aligned:
        loop(SUBS, lambda part: send_near(near_sems, 1, rv_own, rv_in, part))

    half = SUBS // 2
    slots_all = n * cap

    def grad_query(group, part):
        made = []
        for index, head in group_heads(group * half + part):
            at = rows_at(head, HS)
            grad = go_ref[:, at]
            back = jnp.where(visible, dot(grad, v_ref[:, at], 1, 1), 0.0).astype(BF16)
            back_ref[at, :] = back
            add = dot(grad, fw_carry[at, :], 1, 1)
            result = dot(back, k_ref[:, at], 1, 0) + jnp.where(first_mask, add, 0.0)
            made.append(result.astype(BF16))
        bq_send[group * slots_all : (group + 1) * slots_all, rows_at(part, each * HS)] = dot(
            pack_ref[...], jnp.concatenate(made, axis=1), 1, 0
        ).astype(BF16)

    def send_query(group):
        others(lambda other: copy_rows(bq_send, bq_in, q_sems, group, other, me).start())
        bq_in[rows_at(group * n + me, cap), :] = bq_send[rows_at(group * n + me, cap), :]

    loop(half, lambda part: grad_query(0, part))
    loop(SUBS, lambda part: plane_total(1, part))
    send_query(0)
    loop(half, lambda part: grad_query(1, part))
    send_query(1)

    def inside_back(part):
        for _, head in group_heads(part):
            at = rows_at(head, HS)
            gk_ref[:, at] = dot(back_ref[at, :], q_ref[:, at], 0, 0)
            gv_ref[:, at] = dot(attn_ref[at, :], go_ref[:, at], 0, 0)

    loop(SUBS, lambda part: carries(1, part))
    loop(SUBS, inside_back)
    if not aligned:
        loop(SUBS, lambda part: got_carry(1, part))

    def grad_pair(part):
        if aligned:
            got_carry(1, part)
        made = [[], []]
        for index, head in group_heads(part):
            at = rows_at(head, HS)
            carry = rv_carry[at, :]
            key = gk_ref[:, at] + jnp.where(last_mask, dot(v_ref[:, at], carry, 1, 1), 0.0)
            value = gv_ref[:, at] + jnp.where(last_mask, dot(k_ref[:, at], carry, 1, 0), 0.0)
            made[0].append(key.astype(BF16))
            made[1].append(value.astype(BF16))
        bkv_send[rows_at(part, slots_all), :] = dot(
            pack_ref[...], jnp.concatenate(made[0] + made[1], axis=1), 1, 0
        ).astype(BF16)

        def far_first(index, _):
            away = (index + 1) // 2
            other = lax.rem(me + n // 2 + away * (1 - 2 * lax.rem(index, 2)), n)
            copy_rows(bkv_send, bkv_in, kv_sems, part, other, me).start()
            return 0

        lax.fori_loop(0, n - 1, far_first, 0)
        bkv_in[rows_at(part * n + me, cap), :] = bkv_send[rows_at(part * n + me, cap), :]

    loop(SUBS, grad_pair)

    loop(n, unpack)
    place_ref[...] = unpack_ref[...].T

    def place_query(group, part):
        arrived = bq_in[group * slots_all : (group + 1) * slots_all, rows_at(part, each * HS)]
        placed = dot(place_ref[...], arrived, 1, 0).astype(BF16)
        for index, head in group_heads(group * half + part):
            out_ref[0, :, rows_at(head, HS)] = placed[:, index * HS : (index + 1) * HS]

    for group in range(2):
        others(lambda other: copy_rows(bq_send, bq_in, q_sems, group, other, other).wait_recv())
        loop(half, lambda part: place_query(group, part))

    def place_pair(part):
        others(lambda other: copy_rows(bkv_send, bkv_in, kv_sems, part, other, other).wait_recv())
        placed = dot(place_ref[...], bkv_in[rows_at(part, slots_all), :], 1, 0).astype(BF16)
        for index, head in group_heads(part):
            for which in range(2):
                column = (which * each + index) * HS
                out_ref[which + 1, :, rows_at(head, HS)] = placed[:, column : column + HS]

    loop(SUBS, place_pair)

    others(lambda other: copy_meta(other, me).wait_send())
    lax.fori_loop(1, nh, sum_sent, 0)
    for scan in range(2):
        own, arrived, total_ref, far, send, carry = scans[scan][:6]

        def drain(part):
            sent_near(near_sems, scan, own, arrived, part)
            sent_near(carry_sems, scan, send, carry, part)
            for ahead in (1, 2)[: scan + 1]:
                @pl.when(sends(scan, ahead))
                def _():
                    copy_far(scan, total_ref, far, part, ahead).wait_send()

        loop(SUBS, drain)
    for group in range(2):
        others(lambda other: copy_rows(bq_send, bq_in, q_sems, group, other, me).wait_send())
    loop(
        SUBS,
        lambda part: others(
            lambda other: copy_rows(bkv_send, bkv_in, kv_sems, part, other, me).wait_send()
        ),
    )


def local(n, nh, query, keys, values, grad_normed, norm_gain, doc_ids, home):
    tok, width = query.shape
    heads = width // HS
    cap = max(16, 2 * tok // n)
    states = pltpu.VMEM((heads * HS, HS), BF16)
    total = pltpu.VMEM((heads * HS // PLANE, HS), BF16)
    far = pltpu.VMEM((2 * heads * HS // PLANE, HS), BF16)
    scan = [states, states, total, far, states, states]
    block = pltpu.VMEM((tok, width), BF16)
    wide = pltpu.VMEM((tok, width), F32)
    map_rows = pltpu.VMEM((n * cap, tok), BF16)
    query_rows = pltpu.VMEM((2 * n * cap, width // 2), BF16)
    pair_rows = pltpu.VMEM((SUBS * n * cap, 2 * width // SUBS), BF16)
    dma = pltpu.SemaphoreType.DMA
    result = pl.pallas_call(
        functools.partial(kernel, n, nh, cap),
        out_shape=jax.ShapeDtypeStruct((3, tok, width), BF16),
        in_specs=[pl.BlockSpec(memory_space=pltpu.HBM)] * 7,
        out_specs=pl.BlockSpec(memory_space=pltpu.VMEM),
        scratch_shapes=[
            block, block, block, block,
            pltpu.VMEM((1, width), F32),
            pltpu.VMEM((1, tok), jnp.int32),
            pltpu.VMEM((1, tok), jnp.int32),
            pltpu.VMEM((8, tok), F32),
            pltpu.VMEM((n * 8, tok), F32),
            *scan, *scan,
            states, states,
            wide, block, wide, wide,
            pltpu.VMEM((tok, HS), F32),
            pltpu.VMEM((nh * tok, HS), F32),
            pltpu.VMEM((n, tok), F32),
            map_rows, map_rows,
            pltpu.VMEM((tok, n * cap), BF16),
            query_rows, query_rows, pair_rows, pair_rows,
            dma((7,)),
            dma((2, n)),
            dma((2, 2, PLANE * SUBS)),
            dma((2, 2, 2 * SUBS)),
            dma((2, 2, PLANE * SUBS)),
            dma((2, 2, n)),
            dma((2, SUBS, n)),
            dma((2, nh)),
        ],
        compiler_params=pltpu.CompilerParams(
            collective_id=0, has_side_effects=True, vmem_limit_bytes=56 * 1024 * 1024
        ),
    )(query, keys, values, grad_normed, norm_gain[None, :], doc_ids[None, :], home[None, :])
    return jnp.transpose(result, (1, 0, 2))


def solution(mesh):
    placed = (
        P("seq", "head"),
        P("seq", "head"),
        P("seq", "head"),
        P("seq", "head"),
        P("head"),
        P("seq"),
        P("seq"),
    )
    return jax.shard_map(
        functools.partial(local, mesh.shape["seq"], mesh.shape["head"]),
        mesh=mesh, in_specs=placed, out_specs=P("seq", None, "head"), check_vma=False,
    )
```
